256 devices in a mesh: pack: 32 (over x, y, core), tp: 8 (over z).
Axes of the slice: x: 4, y: 4, z: 8, core: 2. Of those that a mesh axis runs over, the one named last changes fastest.
Arguments:
- queries: bfloat16 [16384, 2048], P('pack', 'tp'), may hold values from -11.5 to 11.5
- keys_values: bfloat16 [16384, 8, 256], P('pack', 'tp'), may hold values from -11.5 to 11.5
- ssm_values: bfloat16 [16384, 4096], P('pack', 'tp'), may hold values from -6 to 6
- ssm_gates: bfloat16 [16384, 4096], P('pack', 'tp'), may hold values from -6 to 6
- ssm_maps: bfloat16 [16384, 512], P('pack'), may hold values from -0.375 to 0.375
- step_size: float32 [16384, 64], P('pack', 'tp'), may hold values from 0.45 to 14000
- decay_log: float32 [64], P('tp'), may hold values from -10 to -3.5
- skip_gain: float32 [64], P('tp'), may hold values from 0.5 to 1.5
- attn_out_weight: bfloat16 [2048, 5120], P('tp'), may hold values from -0.078125 to 0.078125
- ssd_out_weight: bfloat16 [4096, 5120], P('tp'), may hold values from -0.078125 to 0.078125
- lengths: int32 [4], replicated, may hold values from 1 to 8704, 16384 in all
Outputs:
- mixed: bfloat16 [16384, 5120], P(('pack', 'tp'))
The draws below stay inside these ranges and needn't reach their ends.
Inputs may be any that keep to these rules, and one draw needn't show every extreme that they name: The lengths of the 4 requests in packed order; they sum to 16384, and the longest is exactly 8704.
All inputs are finite; a program needn't handle non-finite values.
Results may differ from the reference program's by a relative error of at most 0.023.
Values may be sent and summed in bfloat16 or wider, within the bound.
No kernel may reach another device: no remote copies, remote signals or barrier semaphores. Data moves between devices by JAX's collectives and lax.ppermute only.
A program may use at most 128 MiB of HBM per device.

```python
import math
import jax
import jax.numpy as jnp
import numpy as np
from jax import lax

D = 5120
HD = 128
QH = 16
KVH = 8
SH = 64
SP = 64
SN = 256
BLOCK = 256
REQS = 4
PACKED_TOKEN_SUM = 16384
MOST = 8704
N_TP = 8


def aligned_keys(key, pick_rate, amp_low, amp_high):
    drawn_keys = jnp.clip(jax.random.normal(key, (PACKED_TOKEN_SUM, KVH, HD), jnp.float32), -6.0, 6.0)
    picked = jax.random.bernoulli(jax.random.fold_in(key, 1), pick_rate, (PACKED_TOKEN_SUM, 1, 1))
    amplitude = jax.random.uniform(jax.random.fold_in(key, 2), (PACKED_TOKEN_SUM, 1, 1), jnp.float32, amp_low, amp_high)
    strong_keys = jnp.clip(drawn_keys, -2.0, 2.0) * amplitude
    nudge = 1.0 + jax.random.uniform(jax.random.fold_in(key, 3), (PACKED_TOKEN_SUM, 1, 1), jnp.float32, 0.005, 0.01)
    successor_index = jnp.roll(picked, 1, 0) & jnp.logical_not(picked)
    keys_out = jnp.where(picked, strong_keys, drawn_keys)
    keys_out = jnp.where(successor_index, jnp.roll(strong_keys, 1, 0) * nudge, keys_out)
    return (keys_out, picked, strong_keys, drawn_keys)


def head_rates(key, lowest, highest):
    return jnp.exp(jax.random.uniform(key, (SH,), jnp.float32, math.log(lowest), math.log(highest)))


def draw_queries(key, part):
    pick_rate = 0.0
    keys_out, picked, strong_keys, drawn_keys = aligned_keys(key, pick_rate, 3.5, 5.5)
    key = jax.random.fold_in(key, 11)
    group_size = QH // KVH
    drawn = jnp.clip(jax.random.normal(key, (PACKED_TOKEN_SUM, KVH, group_size, HD), jnp.float32), -6.0, 6.0)
    far_aimed = jax.random.bernoulli(jax.random.fold_in(key, 4), 0.25, (PACKED_TOKEN_SUM, KVH, group_size))
    back_steps = jax.random.randint(jax.random.fold_in(key, 5), (PACKED_TOKEN_SUM, KVH, group_size), MOST // 4, MOST)
    token_positions = jnp.arange(PACKED_TOKEN_SUM, dtype=jnp.int32)
    source_rows = jnp.clip(token_positions[:, None, None] - back_steps, 0, PACKED_TOKEN_SUM - 1).astype(jnp.int32)
    head_numbers = jnp.arange(KVH, dtype=jnp.int32)[None, :, None]
    far_source = drawn_keys[source_rows, head_numbers]
    drawn = jnp.where(far_aimed[:, :, :, None], 1.5 * far_source, drawn)
    aimed = jnp.roll(picked, 3, 0)[:, :, :, None]
    source = jnp.roll(strong_keys, 3, 0)[:, :, None, :]
    drawn = jnp.where(aimed, source, drawn)
    return drawn.reshape(PACKED_TOKEN_SUM, QH * HD).astype(jnp.bfloat16)


def draw_keys_values(key, part):
    pick_rate = 0.0
    keys_out, picked, strong_keys, drawn_keys = aligned_keys(key, pick_rate, 3.5, 5.5)
    key = jax.random.fold_in(key, 12)
    values_out = jnp.clip(jax.random.normal(key, (PACKED_TOKEN_SUM, KVH, HD), jnp.float32), -6.0, 6.0)
    return jnp.concatenate([keys_out, values_out], axis=2).astype(jnp.bfloat16)


def draw_decay_log(key, part):
    fading_rates = head_rates(key, 5e-05, 0.03)
    return jnp.log(fading_rates)


def draw_step_size(key, part):
    fading_rates = head_rates(key, 5e-05, 0.03)
    key = jax.random.fold_in(key, 21)
    rough_guess = jnp.exp(jax.random.uniform(key, (PACKED_TOKEN_SUM, SH), jnp.float32, -0.7, 0.7))
    request_starts = jax.random.randint(jax.random.fold_in(key, 1), (3,), 0, PACKED_TOKEN_SUM)
    token_positions = jnp.arange(PACKED_TOKEN_SUM, dtype=jnp.int32)
    preempted_batch = jnp.any(token_positions[:, None] == request_starts[None, :], axis=1)[:, None]
    mismatch_amounts = jax.random.uniform(jax.random.fold_in(key, 2), (PACKED_TOKEN_SUM, SH), jnp.float32, 0.22, 0.7)
    return jnp.where(preempted_batch, mismatch_amounts / fading_rates[None, :], rough_guess)


def block_levels(stream_key, shape, split, low, high):
    def one(position, parts):
        steps = jax.random.uniform(jax.random.fold_in(jax.random.fold_in(stream_key, 6), position), (parts,), jnp.float32, low / len(split), high / len(split))
        return jnp.repeat(jnp.exp(steps), shape[position] // parts).reshape((-1,) + (1,) * (len(shape) - position - 1))

    factor_of = one(*split[0])
    for cut in split[1:]:
        factor_of = factor_of * one(*cut)
    return factor_of


def split_up(amount, total, reach, slope):
    loads = [(1 << 20) // math.isqrt(standing ** slope) + 1 for standing in range(2, amount + 1)]
    rest, given = total - reach - (amount - 1), [1] * (amount - 1)
    while rest > 0:
        movable = [i for i in range(amount - 1) if given[i] < reach]
        whole, budget = sum([loads[i] for i in movable]), rest
        for i in movable:
            extra = min(reach - given[i], max(1, budget * loads[i] // whole), rest)
            given[i] = given[i] + extra
            rest = rest - extra
    return np.array([reach] + given)


def ragged_sizes(own_key, count, total, reach, skew):
    if count == 2:
        one = jax.random.randint(own_key, (), max(1, total - reach), min(reach, total - 1) + 1)
        return jnp.stack([one, total - one])
    sizes = jnp.asarray(split_up(count, total, reach, skew), jnp.int32)
    twos = (count - 1) // 2
    donor, sink = sizes[1:1 + 2 * twos:2], sizes[2:2 + 2 * twos:2]
    slack = jnp.minimum(donor - 1, reach - sink)
    moved = jax.random.randint(jax.random.fold_in(own_key, 1), (twos,), 0, 1 << 20) % (slack + 1)
    sizes = sizes.at[1:1 + 2 * twos:2].set(donor - moved).at[2:2 + 2 * twos:2].set(sink + moved)
    return sizes[jax.random.permutation(jax.random.fold_in(own_key, 2), count)]


def normal_values(own_key, shape, width, most, split=(), kind=jnp.bfloat16):
    gain = block_levels(own_key, shape, split, -0.22, 0.18) if split else 1.0
    entries = jax.random.normal(own_key, shape, jnp.float32) * width * gain
    return jnp.minimum(jnp.maximum(entries, -most), most).astype(kind)


def setup_inputs(seed: int = 0) -> dict:
    key_list = jax.random.split(jax.random.key(seed), 12)
    return {
        "queries": draw_queries(jax.random.fold_in(key_list[11], 71), 0),
        "keys_values": draw_keys_values(jax.random.fold_in(key_list[11], 71), 0),
        "ssm_values": normal_values(key_list[2], (PACKED_TOKEN_SUM, SH * SP), 1.0, 6.0, ((0, 32), (1, 8))),
        "ssm_gates": normal_values(key_list[3], (PACKED_TOKEN_SUM, SH * SP), 1.0, 6.0, ((0, 32), (1, 8))),
        "ssm_maps": normal_values(key_list[4], (PACKED_TOKEN_SUM, 2 * SN), SN ** -0.5, 0.375, ((0, 32),)),
        "step_size": draw_step_size(jax.random.fold_in(key_list[11], 71), 0),
        "decay_log": draw_decay_log(jax.random.fold_in(key_list[11], 71), 0),
        "skip_gain": jnp.clip(0.5 + 1.0 * jax.random.uniform(key_list[7], (SH,), jnp.float32) ** block_levels(key_list[7], (SH,), ((0, 8),), -0.2, 0.2), 0.5, 1.5),
        "attn_out_weight": normal_values(key_list[8], (QH * HD, D), (QH * HD + SH * SP) ** -0.5, 0.078125, ((0, 8),)),
        "ssd_out_weight": normal_values(key_list[9], (SH * SP, D), (QH * HD + SH * SP) ** -0.5, 0.078125, ((0, 8),)),
        "lengths": ragged_sizes(key_list[10], REQS, PACKED_TOKEN_SUM, MOST, 2).astype(jnp.int32),
    }


masked_value = -1e30


def segment_of(positions, lengths):
    ends = jnp.cumsum(lengths).astype(jnp.int32)
    return jnp.sum((positions[:, None] >= ends[None, :]).astype(jnp.int32), axis=1).astype(jnp.int32)


def scan_block(recurrent_memory, values, maps, steps, fading_rates, skip, segs, prior_seg):
    block_size = values.shape[0]
    state_width = maps.shape[1] // 2
    write_map = maps[:, :state_width]
    read_map = maps[:, state_width:]
    decay_logarithm = -fading_rates[None, :] * steps
    cumulative = jnp.cumsum(decay_logarithm, axis=0)
    indices = jnp.arange(block_size, dtype=jnp.int32)
    allowed = (segs[:, None] == segs[None, :]) & (indices[None, :] <= indices[:, None])
    products = jnp.dot(read_map, write_map.T, preferred_element_type=jnp.float32)
    decay_gap = jnp.where(allowed[None], cumulative.T[:, :, None] - cumulative.T[:, None, :], masked_value)
    block_weights = (jnp.exp(decay_gap) * products[None]).astype(jnp.bfloat16)
    within = jnp.einsum("htu,uhp->thp", block_weights.astype(jnp.float32), values.astype(jnp.float32))
    continuing = segs == prior_seg
    reads = jnp.einsum("ln,hpn->lhp", read_map.astype(jnp.float32), recurrent_memory, precision=lax.Precision.HIGHEST)
    carried_in = jnp.where(continuing[:, None, None], reads * jnp.exp(cumulative)[:, :, None], 0.0)
    last_seg = segs[block_size - 1]
    tail_decay = jnp.where((segs == last_seg)[:, None], jnp.exp(cumulative[block_size - 1][None, :] - cumulative), 0.0)
    weighted = (values.astype(jnp.float32) * tail_decay[:, :, None]).astype(jnp.bfloat16)
    new_part = jnp.einsum("lhp,ln->hpn", weighted.astype(jnp.float32), write_map.astype(jnp.float32))
    keep_old = jnp.where(last_seg == prior_seg, jnp.exp(cumulative[block_size - 1]), 0.0)
    new_state = new_part + keep_old[:, None, None] * recurrent_memory
    ssm_y = within + carried_in + skip[None, :, None] * values.astype(jnp.float32)
    return new_state, ssm_y


def attend_all(queries, keys_values, segments):
    group_size = QH // KVH
    query_block = min(512, PACKED_TOKEN_SUM)
    key_window = min(PACKED_TOKEN_SUM, MOST + query_block)
    query_heads = queries.reshape(PACKED_TOKEN_SUM, KVH, group_size, HD)
    key_rows = keys_values[:, :, :HD]
    value_rows = keys_values[:, :, HD:]
    scaling = HD ** -0.5

    def one_block(block_index):
        query_start = (block_index * query_block).astype(jnp.int32)
        key_offset = jnp.clip(query_start - MOST, 0, PACKED_TOKEN_SUM - key_window).astype(jnp.int32)
        query_part = lax.dynamic_slice_in_dim(query_heads, query_start, query_block, 0)
        key_part = lax.dynamic_slice_in_dim(key_rows, key_offset, key_window, 0)
        value_part = lax.dynamic_slice_in_dim(value_rows, key_offset, key_window, 0)
        query_pos = query_start + jnp.arange(query_block, dtype=jnp.int32)
        key_pos = key_offset + jnp.arange(key_window, dtype=jnp.int32)
        query_seg = lax.dynamic_slice_in_dim(segments, query_start, query_block, 0)
        key_seg = lax.dynamic_slice_in_dim(segments, key_offset, key_window, 0)
        allowed = (query_seg[:, None] == key_seg[None, :]) & (key_pos[None, :] <= query_pos[:, None])
        wide_mask = allowed[:, None, None, :]
        scores = jnp.einsum("rkgd,skd->rkgs", query_part.astype(jnp.float32), key_part.astype(jnp.float32)) * scaling
        scores = jnp.where(wide_mask, scores, masked_value)
        row_max = jnp.max(scores, axis=-1)
        raw_weights = jnp.where(wide_mask, jnp.exp(scores - row_max[..., None]), 0.0)
        totals = jnp.sum(raw_weights, axis=-1)
        attn_weights = raw_weights.astype(jnp.bfloat16)
        summed = jnp.einsum("rkgs,skd->rkgd", attn_weights.astype(jnp.float32), value_part.astype(jnp.float32))
        return (summed / totals[..., None]).astype(jnp.bfloat16).reshape(query_block, QH * HD)

    blocks = lax.map(one_block, jnp.arange(PACKED_TOKEN_SUM // query_block, dtype=jnp.int32))
    return blocks.reshape(PACKED_TOKEN_SUM, QH * HD)


def ssm_all(ssm_values, ssm_gates, ssm_maps, step_size, decay_log, skip_gain, segments):
    block_count = PACKED_TOKEN_SUM // BLOCK
    seg_blocks = segments.reshape(block_count, BLOCK)
    priors = jnp.concatenate([jnp.full((1,), -1, jnp.int32), seg_blocks[:-1, BLOCK - 1]]).astype(jnp.int32)
    fading_rates = jnp.exp(decay_log)

    def advance(recurrent_memory, pieces):
        values, maps, steps, segs, prior_seg = pieces
        return scan_block(recurrent_memory, values, maps, steps, fading_rates, skip_gain, segs, prior_seg)

    inputs_seq = (ssm_values.reshape(block_count, BLOCK, SH, SP), ssm_maps.reshape(block_count, BLOCK, 2 * SN),
                  step_size.reshape(block_count, BLOCK, SH), seg_blocks, priors)
    zero_state = jnp.zeros((SH, SP, SN), jnp.float32)
    closing_state, ssm_y = lax.scan(advance, zero_state, inputs_seq)
    ssm_y = ssm_y.reshape(PACKED_TOKEN_SUM, SH, SP)
    gated = ssm_y * jax.nn.silu(ssm_gates.reshape(PACKED_TOKEN_SUM, SH, SP).astype(jnp.float32))
    return gated.astype(jnp.bfloat16).reshape(PACKED_TOKEN_SUM, SH * SP)


def reference(queries, keys_values, ssm_values, ssm_gates, ssm_maps, step_size, decay_log, skip_gain, attn_out_weight, ssd_out_weight, lengths):
    positions = jnp.arange(PACKED_TOKEN_SUM, dtype=jnp.int32)
    segments = segment_of(positions, lengths)
    attended = attend_all(queries, keys_values, segments)
    ssd_out = ssm_all(ssm_values, ssm_gates, ssm_maps, step_size, decay_log, skip_gain, segments)
    attn_cols = QH * HD // N_TP
    ssd_cols = SH * SP // N_TP
    summed = jnp.zeros((PACKED_TOKEN_SUM, D), jnp.float32)
    for group_index in range(N_TP):
        attn_part = attended[:, group_index * attn_cols:(group_index + 1) * attn_cols]
        ssd_part = ssd_out[:, group_index * ssd_cols:(group_index + 1) * ssd_cols]
        term = jnp.dot(attn_part, attn_out_weight[group_index * attn_cols:(group_index + 1) * attn_cols], preferred_element_type=jnp.float32)
        term = term + jnp.dot(ssd_part, ssd_out_weight[group_index * ssd_cols:(group_index + 1) * ssd_cols], preferred_element_type=jnp.float32)
        summed = summed + lax.optimization_barrier(term.astype(jnp.bfloat16)).astype(jnp.float32)
    return summed.astype(jnp.bfloat16)
```

```python
import functools

import jax
import jax.numpy as jnp
from jax import lax
from jax.experimental import pallas as pl
from jax.experimental.pallas import tpu as pltpu
from jax.sharding import PartitionSpec as P

ROWS = 512
BLOCK = 256
HD = 128
HEADS = 8
HP = 512
SN = 256
DM = 5120
CHUNK = 512
LOW = -1e30
LOG2E = 1.4426950408889634
HIGH = lax.Precision.HIGHEST
STATE_ROWS = SN + 16
VMEM = pl.BlockSpec(memory_space=pltpu.VMEM)
SMEM = pl.BlockSpec(memory_space=pltpu.SMEM)


def iota(shape, dim):
    return lax.broadcasted_iota(jnp.int32, shape, dim)


def ends_of(len_ref):
    e0 = len_ref[0]
    e1 = e0 + len_ref[1]
    return e0, e1, e1 + len_ref[2]


def start_of(pos, ends):
    e0, e1, e2 = ends
    zero = jnp.zeros_like(pos)
    out = jnp.where(pos >= e0, zero + e0, zero)
    out = jnp.where(pos >= e1, zero + e1, out)
    return jnp.where(pos >= e2, zero + e2, out)


def spread():
    return (iota((HEADS, HP), 1) // (HP // HEADS) == iota((HEADS, HP), 0)).astype(jnp.float32)


def widen(a, expand):
    return jnp.dot(a, expand, precision=HIGH, preferred_element_type=jnp.float32)


def ssd_kernel(len_ref, dl_ref, skip_ref, first_ref, x_ref, maps_ref, step_ref, y_ref, st_ref, fac_ref):
    first = first_ref[0]
    ends = ends_of(len_ref)
    expand = spread()
    head_lane = iota((1, HEADS), 1)
    wide_lane = iota((1, HP), 1) // (HP // HEADS)
    rate = jnp.zeros((1, HEADS), jnp.float32)
    skip = jnp.zeros((1, HP), jnp.float32)
    for h in range(HEADS):
        rate = jnp.where(head_lane == h, dl_ref[h], rate)
        skip = jnp.where(wide_lane == h, skip_ref[h], skip)
    rate = -jnp.exp(rate)
    row = iota((BLOCK, 1), 0)
    col = iota((1, BLOCK), 1)
    tri = (row >= col).astype(jnp.float32)
    half = iota((1, 128), 1) < 64
    state = None
    before = None
    for n in range(ROWS // BLOCK):
        rows = slice(n * BLOCK, (n + 1) * BLOCK)
        base = first + n * BLOCK
        start_col = start_of(base + row, ends)
        last_start = start_of(base + (BLOCK - 1), ends)
        cum = jnp.dot(tri, rate * step_ref[rows, :], precision=HIGH, preferred_element_type=jnp.float32)
        cum_t = cum.T
        write = maps_ref[rows, :SN]
        read = maps_ref[rows, SN:]
        prod = lax.dot_general(read, write, (((1,), (1,)), ((), ())), preferred_element_type=jnp.float32)
        allowed = (base + col >= start_col) & (col <= row)
        for pair in range(HEADS // 2):
            lanes = slice(pair * 128, (pair + 1) * 128)
            x = x_ref[rows, lanes]
            total = skip[:, lanes] * x.astype(jnp.float32)
            for which in range(2):
                h = pair * 2 + which
                gap = jnp.where(allowed, cum[:, h : h + 1] - cum_t[h : h + 1, :], LOW)
                weights = (jnp.exp(gap) * prod).astype(jnp.bfloat16)
                part = jnp.where(half if which == 0 else ~half, x, jnp.zeros_like(x))
                total = total + jnp.dot(weights, part, preferred_element_type=jnp.float32)
            y_ref[rows, lanes] = total
        ecum = jnp.exp(cum)
        if state is not None:
            local = widen(jnp.where(start_col < base, ecum, 0.0), expand)
            reads = jnp.dot(read, state.astype(jnp.bfloat16), preferred_element_type=jnp.float32)
            y_ref[rows, :] += reads * local
        carry = jnp.where(start_col < first, ecum, 0.0)
        if before is not None:
            carry = carry * before
        fac_ref[rows, :] = carry
        tail = jnp.exp(cum[BLOCK - 1 : BLOCK, :] - cum)
        tail = widen(jnp.where(base + row >= last_start, tail, 0.0), expand)
        weighted = (x_ref[rows, :].astype(jnp.float32) * tail).astype(jnp.bfloat16)
        new = lax.dot_general(write, weighted, (((0,), (0,)), ((), ())), preferred_element_type=jnp.float32)
        end = ecum[BLOCK - 8 :, :]
        if state is not None:
            keep = jnp.where(last_start < base, 1.0, 0.0)
            new = new + (keep * widen(end, expand)[7:8, :]) * state
            end = end * before
        state = new
        before = end[7:8, :]
    through = jnp.where(last_start < first, 1.0, 0.0) * widen(end, expand)[7:8, :]
    st_ref[:SN, :] = state.astype(jnp.bfloat16)
    store_through(st_ref, through)


def store_through(ref, through):
    high = through.astype(jnp.bfloat16).astype(jnp.float32)
    low = through - high
    sub = iota((16, 1), 0)
    ref[SN:, :] = jnp.where(sub == 0, high, jnp.where(sub == 1, low, 0.0)).astype(jnp.bfloat16)


def through_of(ref):
    tail = ref[SN:, :].astype(jnp.float32)
    return tail[0:1, :] + tail[1:2, :]


def join_kernel(*refs):
    out = refs[-1]
    state = refs[0][:SN, :].astype(jnp.float32)
    through = through_of(refs[0])
    for ref in refs[1:-1]:
        t = through_of(ref)
        state = ref[:SN, :].astype(jnp.float32) + t * state
        through = through * t
    out[:SN, :] = state.astype(jnp.bfloat16)
    store_through(out, through)


def attn_kernel(len_ref, first_ref, q_ref, kv_ref, o_ref, q_scr, m_scr, l_scr, acc_scr):
    first = first_ref[0]
    ends = ends_of(len_ref)
    tile = 256
    tiles = 2 * ROWS // tile
    q_scr[:ROWS, :] = q_ref[:, :HD]
    q_scr[ROWS:, :] = q_ref[:, HD:]
    factor = LOG2E * HD**-0.5

    def step(j, masked, opening):
        base = j * CHUNK
        k = kv_ref[pl.ds(pl.multiple_of(base, CHUNK), CHUNK), :HD]
        v = kv_ref[pl.ds(pl.multiple_of(base, CHUNK), CHUNK), HD:]
        for r in range(tiles):
            rows = slice(r * tile, (r + 1) * tile)
            s = lax.dot_general(q_scr[rows, :], k, (((1,), (1,)), ((), ())), preferred_element_type=jnp.float32)
            s = s * factor
            if masked:
                pos = first + (r * tile) % ROWS + iota((tile, 1), 0)
                key = base + iota((1, CHUNK), 1)
                s = jnp.where((key >= start_of(pos, ends)) & (key <= pos), s, LOW)
            m = jnp.max(s, axis=1, keepdims=True)
            if opening:
                m = jnp.broadcast_to(m, (tile, 128))
            else:
                old = m_scr[rows, :]
                m = jnp.maximum(old, m)
                alpha = jnp.exp2(old - m)
            p = jnp.exp2(s - jnp.concatenate([m] * (CHUNK // 128), axis=1))
            total = p[:, :128]
            for i in range(1, CHUNK // 128):
                total = total + p[:, i * 128 : (i + 1) * 128]
            out = jnp.dot(p.astype(jnp.bfloat16), v, preferred_element_type=jnp.float32)
            if not opening:
                total = total + l_scr[rows, :] * alpha
                out = out + acc_scr[rows, :] * alpha
            m_scr[rows, :] = m
            l_scr[rows, :] = total
            acc_scr[rows, :] = out

    mine = first // CHUNK
    low = start_of(first, ends) // CHUNK
    clear = jnp.clip((start_of(first + ROWS - 1, ends) + CHUNK - 1) // CHUNK, low, mine)
    step(mine, True, True)
    lax.fori_loop(low, clear, lambda j, _: (step(j, True, False), 0)[1], 0)
    lax.fori_loop(clear, mine, lambda j, _: (step(j, False, False), 0)[1], 0)
    for g in range(2):
        rows = slice(g * ROWS, (g + 1) * ROWS)
        total = jnp.sum(l_scr[rows, :], axis=1, keepdims=True)
        o_ref[:, g * HD : (g + 1) * HD] = (acc_scr[rows, :] / total).astype(jnp.bfloat16)


def proj_kernel(att_ref, y_ref, z_ref, read_ref, fac_ref, far_ref, near_ref, wa_ref, ws_ref, o_ref, act):
    @pl.when(pl.program_id(0) == 0)
    def _():
        state = near_ref[:SN, :].astype(jnp.float32)
        state = state + through_of(near_ref) * far_ref[:SN, :].astype(jnp.float32)
        reads = jnp.dot(read_ref[...], state.astype(jnp.bfloat16), preferred_element_type=jnp.float32)
        y = y_ref[...] + reads * widen(fac_ref[...], spread())
        z = z_ref[...].astype(jnp.float32)
        act[:, : 2 * HD] = att_ref[...]
        act[:, 2 * HD :] = (y * (z / (1.0 + jnp.exp(-z)))).astype(jnp.bfloat16)

    out = jnp.dot(act[:, : 2 * HD], wa_ref[...], preferred_element_type=jnp.float32)
    out = out + jnp.dot(act[:, 2 * HD :], ws_ref[...], preferred_element_type=jnp.float32)
    o_ref[...] = out.astype(jnp.bfloat16)


def big(**more):
    return pltpu.CompilerParams(vmem_limit_bytes=56 * 2**20, **more)


def shifted(block, distance):
    n = lax.axis_size("pack")
    return lax.ppermute(block, "pack", [(i, i + distance) for i in range(n - distance)])


def join(*runs):
    return pl.pallas_call(
        join_kernel,
        out_shape=jax.ShapeDtypeStruct((STATE_ROWS, HP), jnp.bfloat16),
        in_specs=[VMEM] * len(runs),
        out_specs=VMEM,
        compiler_params=big(),
    )(*runs)


def local(
    queries,
    keys_values,
    ssm_values,
    ssm_gates,
    ssm_maps,
    step_size,
    decay_log,
    skip_gain,
    attn_out_weight,
    ssd_out_weight,
    lengths,
):
    first = jnp.reshape(lax.axis_index("pack") * ROWS, (1,)).astype(jnp.int32)
    kv = lax.all_gather(keys_values.reshape(ROWS, 2 * HD), "pack", axis=0, tiled=True)

    y_local, summary, fac = pl.pallas_call(
        ssd_kernel,
        out_shape=(
            jax.ShapeDtypeStruct((ROWS, HP), jnp.float32),
            jax.ShapeDtypeStruct((STATE_ROWS, HP), jnp.bfloat16),
            jax.ShapeDtypeStruct((ROWS, HEADS), jnp.float32),
        ),
        in_specs=[SMEM] * 4 + [VMEM] * 3,
        out_specs=(VMEM, VMEM, VMEM),
        compiler_params=big(),
        cost_estimate=pl.CostEstimate(flops=10**9, bytes_accessed=4 * 10**6, transcendentals=10**6),
        name="ssd_local",
    )(lengths, decay_log, skip_gain, first, ssm_values, ssm_maps, step_size)

    three = join(shifted(summary, 3), shifted(summary, 2), shifted(summary, 1))
    nine = join(shifted(three, 6), shifted(three, 3), three)
    far = shifted(nine, 9)

    attended = pl.pallas_call(
        attn_kernel,
        out_shape=jax.ShapeDtypeStruct((ROWS, 2 * HD), jnp.bfloat16),
        in_specs=[SMEM] * 2 + [VMEM] * 2,
        out_specs=VMEM,
        scratch_shapes=[
            pltpu.VMEM((2 * ROWS, HD), jnp.bfloat16),
            pltpu.VMEM((2 * ROWS, 128), jnp.float32),
            pltpu.VMEM((2 * ROWS, 128), jnp.float32),
            pltpu.VMEM((2 * ROWS, HD), jnp.float32),
        ],
        compiler_params=big(),
        cost_estimate=pl.CostEstimate(flops=5 * 10**9, bytes_accessed=9 * 10**6, transcendentals=9 * 10**6),
        name="attention",
    )(lengths, first, queries, kv)

    cols = 1280
    whole = lambda *shape: pl.BlockSpec(shape, lambda i: (0,) * len(shape))
    terms = pl.pallas_call(
        proj_kernel,
        out_shape=jax.ShapeDtypeStruct((ROWS, DM), jnp.bfloat16),
        grid=(DM // cols,),
        in_specs=[
            whole(ROWS, 2 * HD),
            whole(ROWS, HP),
            whole(ROWS, HP),
            pl.BlockSpec((ROWS, SN), lambda i: (0, 1)),
            whole(ROWS, HEADS),
            whole(STATE_ROWS, HP),
            whole(STATE_ROWS, HP),
            pl.BlockSpec((2 * HD, cols), lambda i: (0, i)),
            pl.BlockSpec((HP, cols), lambda i: (0, i)),
        ],
        out_specs=pl.BlockSpec((ROWS, cols), lambda i: (0, i)),
        scratch_shapes=[pltpu.VMEM((ROWS, 2 * HD + HP), jnp.bfloat16)],
        compiler_params=big(),
        cost_estimate=pl.CostEstimate(flops=4 * 10**9, bytes_accessed=16 * 10**6, transcendentals=10**6),
        name="project",
    )(attended, y_local, ssm_gates, ssm_maps, fac, far, nine, attn_out_weight, ssd_out_weight)
    return lax.psum_scatter(terms, "tp", scatter_dimension=0, tiled=True)


def solution(mesh):
    return jax.shard_map(
        local,
        mesh=mesh,
        in_specs=(
            P("pack", "tp"),
            P("pack", "tp", None),
            P("pack", "tp"),
            P("pack", "tp"),
            P("pack", None),
            P("pack", "tp"),
            P("tp"),
            P("tp"),
            P("tp", None),
            P("tp", None),
            P(),
        ),
        out_specs=P(("pack", "tp"), None),
        check_vma=False,
    )
```

```python
import jax
import jax.numpy as jnp
from jax import lax
from jax.experimental import pallas as pl
from jax.experimental.pallas import tpu as pltpu
from jax.sharding import PartitionSpec as P

ROWS = 512
BLOCK = 256
HD = 128
HEADS = 8
HP = 512
SN = 256
DM = 5120
CHUNK = 512
SLOTS = 18
TILE = 256
COLS = 1280
LOW = -1e30
LOG2E = 1.4426950408889634
HIGH = lax.Precision.HIGHEST
STATE_ROWS = SN + 16
VMEM = pl.BlockSpec(memory_space=pltpu.VMEM)
SMEM = pl.BlockSpec(memory_space=pltpu.SMEM)
ANY = pl.BlockSpec(memory_space=pl.ANY)


def iota(shape, dim):
    return lax.broadcasted_iota(jnp.int32, shape, dim)


def ends_of(len_ref):
    e0 = len_ref[0]
    e1 = e0 + len_ref[1]
    return e0, e1, e1 + len_ref[2]


def start_of(pos, ends):
    e0, e1, e2 = ends
    zero = jnp.zeros_like(pos)
    out = jnp.where(pos >= e0, zero + e0, zero)
    out = jnp.where(pos >= e1, zero + e1, out)
    return jnp.where(pos >= e2, zero + e2, out)


def spread():
    return (iota((HEADS, HP), 1) // (HP // HEADS) == iota((HEADS, HP), 0)).astype(jnp.float32)


def widen(a, expand):
    return jnp.dot(a, expand, precision=HIGH, preferred_element_type=jnp.float32)


def ssd_kernel(len_ref, dl_ref, skip_ref, first_ref, x_ref, maps_ref, step_ref, y_ref, st_ref, fac_ref):
    first = first_ref[0]
    ends = ends_of(len_ref)
    expand = spread()
    head_lane = iota((1, HEADS), 1)
    wide_lane = iota((1, HP), 1) // (HP // HEADS)
    rate = jnp.zeros((1, HEADS), jnp.float32)
    skip = jnp.zeros((1, HP), jnp.float32)
    for h in range(HEADS):
        rate = jnp.where(head_lane == h, dl_ref[h], rate)
        skip = jnp.where(wide_lane == h, skip_ref[h], skip)
    rate = -jnp.exp(rate)
    row = iota((BLOCK, 1), 0)
    col = iota((1, BLOCK), 1)
    tri = (row >= col).astype(jnp.float32)
    half = iota((1, 128), 1) < 64
    state = None
    before = None
    for n in range(ROWS // BLOCK):
        rows = slice(n * BLOCK, (n + 1) * BLOCK)
        base = first + n * BLOCK
        start_col = start_of(base + row, ends)
        last_start = start_of(base + (BLOCK - 1), ends)
        cum = jnp.dot(tri, rate * step_ref[rows, :], precision=HIGH, preferred_element_type=jnp.float32)
        cum_t = cum.T
        write = maps_ref[rows, :SN]
        read = maps_ref[rows, SN:]
        prod = lax.dot_general(read, write, (((1,), (1,)), ((), ())), preferred_element_type=jnp.float32)
        allowed = (base + col >= start_col) & (col <= row)
        for pair in range(HEADS // 2):
            lanes = slice(pair * 128, (pair + 1) * 128)
            x = x_ref[rows, lanes]
            total = skip[:, lanes] * x.astype(jnp.float32)
            for which in range(2):
                h = pair * 2 + which
                gap = jnp.where(allowed, cum[:, h : h + 1] - cum_t[h : h + 1, :], LOW)
                weights = (jnp.exp(gap) * prod).astype(jnp.bfloat16)
                part = jnp.where(half if which == 0 else ~half, x, jnp.zeros_like(x))
                total = total + jnp.dot(weights, part, preferred_element_type=jnp.float32)
            y_ref[rows, lanes] = total
        ecum = jnp.exp(cum)
        if state is not None:
            local = widen(jnp.where(start_col < base, ecum, 0.0), expand)
            reads = jnp.dot(read, state.astype(jnp.bfloat16), preferred_element_type=jnp.float32)
            y_ref[rows, :] += reads * local
        carry = jnp.where(start_col < first, ecum, 0.0)
        if before is not None:
            carry = carry * before
        fac_ref[rows, :] = carry
        tail = jnp.exp(cum[BLOCK - 1 : BLOCK, :] - cum)
        tail = widen(jnp.where(base + row >= last_start, tail, 0.0), expand)
        weighted = (x_ref[rows, :].astype(jnp.float32) * tail).astype(jnp.bfloat16)
        new = lax.dot_general(write, weighted, (((0,), (0,)), ((), ())), preferred_element_type=jnp.float32)
        end = ecum[BLOCK - 8 :, :]
        if state is not None:
            keep = jnp.where(last_start < base, 1.0, 0.0)
            new = new + (keep * widen(end, expand)[7:8, :]) * state
            end = end * before
        state = new
        before = end[7:8, :]
    through = jnp.where(last_start < first, 1.0, 0.0) * widen(end, expand)[7:8, :]
    st_ref[:SN, :] = state.astype(jnp.bfloat16)
    store_through(st_ref, through)


def store_through(ref, through):
    high = through.astype(jnp.bfloat16).astype(jnp.float32)
    low = through - high
    sub = iota((16, 1), 0)
    ref[SN:, :] = jnp.where(sub == 0, high, jnp.where(sub == 1, low, 0.0)).astype(jnp.bfloat16)


def through_of(ref):
    tail = ref[SN:, :].astype(jnp.float32)
    return tail[0:1, :] + tail[1:2, :]


def join_kernel(*refs):
    out = refs[-1]
    state = refs[0][:SN, :].astype(jnp.float32)
    through = through_of(refs[0])
    for ref in refs[1:-1]:
        t = through_of(ref)
        state = ref[:SN, :].astype(jnp.float32) + t * state
        through = through * t
    out[:SN, :] = state.astype(jnp.bfloat16)
    store_through(out, through)


def gate_kernel(y_ref, z_ref, read_ref, fac_ref, far_ref, near_ref, act_ref):
    state = near_ref[:SN, :].astype(jnp.float32)
    state = state + through_of(near_ref) * far_ref[:SN, :].astype(jnp.float32)
    reads = jnp.dot(read_ref[...], state.astype(jnp.bfloat16), preferred_element_type=jnp.float32)
    y = y_ref[...] + reads * widen(fac_ref[...], spread())
    z = z_ref[...].astype(jnp.float32)
    act_ref[...] = (y * (z / (1.0 + jnp.exp(-z)))).astype(jnp.bfloat16)


def mix_kernel(
    len_ref,
    first_ref,
    q_ref,
    act_ref,
    kv_hbm,
    wa_hbm,
    ws_hbm,
    o_hbm,
    q_scr,
    kv_scr,
    acc_scr,
    m_scr,
    w_scr,
    in_scr,
    o_scr,
    kv_sem,
    w_sem,
    o_sem,
):
    first = first_ref[0]
    ends = ends_of(len_ref)
    mine = first // CHUNK
    low = start_of(first, ends) // CHUNK
    last_start = start_of(first + ROWS - 1, ends)
    count = mine - low + 1

    def chunk_of(i):
        return jnp.where(i == 0, mine, low + i - 1)

    def kv_copy(i):
        rows = pl.ds(pl.multiple_of(chunk_of(i) * CHUNK, CHUNK), CHUNK)
        return pltpu.make_async_copy(kv_hbm.at[rows], kv_scr.at[i], kv_sem.at[i])

    lax.fori_loop(0, count, lambda i, _: (kv_copy(i).start(), 0)[1], 0)
    weights = [
        pltpu.make_async_copy(wa_hbm, w_scr.at[pl.ds(0, 2 * HD)], w_sem.at[0]),
        pltpu.make_async_copy(ws_hbm, w_scr.at[pl.ds(2 * HD, HP)], w_sem.at[1]),
    ]
    for copy in weights:
        copy.start()
    for g in range(2):
        rows = slice(g * ROWS, (g + 1) * ROWS)
        scaled = q_ref[:, g * HD : (g + 1) * HD].astype(jnp.float32) * (LOG2E * HD**-0.5)
        high = scaled.astype(jnp.bfloat16)
        q_scr[rows, :HD] = high
        q_scr[rows, HD:] = (scaled - high.astype(jnp.float32)).astype(jnp.bfloat16)
    one = jnp.ones((CHUNK, HD), jnp.bfloat16)

    def scores(i, rows, masked):
        k = kv_scr[i, :, :HD]
        s = lax.dot_general(
            q_scr[rows, :],
            jnp.concatenate([k, k], axis=1),
            (((1,), (1,)), ((), ())),
            preferred_element_type=jnp.float32,
        )
        if masked:
            pos = first + rows.start % ROWS + iota((rows.stop - rows.start, 1), 0)
            key = chunk_of(i) * CHUNK + iota((1, CHUNK), 1)
            s = jnp.where((key >= start_of(pos, ends)) & (key <= pos), s, LOW)
        return s

    def plain(i, masked):
        v = jnp.concatenate([kv_scr[i, :, HD:], one], axis=1)
        for r in range(2 * ROWS // TILE):
            rows = slice(r * TILE, (r + 1) * TILE)
            p = jnp.exp2(scores(i, rows, masked)).astype(jnp.bfloat16)
            acc_scr[rows, :] += jnp.dot(p, v, preferred_element_type=jnp.float32)

    def guarded(i, masked):
        v = jnp.concatenate([kv_scr[i, :, HD:], one], axis=1)
        for r in range(2 * ROWS // TILE):
            rows = slice(r * TILE, (r + 1) * TILE)
            s = scores(i, rows, masked)
            old = m_scr[rows, :]
            m = jnp.maximum(old, jnp.max(s, axis=1, keepdims=True))
            alpha = jnp.exp2(old - m)
            p = jnp.exp2(s - jnp.concatenate([m] * (CHUNK // 128), axis=1)).astype(jnp.bfloat16)
            out = jnp.dot(p, v, preferred_element_type=jnp.float32)
            acc_scr[rows, :] = acc_scr[rows, :] * jnp.concatenate([alpha, alpha], axis=1) + out
            m_scr[rows, :] = m

    def over_chunks(step, wait):
        def one_chunk(i, _):
            if wait:
                kv_copy(i).wait()
            masked = (i == 0) | (chunk_of(i) * CHUNK < last_start)
            pl.when(masked)(lambda: step(i, True))
            pl.when(jnp.logical_not(masked))(lambda: step(i, False))
            return 0

        lax.fori_loop(0, count, one_chunk, 0)

    acc_scr[...] = jnp.zeros_like(acc_scr)
    over_chunks(plain, True)
    total = acc_scr[:, HD:]
    fine = (jnp.min(total) > 2.0**-60) & (jnp.max(total) < 2.0**110)

    @pl.when(jnp.logical_not(fine))
    def _():
        acc_scr[...] = jnp.zeros_like(acc_scr)
        m_scr[...] = jnp.full(m_scr.shape, LOW, jnp.float32)
        over_chunks(guarded, False)

    for g in range(2):
        rows = slice(g * ROWS, (g + 1) * ROWS)
        in_scr[:, g * HD : (g + 1) * HD] = (acc_scr[rows, :HD] / acc_scr[rows, HD:]).astype(jnp.bfloat16)
    in_scr[:, 2 * HD :] = act_ref[...]
    for copy in weights:
        copy.wait()

    def out_copy(i):
        cols = pl.ds(i * COLS, COLS)
        return pltpu.make_async_copy(o_scr.at[:, cols], o_hbm.at[:, cols], o_sem.at[i])

    for i in range(DM // COLS):
        cols = slice(i * COLS, (i + 1) * COLS)
        o_scr[:, cols] = jnp.dot(in_scr[...], w_scr[:, cols], preferred_element_type=jnp.float32).astype(jnp.bfloat16)
        out_copy(i).start()
    for i in range(DM // COLS):
        out_copy(i).wait()


def big(**more):
    return pltpu.CompilerParams(vmem_limit_bytes=56 * 2**20, **more)


def shifted(block, distance):
    n = lax.axis_size("pack")
    return lax.ppermute(block, "pack", [(i, i + distance) for i in range(n - distance)])


def join(*runs):
    return pl.pallas_call(
        join_kernel,
        out_shape=jax.ShapeDtypeStruct((STATE_ROWS, HP), jnp.bfloat16),
        in_specs=[VMEM] * len(runs),
        out_specs=VMEM,
        compiler_params=big(),
    )(*runs)


def local(
    queries,
    keys_values,
    ssm_values,
    ssm_gates,
    ssm_maps,
    step_size,
    decay_log,
    skip_gain,
    attn_out_weight,
    ssd_out_weight,
    lengths,
):
    first = jnp.reshape(lax.axis_index("pack") * ROWS, (1,)).astype(jnp.int32)
    kv = lax.all_gather(keys_values.reshape(ROWS, 2 * HD), "pack", axis=0, tiled=True)

    y_local, summary, fac = pl.pallas_call(
        ssd_kernel,
        out_shape=(
            jax.ShapeDtypeStruct((ROWS, HP), jnp.float32),
            jax.ShapeDtypeStruct((STATE_ROWS, HP), jnp.bfloat16),
            jax.ShapeDtypeStruct((ROWS, HEADS), jnp.float32),
        ),
        in_specs=[SMEM] * 4 + [VMEM] * 3,
        out_specs=(VMEM, VMEM, VMEM),
        compiler_params=big(),
        cost_estimate=pl.CostEstimate(flops=10**9, bytes_accessed=4 * 10**6, transcendentals=10**6),
        name="ssd_local",
    )(lengths, decay_log, skip_gain, first, ssm_values, ssm_maps, step_size)

    three = join(shifted(summary, 3), shifted(summary, 2), shifted(summary, 1))
    nine = join(shifted(three, 6), shifted(three, 3), three)
    far = shifted(nine, 9)

    act = pl.pallas_call(
        gate_kernel,
        out_shape=jax.ShapeDtypeStruct((ROWS, HP), jnp.bfloat16),
        grid=(1,),
        in_specs=[
            pl.BlockSpec((ROWS, HP), lambda i: (0, 0)),
            pl.BlockSpec((ROWS, HP), lambda i: (0, 0)),
            pl.BlockSpec((ROWS, SN), lambda i: (0, 1)),
            pl.BlockSpec((ROWS, HEADS), lambda i: (0, 0)),
            pl.BlockSpec((STATE_ROWS, HP), lambda i: (0, 0)),
            pl.BlockSpec((STATE_ROWS, HP), lambda i: (0, 0)),
        ],
        out_specs=pl.BlockSpec((ROWS, HP), lambda i: (0, 0)),
        compiler_params=big(),
        cost_estimate=pl.CostEstimate(flops=10**8, bytes_accessed=3 * 10**6, transcendentals=3 * 10**5),
        name="gate",
    )(y_local, ssm_gates, ssm_maps, fac, far, nine)

    terms = pl.pallas_call(
        mix_kernel,
        out_shape=jax.ShapeDtypeStruct((ROWS, DM), jnp.bfloat16),
        in_specs=[SMEM] * 2 + [VMEM] * 2 + [ANY] * 3,
        out_specs=ANY,
        scratch_shapes=[
            pltpu.VMEM((2 * ROWS, 2 * HD), jnp.bfloat16),
            pltpu.VMEM((SLOTS, CHUNK, 2 * HD), jnp.bfloat16),
            pltpu.VMEM((2 * ROWS, 2 * HD), jnp.float32),
            pltpu.VMEM((2 * ROWS, HD), jnp.float32),
            pltpu.VMEM((2 * HD + HP, DM), jnp.bfloat16),
            pltpu.VMEM((ROWS, 2 * HD + HP), jnp.bfloat16),
            pltpu.VMEM((ROWS, DM), jnp.bfloat16),
            pltpu.SemaphoreType.DMA((SLOTS,)),
            pltpu.SemaphoreType.DMA((2,)),
            pltpu.SemaphoreType.DMA((DM // COLS,)),
        ],
        compiler_params=big(),
        cost_estimate=pl.CostEstimate(flops=9 * 10**9, bytes_accessed=25 * 10**6, transcendentals=9 * 10**6),
        name="mix",
    )(lengths, first, queries, act, kv, attn_out_weight, ssd_out_weight)
    return lax.psum_scatter(terms, "tp", scatter_dimension=0, tiled=True)


def solution(mesh):
    return jax.shard_map(
        local,
        mesh=mesh,
        in_specs=(
            P("pack", "tp"),
            P("pack", "tp", None),
            P("pack", "tp"),
            P("pack", "tp"),
            P("pack", None),
            P("pack", "tp"),
            P("tp"),
            P("tp"),
            P("tp", None),
            P("tp", None),
            P(),
        ),
        out_specs=P(("pack", "tp"), None),
        check_vma=False,
    )
```

```python
import jax
import jax.numpy as jnp
from jax import lax
from jax.experimental import pallas as pl
from jax.experimental.pallas import tpu as pltpu
from jax.sharding import PartitionSpec as P

ROWS = 512
BLOCK = 256
HD = 128
HEADS = 8
HP = 512
SN = 256
DM = 5120
CHUNK = 512
SLOTS = 18
TILE = 256
COLS = 1280
LOW = -1e30
LOG2E = 1.4426950408889634
HIGH = lax.Precision.HIGHEST
HALF = HP // 2
STATE_ROWS = SN + 16
Y_OFF = (0, 3, 1, 2)
ROW_OF_GROUP = (0, 1, 99, 2)
ROW_OF_SLOT = (0, 1, 3, 2)
VMEM = pl.BlockSpec(memory_space=pltpu.VMEM)
SMEM = pl.BlockSpec(memory_space=pltpu.SMEM)
ANY = pl.BlockSpec(memory_space=pl.ANY)


def iota(shape, dim):
    return lax.broadcasted_iota(jnp.int32, shape, dim)


def ends_of(len_ref):
    e0 = len_ref[0]
    e1 = e0 + len_ref[1]
    return e0, e1, e1 + len_ref[2]


def start_of(pos, ends):
    e0, e1, e2 = ends
    zero = jnp.zeros_like(pos)
    out = jnp.where(pos >= e0, zero + e0, zero)
    out = jnp.where(pos >= e1, zero + e1, out)
    return jnp.where(pos >= e2, zero + e2, out)


def spread():
    return (iota((HEADS, HP), 1) // (HP // HEADS) == iota((HEADS, HP), 0)).astype(jnp.float32)


def widen(a, expand):
    return jnp.dot(a, expand, precision=HIGH, preferred_element_type=jnp.float32)


def ssd_kernel(len_ref, dl_ref, skip_ref, first_ref, x_ref, maps_ref, step_ref, y_ref, keep_ref, send_ref, fac_ref):
    first = first_ref[0]
    ends = ends_of(len_ref)
    expand = spread()
    head_sub = iota((HEADS, 1), 0)
    wide_lane = iota((1, HP), 1) // (HP // HEADS)
    rate = jnp.zeros((HEADS, 1), jnp.float32)
    skip = jnp.zeros((1, HP), jnp.float32)
    for h in range(HEADS):
        rate = jnp.where(head_sub == h, dl_ref[h], rate)
        skip = jnp.where(wide_lane == h, skip_ref[h], skip)
    rate = -jnp.exp(rate)
    row = iota((BLOCK, 1), 0)
    col = iota((1, BLOCK), 1)
    tri = (row >= col).astype(jnp.float32)
    half = iota((1, 128), 1) < 64
    state = None
    before = None
    for n in range(ROWS // BLOCK):
        rows = slice(n * BLOCK, (n + 1) * BLOCK)
        base = first + n * BLOCK
        start_col = start_of(base + row, ends)
        last_start = start_of(base + (BLOCK - 1), ends)
        cum_t = lax.dot_general(
            rate * step_ref[:, rows], tri, (((1,), (1,)), ((), ())), precision=HIGH, preferred_element_type=jnp.float32
        )
        cum = cum_t.T
        write = maps_ref[rows, :SN]
        read = maps_ref[rows, SN:]
        prod = lax.dot_general(read, write, (((1,), (1,)), ((), ())), preferred_element_type=jnp.float32)
        allowed = (base + col >= start_col) & (col <= row)
        for pair in range(HEADS // 2):
            lanes = slice(pair * 128, (pair + 1) * 128)
            x = x_ref[rows, lanes]
            total = skip[:, lanes] * x.astype(jnp.float32)
            for which in range(2):
                h = pair * 2 + which
                gap = jnp.where(allowed, cum[:, h : h + 1] - cum_t[h : h + 1, :], LOW)
                weights = (jnp.exp(gap) * prod).astype(jnp.bfloat16)
                part = jnp.where(half if which == 0 else ~half, x, jnp.zeros_like(x))
                total = total + jnp.dot(weights, part, preferred_element_type=jnp.float32)
            y_ref[rows, lanes] = total
        ecum = jnp.exp(cum)
        if state is not None:
            local = widen(jnp.where(start_col < base, ecum, 0.0), expand)
            reads = jnp.dot(read, state.astype(jnp.bfloat16), preferred_element_type=jnp.float32)
            y_ref[rows, :] += reads * local
        carry = jnp.where(start_col < first, ecum, 0.0)
        if before is not None:
            carry = carry * before
        fac_ref[rows, :] = carry
        tail = jnp.exp(cum[BLOCK - 1 : BLOCK, :] - cum)
        tail = widen(jnp.where(base + row >= last_start, tail, 0.0), expand)
        weighted = (x_ref[rows, :].astype(jnp.float32) * tail).astype(jnp.bfloat16)
        new = lax.dot_general(write, weighted, (((0,), (0,)), ((), ())), preferred_element_type=jnp.float32)
        end = ecum[BLOCK - 8 :, :]
        if state is not None:
            keep = jnp.where(last_start < base, 1.0, 0.0)
            new = new + (keep * widen(end, expand)[7:8, :]) * state
            end = end * before
        state = new
        before = end[7:8, :]
    through = jnp.where(last_start < first, 1.0, 0.0) * widen(end, expand)[7:8, :]
    core = (first // ROWS) % 2
    left, right = slice(0, HALF), slice(HALF, HP)
    for ref, wanted in ((keep_ref, 0), (send_ref, 1)):
        store_run(
            ref,
            jnp.where(core == wanted, state[:, left], state[:, right]),
            jnp.where(core == wanted, through[:, left], through[:, right]),
        )


def store_run(ref, state, through):
    high = through.astype(jnp.bfloat16).astype(jnp.float32)
    low = through - high
    sub = iota((16, 1), 0)
    ref[:SN, :] = state.astype(jnp.bfloat16)
    ref[SN:, :] = jnp.where(sub == 0, high, jnp.where(sub == 1, low, 0.0)).astype(jnp.bfloat16)


def load_run(ref):
    tail = ref[SN:, :].astype(jnp.float32)
    return ref[:SN, :].astype(jnp.float32), tail[0:1, :] + tail[1:2, :]


def pick(cond, one, other):
    return jnp.where(cond, one[0], other[0]), jnp.where(cond, one[1], other[1])


def after(earlier, later):
    return later[0] + later[1] * earlier[0], earlier[1] * later[1]


def chip_kernel(first_ref, mine_ref, other_ref, out_ref):
    core = (first_ref[0] // ROWS) % 2
    mine, other = load_run(mine_ref), load_run(other_ref)
    store_run(out_ref, *after(pick(core == 0, mine, other), pick(core == 0, other, mine)))


def row_kernel(first_ref, mine_ref, below_ref, above_ref, across_ref, prefix_ref, total_ref):
    y = (first_ref[0] // (2 * ROWS)) % 4
    by_distance = [load_run(ref) for ref in (mine_ref, below_ref, across_ref, above_ref)]
    run = (jnp.zeros((SN, HALF), jnp.float32), jnp.ones((1, HALF), jnp.float32))
    prefix = run
    for place in range(4):
        distance = (y - place) % 4
        piece = by_distance[0]
        for d in range(1, 4):
            piece = pick(distance == d, by_distance[d], piece)
        prefix = pick(y == place, run, prefix)
        run = after(run, piece)
    store_run(prefix_ref, *prefix)
    store_run(total_ref, *run)


def carry_kernel(first_ref, row3_ref, row2_ref, row1_ref, prefix_ref, mine_ref, other_ref, keep_ref, send_ref):
    core = (first_ref[0] // ROWS) % 2
    run = load_run(row3_ref)
    for ref in (row2_ref, row1_ref, prefix_ref):
        run = after(run, load_run(ref))
    behind = after(run, pick(core == 0, load_run(mine_ref), load_run(other_ref)))
    keep_ref[...] = jnp.where(core == 0, run[0], behind[0]).astype(jnp.bfloat16)
    send_ref[...] = jnp.where(core == 0, behind[0], run[0]).astype(jnp.bfloat16)


def gate_kernel(first_ref, y_ref, z_ref, maps_ref, fac_ref, keep_ref, got_ref, act_ref):
    core = (first_ref[0] // ROWS) % 2
    keep, got = keep_ref[...], got_ref[...]
    state = jnp.concatenate([jnp.where(core == 0, keep, got), jnp.where(core == 0, got, keep)], axis=1)
    reads = jnp.dot(maps_ref[:, SN:], state, preferred_element_type=jnp.float32)
    y = y_ref[...] + reads * widen(fac_ref[...], spread())
    z = z_ref[...].astype(jnp.float32)
    act_ref[...] = (y * (z / (1.0 + jnp.exp(-z)))).astype(jnp.bfloat16)


def mix_kernel(
    len_ref,
    first_ref,
    q_ref,
    act_ref,
    g0,
    g1,
    g2,
    g3,
    h0,
    h1,
    h2,
    h3,
    wa_hbm,
    ws_hbm,
    o_hbm,
    q_scr,
    kv_scr,
    acc_scr,
    m_scr,
    w_scr,
    in_scr,
    o_scr,
    ids,
    kv_sem,
    w_sem,
    o_sem,
):
    first = first_ref[0]
    ends = ends_of(len_ref)
    mine = first // CHUNK
    low = start_of(first, ends) // CHUNK
    last_start = start_of(first + ROWS - 1, ends)
    x, y, core = mine // 8, (mine // 2) % 4, mine % 2

    def kv_copy(src, slot, i):
        return pltpu.make_async_copy(src.at[pl.ds(slot * CHUNK, CHUNK)], kv_scr.at[i], kv_sem.at[i])

    ids[0] = mine
    kv_copy(g0, 0, 0).start()
    count = jnp.int32(1)
    for which, group in enumerate((g0, g1, g2, g3, h0, h1, h2, h3)):
        odd = (core + which // 4) % 2 == 1
        for slot in range(4):
            if which == 0 and slot == 0:
                continue
            even_x = x - ROW_OF_GROUP[which % 4]
            odd_x = x - ROW_OF_SLOT[slot]
            row = jnp.where(odd, odd_x, even_x)
            place = jnp.where(odd, (y + Y_OFF[which % 4]) % 4, (y + Y_OFF[slot]) % 4)
            block = row * 8 + place * 2 + odd.astype(jnp.int32)
            needed = (row >= 0) & (block >= low) & (block < mine)

            @pl.when(needed)
            def _(group=group, slot=slot, block=block, count=count):
                ids[count] = block
                kv_copy(group, slot, count).start()

            count = count + needed.astype(jnp.int32)

    def chunk_of(i):
        return ids[i]

    weights = [
        pltpu.make_async_copy(wa_hbm, w_scr.at[pl.ds(0, 2 * HD)], w_sem.at[0]),
        pltpu.make_async_copy(ws_hbm, w_scr.at[pl.ds(2 * HD, HP)], w_sem.at[1]),
    ]
    for copy in weights:
        copy.start()
    for g in range(2):
        rows = slice(g * ROWS, (g + 1) * ROWS)
        scaled = q_ref[:, g * HD : (g + 1) * HD].astype(jnp.float32) * (LOG2E * HD**-0.5)
        high = scaled.astype(jnp.bfloat16)
        q_scr[rows, :HD] = high
        q_scr[rows, HD:] = (scaled - high.astype(jnp.float32)).astype(jnp.bfloat16)
    one = jnp.ones((CHUNK, HD), jnp.bfloat16)

    def scores(i, rows, masked):
        k = kv_scr[i, :, :HD]
        s = lax.dot_general(
            q_scr[rows, :],
            jnp.concatenate([k, k], axis=1),
            (((1,), (1,)), ((), ())),
            preferred_element_type=jnp.float32,
        )
        if masked:
            pos = first + rows.start % ROWS + iota((rows.stop - rows.start, 1), 0)
            key = chunk_of(i) * CHUNK + iota((1, CHUNK), 1)
            s = jnp.where((key >= start_of(pos, ends)) & (key <= pos), s, LOW)
        return s

    def plain(i, masked):
        v = jnp.concatenate([kv_scr[i, :, HD:], one], axis=1)
        for r in range(2 * ROWS // TILE):
            rows = slice(r * TILE, (r + 1) * TILE)
            p = jnp.exp2(scores(i, rows, masked)).astype(jnp.bfloat16)
            acc_scr[rows, :] += jnp.dot(p, v, preferred_element_type=jnp.float32)

    def guarded(i, masked):
        v = jnp.concatenate([kv_scr[i, :, HD:], one], axis=1)
        for r in range(2 * ROWS // TILE):
            rows = slice(r * TILE, (r + 1) * TILE)
            s = scores(i, rows, masked)
            old = m_scr[rows, :]
            m = jnp.maximum(old, jnp.max(s, axis=1, keepdims=True))
            alpha = jnp.exp2(old - m)
            p = jnp.exp2(s - jnp.concatenate([m] * (CHUNK // 128), axis=1)).astype(jnp.bfloat16)
            out = jnp.dot(p, v, preferred_element_type=jnp.float32)
            acc_scr[rows, :] = acc_scr[rows, :] * jnp.concatenate([alpha, alpha], axis=1) + out
            m_scr[rows, :] = m

    def over_chunks(step, wait):
        def one_chunk(i, _):
            if wait:
                kv_copy(g0, 0, i).wait()
            masked = (i == 0) | (chunk_of(i) * CHUNK < last_start)
            pl.when(masked)(lambda: step(i, True))
            pl.when(jnp.logical_not(masked))(lambda: step(i, False))
            return 0

        lax.fori_loop(0, count, one_chunk, 0)

    acc_scr[...] = jnp.zeros_like(acc_scr)
    over_chunks(plain, True)
    total = acc_scr[:, HD:]
    fine = (jnp.min(total) > 2.0**-60) & (jnp.max(total) < 2.0**110)

    @pl.when(jnp.logical_not(fine))
    def _():
        acc_scr[...] = jnp.zeros_like(acc_scr)
        m_scr[...] = jnp.full(m_scr.shape, LOW, jnp.float32)
        over_chunks(guarded, False)

    for g in range(2):
        rows = slice(g * ROWS, (g + 1) * ROWS)
        in_scr[:, g * HD : (g + 1) * HD] = (acc_scr[rows, :HD] / acc_scr[rows, HD:]).astype(jnp.bfloat16)
    in_scr[:, 2 * HD :] = act_ref[...]
    for copy in weights:
        copy.wait()

    def out_copy(i):
        cols = pl.ds(i * COLS, COLS)
        return pltpu.make_async_copy(o_scr.at[:, cols], o_hbm.at[:, cols], o_sem.at[i])

    for i in range(DM // COLS):
        cols = slice(i * COLS, (i + 1) * COLS)
        o_scr[:, cols] = jnp.dot(in_scr[...], w_scr[:, cols], preferred_element_type=jnp.float32).astype(jnp.bfloat16)
        out_copy(i).start()
    for i in range(DM // COLS):
        out_copy(i).wait()


def big(**more):
    return pltpu.CompilerParams(vmem_limit_bytes=56 * 2**20, **more)


def moved(block, route0, route1):
    pairs = []
    for x in range(4):
        for y in range(4):
            for core, route in enumerate((route0, route1)):
                to = route(x, y)
                if to is not None:
                    pairs.append((x * 8 + y * 2 + core, to[0] * 8 + to[1] * 2 + core))
    return lax.ppermute(block, "pack", pairs)


def along_x(distance):
    return lambda x, y: (x + distance, y) if x + distance < 4 else None


def along_y(distance):
    return lambda x, y: (x, (y + distance) % 4)


def swapped(block):
    return lax.ppermute(block, "pack", [(i, i ^ 1) for i in range(32)])


def call(kernel, shapes, ins, *args):
    return pl.pallas_call(
        kernel,
        out_shape=tuple(jax.ShapeDtypeStruct(shape, jnp.bfloat16) for shape in shapes),
        in_specs=[SMEM] + [VMEM] * ins,
        out_specs=(VMEM,) * len(shapes),
        compiler_params=big(),
        cost_estimate=pl.CostEstimate(flops=10**6, bytes_accessed=10**6, transcendentals=0),
    )(*args)


def local(
    queries,
    keys_values,
    ssm_values,
    ssm_gates,
    ssm_maps,
    step_size,
    decay_log,
    skip_gain,
    attn_out_weight,
    ssd_out_weight,
    lengths,
):
    first = jnp.reshape(lax.axis_index("pack") * ROWS, (1,)).astype(jnp.int32)
    kv = keys_values.reshape(ROWS, 2 * HD)
    nowhere = lambda x, y: None
    below = moved(kv, along_y(1), along_x(1))
    above = moved(kv, along_y(3), along_x(3))
    across = moved(kv, along_y(2), along_x(2))

    y_local, run_keep, run_send, fac = pl.pallas_call(
        ssd_kernel,
        out_shape=(
            jax.ShapeDtypeStruct((ROWS, HP), jnp.float32),
            jax.ShapeDtypeStruct((STATE_ROWS, HALF), jnp.bfloat16),
            jax.ShapeDtypeStruct((STATE_ROWS, HALF), jnp.bfloat16),
            jax.ShapeDtypeStruct((ROWS, HEADS), jnp.float32),
        ),
        in_specs=[SMEM] * 4 + [VMEM] * 3,
        out_specs=(VMEM, VMEM, VMEM, VMEM),
        compiler_params=big(),
        cost_estimate=pl.CostEstimate(flops=10**9, bytes_accessed=4 * 10**6, transcendentals=10**6),
        name="ssd_local",
    )(lengths, decay_log, skip_gain, first, ssm_values, ssm_maps, step_size.T)

    below, above, across = lax.optimization_barrier((below, above, across, fac))[:3]
    group = jnp.concatenate([kv, below, above, across], axis=0)
    groups = [
        group,
        moved(group, along_x(1), along_y(1)),
        moved(group, nowhere, along_y(3)),
        moved(group, along_x(2), along_y(2)),
    ]
    run = (STATE_ROWS, HALF)
    run_got = swapped(run_send)
    (chip,) = call(chip_kernel, [run], 2, first, run_keep, run_got)
    chips = [moved(chip, along_y(d), along_y(d)) for d in (1, 3, 2)]
    prefix, total = call(row_kernel, [run, run], 4, first, chip, *chips)
    rows = [moved(total, along_x(d), along_x(d)) for d in (3, 2, 1)]
    groups = [groups[0], *lax.optimization_barrier((*groups[1:], *rows))[:3]]
    groups = groups + [swapped(g) for g in groups]
    keep, send = call(carry_kernel, [(SN, HALF)] * 2, 6, first, *rows, prefix, run_keep, run_got)
    got = swapped(send)
    act = pl.pallas_call(
        gate_kernel,
        out_shape=jax.ShapeDtypeStruct((ROWS, HP), jnp.bfloat16),
        in_specs=[SMEM] + [VMEM] * 6,
        out_specs=VMEM,
        compiler_params=big(),
        cost_estimate=pl.CostEstimate(flops=10**8, bytes_accessed=3 * 10**6, transcendentals=3 * 10**5),
        name="gate",
    )(first, y_local, ssm_gates, ssm_maps, fac, keep, got)

    terms = pl.pallas_call(
        mix_kernel,
        out_shape=jax.ShapeDtypeStruct((ROWS, DM), jnp.bfloat16),
        in_specs=[SMEM] * 2 + [VMEM] * 2 + [ANY] * 10,
        out_specs=ANY,
        scratch_shapes=[
            pltpu.VMEM((2 * ROWS, 2 * HD), jnp.bfloat16),
            pltpu.VMEM((SLOTS, CHUNK, 2 * HD), jnp.bfloat16),
            pltpu.VMEM((2 * ROWS, 2 * HD), jnp.float32),
            pltpu.VMEM((2 * ROWS, HD), jnp.float32),
            pltpu.VMEM((2 * HD + HP, DM), jnp.bfloat16),
            pltpu.VMEM((ROWS, 2 * HD + HP), jnp.bfloat16),
            pltpu.VMEM((ROWS, DM), jnp.bfloat16),
            pltpu.SMEM((SLOTS,), jnp.int32),
            pltpu.SemaphoreType.DMA((SLOTS,)),
            pltpu.SemaphoreType.DMA((2,)),
            pltpu.SemaphoreType.DMA((DM // COLS,)),
        ],
        compiler_params=big(),
        cost_estimate=pl.CostEstimate(flops=9 * 10**9, bytes_accessed=25 * 10**6, transcendentals=9 * 10**6),
        name="mix",
    )(lengths, first, queries, act, *groups, attn_out_weight, ssd_out_weight)
    return lax.psum_scatter(terms, "tp", scatter_dimension=0, tiled=True)


def solution(mesh):
    return jax.shard_map(
        local,
        mesh=mesh,
        in_specs=(
            P("pack", "tp"),
            P("pack", "tp", None),
            P("pack", "tp"),
            P("pack", "tp"),
            P("pack", None),
            P("pack", "tp"),
            P("tp"),
            P("tp"),
            P("tp", None),
            P("tp", None),
            P(),
        ),
        out_specs=P(("pack", "tp"), None),
        check_vma=False,
    )
```

```python
import jax
import jax.numpy as jnp
from jax import lax
from jax.experimental import pallas as pl
from jax.experimental.pallas import tpu as pltpu
from jax.sharding import PartitionSpec as P

ROWS = 512
BLOCK = 256
HD = 128
HEADS = 8
HP = 512
SN = 256
DM = 5120
CHUNK = 512
SLOTS = 18
TILE = 256
COLS = 1280
LOW = -1e30
LOG2E = 1.4426950408889634
HIGH = lax.Precision.HIGHEST
HALF = HP // 2
STATE_ROWS = SN + 16
VMEM = pl.BlockSpec(memory_space=pltpu.VMEM)
SMEM = pl.BlockSpec(memory_space=pltpu.SMEM)
ANY = pl.BlockSpec(memory_space=pl.ANY)


def iota(shape, dim):
    return lax.broadcasted_iota(jnp.int32, shape, dim)


def ends_of(len_ref):
    e0 = len_ref[0]
    e1 = e0 + len_ref[1]
    return e0, e1, e1 + len_ref[2]


def start_of(pos, ends):
    e0, e1, e2 = ends
    zero = jnp.zeros_like(pos)
    out = jnp.where(pos >= e0, zero + e0, zero)
    out = jnp.where(pos >= e1, zero + e1, out)
    return jnp.where(pos >= e2, zero + e2, out)


def spread():
    return (iota((HEADS, HP), 1) // (HP // HEADS) == iota((HEADS, HP), 0)).astype(jnp.float32)


def widen(a, expand):
    return jnp.dot(a, expand, precision=HIGH, preferred_element_type=jnp.float32)


def ssd_kernel(len_ref, dl_ref, skip_ref, first_ref, x_ref, maps_ref, step_ref, y_ref, keep_ref, send_ref, fac_ref):
    first = first_ref[0]
    ends = ends_of(len_ref)
    expand = spread()
    head_sub = iota((HEADS, 1), 0)
    wide_lane = iota((1, HP), 1) // (HP // HEADS)
    rate = jnp.zeros((HEADS, 1), jnp.float32)
    skip = jnp.zeros((1, HP), jnp.float32)
    for h in range(HEADS):
        rate = jnp.where(head_sub == h, dl_ref[h], rate)
        skip = jnp.where(wide_lane == h, skip_ref[h], skip)
    rate = -jnp.exp(rate)
    row = iota((BLOCK, 1), 0)
    col = iota((1, BLOCK), 1)
    tri = (row >= col).astype(jnp.float32)
    half = iota((1, 128), 1) < 64
    state = None
    before = None
    for n in range(ROWS // BLOCK):
        rows = slice(n * BLOCK, (n + 1) * BLOCK)
        base = first + n * BLOCK
        start_col = start_of(base + row, ends)
        last_start = start_of(base + (BLOCK - 1), ends)
        cum_t = lax.dot_general(
            rate * step_ref[:, rows], tri, (((1,), (1,)), ((), ())), precision=HIGH, preferred_element_type=jnp.float32
        )
        cum = cum_t.T
        write = maps_ref[rows, :SN]
        read = maps_ref[rows, SN:]
        prod = lax.dot_general(read, write, (((1,), (1,)), ((), ())), preferred_element_type=jnp.float32)
        allowed = (base + col >= start_col) & (col <= row)
        for pair in range(HEADS // 2):
            lanes = slice(pair * 128, (pair + 1) * 128)
            x = x_ref[rows, lanes]
            total = skip[:, lanes] * x.astype(jnp.float32)
            for which in range(2):
                h = pair * 2 + which
                gap = jnp.where(allowed, cum[:, h : h + 1] - cum_t[h : h + 1, :], LOW)
                weights = (jnp.exp(gap) * prod).astype(jnp.bfloat16)
                part = jnp.where(half if which == 0 else ~half, x, jnp.zeros_like(x))
                total = total + jnp.dot(weights, part, preferred_element_type=jnp.float32)
            y_ref[rows, lanes] = total
        ecum = jnp.exp(cum)
        if state is not None:
            local = widen(jnp.where(start_col < base, ecum, 0.0), expand)
            reads = jnp.dot(read, state.astype(jnp.bfloat16), preferred_element_type=jnp.float32)
            y_ref[rows, :] += reads * local
        carry = jnp.where(start_col < first, ecum, 0.0)
        if before is not None:
            carry = carry * before
        fac_ref[rows, :] = carry
        tail = jnp.exp(cum[BLOCK - 1 : BLOCK, :] - cum)
        tail = widen(jnp.where(base + row >= last_start, tail, 0.0), expand)
        weighted = (x_ref[rows, :].astype(jnp.float32) * tail).astype(jnp.bfloat16)
        new = lax.dot_general(write, weighted, (((0,), (0,)), ((), ())), preferred_element_type=jnp.float32)
        end = ecum[BLOCK - 8 :, :]
        if state is not None:
            keep = jnp.where(last_start < base, 1.0, 0.0)
            new = new + (keep * widen(end, expand)[7:8, :]) * state
            end = end * before
        state = new
        before = end[7:8, :]
    through = jnp.where(last_start < first, 1.0, 0.0) * widen(end, expand)[7:8, :]
    core = (first // ROWS) % 2
    left, right = slice(0, HALF), slice(HALF, HP)
    for ref, wanted in ((keep_ref, 0), (send_ref, 1)):
        store_run(
            ref,
            jnp.where(core == wanted, state[:, left], state[:, right]),
            jnp.where(core == wanted, through[:, left], through[:, right]),
        )


def store_run(ref, state, through):
    high = through.astype(jnp.bfloat16).astype(jnp.float32)
    low = through - high
    sub = iota((16, 1), 0)
    ref[:SN, :] = state.astype(jnp.bfloat16)
    ref[SN:, :] = jnp.where(sub == 0, high, jnp.where(sub == 1, low, 0.0)).astype(jnp.bfloat16)


def load_run(ref):
    tail = ref[SN:, :].astype(jnp.float32)
    return ref[:SN, :].astype(jnp.float32), tail[0:1, :] + tail[1:2, :]


def pick(cond, one, other):
    return jnp.where(cond, one[0], other[0]), jnp.where(cond, one[1], other[1])


def after(earlier, later):
    return later[0] + later[1] * earlier[0], earlier[1] * later[1]


def chip_kernel(first_ref, mine_ref, other_ref, out_ref):
    core = (first_ref[0] // ROWS) % 2
    mine, other = load_run(mine_ref), load_run(other_ref)
    store_run(out_ref, *after(pick(core == 0, mine, other), pick(core == 0, other, mine)))


def row_kernel(first_ref, mine_ref, below_ref, above_ref, across_ref, prefix_ref, total_ref):
    y = (first_ref[0] // (2 * ROWS)) % 4
    by_distance = [load_run(ref) for ref in (mine_ref, below_ref, across_ref, above_ref)]
    run = (jnp.zeros((SN, HALF), jnp.float32), jnp.ones((1, HALF), jnp.float32))
    prefix = run
    for place in range(4):
        distance = (y - place) % 4
        piece = by_distance[0]
        for d in range(1, 4):
            piece = pick(distance == d, by_distance[d], piece)
        prefix = pick(y == place, run, prefix)
        run = after(run, piece)
    store_run(prefix_ref, *prefix)
    store_run(total_ref, *run)


def carry_kernel(first_ref, row3_ref, row2_ref, row1_ref, prefix_ref, mine_ref, other_ref, keep_ref, send_ref):
    core = (first_ref[0] // ROWS) % 2
    run = load_run(row3_ref)
    for ref in (row2_ref, row1_ref, prefix_ref):
        run = after(run, load_run(ref))
    behind = after(run, pick(core == 0, load_run(mine_ref), load_run(other_ref)))
    keep_ref[...] = jnp.where(core == 0, run[0], behind[0]).astype(jnp.bfloat16)
    send_ref[...] = jnp.where(core == 0, behind[0], run[0]).astype(jnp.bfloat16)


def gate_kernel(first_ref, y_ref, z_ref, maps_ref, fac_ref, keep_ref, got_ref, act_ref):
    core = (first_ref[0] // ROWS) % 2
    keep, got = keep_ref[...], got_ref[...]
    state = jnp.concatenate([jnp.where(core == 0, keep, got), jnp.where(core == 0, got, keep)], axis=1)
    reads = jnp.dot(maps_ref[:, SN:], state, preferred_element_type=jnp.float32)
    y = y_ref[...] + reads * widen(fac_ref[...], spread())
    z = z_ref[...].astype(jnp.float32)
    act_ref[...] = (y * (z / (1.0 + jnp.exp(-z)))).astype(jnp.bfloat16)


class Attention:
    def __init__(self, len_ref, first_ref, q_ref, fetched, other, q_scr, kv_scr, kv_sem):
        self.first = first_ref[0]
        self.ends = ends_of(len_ref)
        self.mine = self.first // CHUNK
        self.low = start_of(self.first, self.ends) // CHUNK
        self.last_start = start_of(self.first + ROWS - 1, self.ends)
        self.arrays = (fetched, other)
        self.q_scr, self.kv_scr, self.kv_sem = q_scr, kv_scr, kv_sem
        for g in range(2):
            rows = slice(g * ROWS, (g + 1) * ROWS)
            scaled = q_ref[:, g * HD : (g + 1) * HD].astype(jnp.float32) * (LOG2E * HD**-0.5)
            high = scaled.astype(jnp.bfloat16)
            q_scr[rows, :HD] = high
            q_scr[rows, HD:] = (scaled - high.astype(jnp.float32)).astype(jnp.bfloat16)

    def count(self, far):
        return (self.mine - far - self.low) // 2 + 1

    def block(self, far, i):
        return self.mine - far - 2 * i

    def copy(self, far, i):
        block = self.block(far, i)
        x, y, core = block // 8, (block // 2) % 4, block % 2
        slot = jnp.where(core == 0, x * 4 + y, y * 4 + x)
        rows = pl.ds(pl.multiple_of(slot * CHUNK, CHUNK), CHUNK)
        to = far * (SLOTS // 2) + i
        return pltpu.make_async_copy(self.arrays[far].at[rows], self.kv_scr.at[to], self.kv_sem.at[to])

    def fetch(self, far):
        lax.fori_loop(0, self.count(far), lambda i, _: (self.copy(far, i).start(), 0)[1], 0)

    def scores(self, far, i, rows, masked):
        k = self.kv_scr[far * (SLOTS // 2) + i, :, :HD]
        s = lax.dot_general(
            self.q_scr[rows, :],
            jnp.concatenate([k, k], axis=1),
            (((1,), (1,)), ((), ())),
            preferred_element_type=jnp.float32,
        )
        if masked:
            pos = self.first + rows.start % ROWS + iota((rows.stop - rows.start, 1), 0)
            key = self.block(far, i) * CHUNK + iota((1, CHUNK), 1)
            s = jnp.where((key >= start_of(pos, self.ends)) & (key <= pos), s, LOW)
        return s

    def values(self, far, i):
        return jnp.concatenate([self.kv_scr[far * (SLOTS // 2) + i, :, HD:], jnp.ones((CHUNK, HD), jnp.bfloat16)], axis=1)

    def over_chunks(self, far, step, wait):
        def one_chunk(i, _):
            if wait:
                self.copy(far, i).wait()
            block = self.block(far, i)
            masked = (block == self.mine) | (block * CHUNK < self.last_start)
            pl.when(masked)(lambda: step(far, i, True))
            pl.when(jnp.logical_not(masked))(lambda: step(far, i, False))
            return 0

        lax.fori_loop(0, self.count(far), one_chunk, 0)

    def add(self, far, acc):
        def step(far, i, masked):
            v = self.values(far, i)
            for r in range(2 * ROWS // TILE):
                rows = slice(r * TILE, (r + 1) * TILE)
                p = jnp.exp2(self.scores(far, i, rows, masked)).astype(jnp.bfloat16)
                acc[rows, :] += jnp.dot(p, v, preferred_element_type=jnp.float32)

        self.over_chunks(far, step, True)

    def add_shifted(self, far, acc, m_scr):
        def step(far, i, masked):
            v = self.values(far, i)
            for r in range(2 * ROWS // TILE):
                rows = slice(r * TILE, (r + 1) * TILE)
                s = self.scores(far, i, rows, masked)
                old = m_scr[rows, :]
                m = jnp.maximum(old, jnp.max(s, axis=1, keepdims=True))
                alpha = jnp.exp2(old - m)
                p = jnp.exp2(s - jnp.concatenate([m] * (CHUNK // 128), axis=1)).astype(jnp.bfloat16)
                out = jnp.dot(p, v, preferred_element_type=jnp.float32)
                acc[rows, :] = acc[rows, :] * jnp.concatenate([alpha, alpha], axis=1) + out
                m_scr[rows, :] = m

        self.over_chunks(far, step, False)


def part_kernel(len_ref, first_ref, q_ref, fetched, acc_ref, q_scr, kv_scr, kv_sem):
    attention = Attention(len_ref, first_ref, q_ref, fetched, None, q_scr, kv_scr, kv_sem)
    attention.fetch(0)
    acc_ref[...] = jnp.zeros_like(acc_ref)
    attention.add(0, acc_ref)


def mix_kernel(
    len_ref,
    first_ref,
    q_ref,
    act_ref,
    acc_ref,
    fetched,
    other,
    wa_hbm,
    ws_hbm,
    o_hbm,
    q_scr,
    kv_scr,
    kv_sem,
    acc_scr,
    m_scr,
    w_scr,
    in_scr,
    o_scr,
    w_sem,
    o_sem,
):
    attention = Attention(len_ref, first_ref, q_ref, fetched, other, q_scr, kv_scr, kv_sem)
    attention.fetch(1)
    weights = [
        pltpu.make_async_copy(wa_hbm, w_scr.at[pl.ds(0, 2 * HD)], w_sem.at[0]),
        pltpu.make_async_copy(ws_hbm, w_scr.at[pl.ds(2 * HD, HP)], w_sem.at[1]),
    ]
    for copy in weights:
        copy.start()

    acc_scr[...] = acc_ref[...]
    attention.add(1, acc_scr)
    total = acc_scr[:, HD:]
    fine = (jnp.min(total) > 2.0**-60) & (jnp.max(total) < 2.0**110)

    @pl.when(jnp.logical_not(fine))
    def _():
        attention.fetch(0)
        lax.fori_loop(0, attention.count(0), lambda i, _: (attention.copy(0, i).wait(), 0)[1], 0)
        acc_scr[...] = jnp.zeros_like(acc_scr)
        m_scr[...] = jnp.full(m_scr.shape, LOW, jnp.float32)
        attention.add_shifted(0, acc_scr, m_scr)
        attention.add_shifted(1, acc_scr, m_scr)

    for g in range(2):
        rows = slice(g * ROWS, (g + 1) * ROWS)
        in_scr[:, g * HD : (g + 1) * HD] = (acc_scr[rows, :HD] / acc_scr[rows, HD:]).astype(jnp.bfloat16)
    in_scr[:, 2 * HD :] = act_ref[...]
    for copy in weights:
        copy.wait()

    def out_copy(i):
        cols = pl.ds(i * COLS, COLS)
        return pltpu.make_async_copy(o_scr.at[:, cols], o_hbm.at[:, cols], o_sem.at[i])

    for i in range(DM // COLS):
        cols = slice(i * COLS, (i + 1) * COLS)
        o_scr[:, cols] = jnp.dot(in_scr[...], w_scr[:, cols], preferred_element_type=jnp.float32).astype(jnp.bfloat16)
        out_copy(i).start()
    for i in range(DM // COLS):
        out_copy(i).wait()


def big(**more):
    return pltpu.CompilerParams(vmem_limit_bytes=56 * 2**20, **more)


def moved(block, route0, route1):
    pairs = []
    for x in range(4):
        for y in range(4):
            for core, route in enumerate((route0, route1)):
                to = route(x, y)
                if to is not None:
                    pairs.append((x * 8 + y * 2 + core, to[0] * 8 + to[1] * 2 + core))
    return lax.ppermute(block, "pack", pairs)


def lines(stage):
    rows = [[x * 8 + y * 2 + stage for y in range(4)] for x in range(4)]
    columns = [[x * 8 + y * 2 + 1 - stage for x in range(4)] for y in range(4)]
    return rows + columns


def along_x(distance):
    return lambda x, y: (x + distance, y) if x + distance < 4 else None


def along_y(distance):
    return lambda x, y: (x, (y + distance) % 4)


def swapped(block):
    return lax.ppermute(block, "pack", [(i, i ^ 1) for i in range(32)])


def call(kernel, shapes, ins, *args):
    return pl.pallas_call(
        kernel,
        out_shape=tuple(jax.ShapeDtypeStruct(shape, jnp.bfloat16) for shape in shapes),
        in_specs=[SMEM] + [VMEM] * ins,
        out_specs=(VMEM,) * len(shapes),
        compiler_params=big(),
        cost_estimate=pl.CostEstimate(flops=10**6, bytes_accessed=10**6, transcendentals=0),
    )(*args)


def local(
    queries,
    keys_values,
    ssm_values,
    ssm_gates,
    ssm_maps,
    step_size,
    decay_log,
    skip_gain,
    attn_out_weight,
    ssd_out_weight,
    lengths,
):
    first = jnp.reshape(lax.axis_index("pack") * ROWS, (1,)).astype(jnp.int32)
    kv = keys_values.reshape(ROWS, 2 * HD)
    nowhere = lambda x, y: None
    first_stage = lax.all_gather(kv, "pack", axis=0, tiled=True, axis_index_groups=lines(0))
    y_local, run_keep, run_send, fac = pl.pallas_call(
        ssd_kernel,
        out_shape=(
            jax.ShapeDtypeStruct((ROWS, HP), jnp.float32),
            jax.ShapeDtypeStruct((STATE_ROWS, HALF), jnp.bfloat16),
            jax.ShapeDtypeStruct((STATE_ROWS, HALF), jnp.bfloat16),
            jax.ShapeDtypeStruct((ROWS, HEADS), jnp.float32),
        ),
        in_specs=[SMEM] * 4 + [VMEM] * 3,
        out_specs=(VMEM, VMEM, VMEM, VMEM),
        compiler_params=big(),
        cost_estimate=pl.CostEstimate(flops=10**9, bytes_accessed=4 * 10**6, transcendentals=10**6),
        name="ssd_local",
    )(lengths, decay_log, skip_gain, first, ssm_values, ssm_maps, step_size.T)

    run = (STATE_ROWS, HALF)
    run_got = swapped(run_send)
    (chip,) = call(chip_kernel, [run], 2, first, run_keep, run_got)
    first_stage = lax.optimization_barrier((first_stage, chip))[0]
    fetched = lax.all_gather(first_stage, "pack", axis=0, tiled=True, axis_index_groups=lines(1))
    chips = [moved(chip, along_y(d), along_y(d)) for d in (1, 3, 2)]
    prefix, total = call(row_kernel, [run, run], 4, first, chip, *chips)
    rows = [moved(total, along_x(d), along_x(d)) for d in (3, 2, 1)]
    keep, send = call(carry_kernel, [(SN, HALF)] * 2, 6, first, *rows, prefix, run_keep, run_got)
    got = swapped(send)
    act = pl.pallas_call(
        gate_kernel,
        out_shape=jax.ShapeDtypeStruct((ROWS, HP), jnp.bfloat16),
        in_specs=[SMEM] + [VMEM] * 6,
        out_specs=VMEM,
        compiler_params=big(),
        cost_estimate=pl.CostEstimate(flops=10**8, bytes_accessed=3 * 10**6, transcendentals=3 * 10**5),
        name="gate",
    )(first, y_local, ssm_gates, ssm_maps, fac, keep, got)

    fetched = lax.optimization_barrier((fetched, act))[0]
    other = swapped(fetched)
    scores_scratch = [
        pltpu.VMEM((2 * ROWS, 2 * HD), jnp.bfloat16),
        pltpu.VMEM((SLOTS, CHUNK, 2 * HD), jnp.bfloat16),
        pltpu.SemaphoreType.DMA((SLOTS,)),
    ]
    partial = pl.pallas_call(
        part_kernel,
        out_shape=jax.ShapeDtypeStruct((2 * ROWS, 2 * HD), jnp.float32),
        in_specs=[SMEM] * 2 + [VMEM, ANY],
        out_specs=VMEM,
        scratch_shapes=scores_scratch,
        compiler_params=big(),
        cost_estimate=pl.CostEstimate(flops=9 * 10**9, bytes_accessed=5 * 10**6, transcendentals=5 * 10**6),
        name="part",
    )(lengths, first, queries, fetched)

    terms = pl.pallas_call(
        mix_kernel,
        out_shape=jax.ShapeDtypeStruct((ROWS, DM), jnp.bfloat16),
        in_specs=[SMEM] * 2 + [VMEM] * 3 + [ANY] * 4,
        out_specs=ANY,
        scratch_shapes=scores_scratch
        + [
            pltpu.VMEM((2 * ROWS, 2 * HD), jnp.float32),
            pltpu.VMEM((2 * ROWS, HD), jnp.float32),
            pltpu.VMEM((2 * HD + HP, DM), jnp.bfloat16),
            pltpu.VMEM((ROWS, 2 * HD + HP), jnp.bfloat16),
            pltpu.VMEM((ROWS, DM), jnp.bfloat16),
            pltpu.SemaphoreType.DMA((2,)),
            pltpu.SemaphoreType.DMA((DM // COLS,)),
        ],
        compiler_params=big(),
        cost_estimate=pl.CostEstimate(flops=9 * 10**9, bytes_accessed=25 * 10**6, transcendentals=9 * 10**6),
        name="mix",
    )(lengths, first, queries, act, partial, fetched, other, attn_out_weight, ssd_out_weight)
    return lax.psum_scatter(terms, "tp", scatter_dimension=0, tiled=True)


def solution(mesh):
    return jax.shard_map(
        local,
        mesh=mesh,
        in_specs=(
            P("pack", "tp"),
            P("pack", "tp", None),
            P("pack", "tp"),
            P("pack", "tp"),
            P("pack", None),
            P("pack", "tp"),
            P("tp"),
            P("tp"),
            P("tp", None),
            P("tp", None),
            P(),
        ),
        out_specs=P(("pack", "tp"), None),
        check_vma=False,
    )
```

```python
import jax
import jax.numpy as jnp
from jax import lax
from jax.experimental import pallas as pl
from jax.experimental.pallas import tpu as pltpu
from jax.sharding import PartitionSpec as P

ROWS = 512
BLOCK = 256
HD = 128
HEADS = 8
HP = 512
SN = 256
DM = 5120
CHUNK = 512
SLOTS = 18
TILE = 256
COLS = 1280
LOW = -1e30
LOG2E = 1.4426950408889634
HIGH = lax.Precision.HIGHEST
HALF = HP // 2
STATE_ROWS = SN + 16
VMEM = pl.BlockSpec(memory_space=pltpu.VMEM)
SMEM = pl.BlockSpec(memory_space=pltpu.SMEM)
ANY = pl.BlockSpec(memory_space=pl.ANY)


def iota(shape, dim):
    return lax.broadcasted_iota(jnp.int32, shape, dim)


def ends_of(len_ref):
    e0 = len_ref[0]
    e1 = e0 + len_ref[1]
    return e0, e1, e1 + len_ref[2]


def start_of(pos, ends):
    e0, e1, e2 = ends
    zero = jnp.zeros_like(pos)
    out = jnp.where(pos >= e0, zero + e0, zero)
    out = jnp.where(pos >= e1, zero + e1, out)
    return jnp.where(pos >= e2, zero + e2, out)


def spread():
    return (iota((HEADS, HP), 1) // (HP // HEADS) == iota((HEADS, HP), 0)).astype(jnp.float32)


def widen(a, expand):
    return jnp.dot(a, expand, precision=HIGH, preferred_element_type=jnp.float32)


def ssd_kernel(len_ref, dl_ref, skip_ref, first_ref, x_ref, maps_ref, step_ref, y_ref, keep_ref, send_ref, fac_ref):
    first = first_ref[0]
    ends = ends_of(len_ref)
    expand = spread()
    head_sub = iota((HEADS, 1), 0)
    wide_lane = iota((1, HP), 1) // (HP // HEADS)
    rate = jnp.zeros((HEADS, 1), jnp.float32)
    skip = jnp.zeros((1, HP), jnp.float32)
    for h in range(HEADS):
        rate = jnp.where(head_sub == h, dl_ref[h], rate)
        skip = jnp.where(wide_lane == h, skip_ref[h], skip)
    rate = -jnp.exp(rate)
    row = iota((BLOCK, 1), 0)
    col = iota((1, BLOCK), 1)
    tri = (row >= col).astype(jnp.float32)
    half = iota((1, 128), 1) < 64
    state = None
    before = None
    for n in range(ROWS // BLOCK):
        rows = slice(n * BLOCK, (n + 1) * BLOCK)
        base = first + n * BLOCK
        start_col = start_of(base + row, ends)
        last_start = start_of(base + (BLOCK - 1), ends)
        cum_t = lax.dot_general(
            rate * step_ref[:, rows], tri, (((1,), (1,)), ((), ())), precision=HIGH, preferred_element_type=jnp.float32
        )
        cum = cum_t.T
        write = maps_ref[rows, :SN]
        read = maps_ref[rows, SN:]
        prod = lax.dot_general(read, write, (((1,), (1,)), ((), ())), preferred_element_type=jnp.float32)
        allowed = (base + col >= start_col) & (col <= row)
        for pair in range(HEADS // 2):
            lanes = slice(pair * 128, (pair + 1) * 128)
            x = x_ref[rows, lanes]
            total = skip[:, lanes] * x.astype(jnp.float32)
            for which in range(2):
                h = pair * 2 + which
                gap = jnp.where(allowed, cum[:, h : h + 1] - cum_t[h : h + 1, :], LOW)
                weights = (jnp.exp(gap) * prod).astype(jnp.bfloat16)
                part = jnp.where(half if which == 0 else ~half, x, jnp.zeros_like(x))
                total = total + jnp.dot(weights, part, preferred_element_type=jnp.float32)
            y_ref[rows, lanes] = total
        ecum = jnp.exp(cum)
        if state is not None:
            local = widen(jnp.where(start_col < base, ecum, 0.0), expand)
            reads = jnp.dot(read, state.astype(jnp.bfloat16), preferred_element_type=jnp.float32)
            y_ref[rows, :] += reads * local
        carry = jnp.where(start_col < first, ecum, 0.0)
        if before is not None:
            carry = carry * before
        fac_ref[rows, :] = carry
        tail = jnp.exp(cum[BLOCK - 1 : BLOCK, :] - cum)
        tail = widen(jnp.where(base + row >= last_start, tail, 0.0), expand)
        weighted = (x_ref[rows, :].astype(jnp.float32) * tail).astype(jnp.bfloat16)
        new = lax.dot_general(write, weighted, (((0,), (0,)), ((), ())), preferred_element_type=jnp.float32)
        end = ecum[BLOCK - 8 :, :]
        if state is not None:
            keep = jnp.where(last_start < base, 1.0, 0.0)
            new = new + (keep * widen(end, expand)[7:8, :]) * state
            end = end * before
        state = new
        before = end[7:8, :]
    through = jnp.where(last_start < first, 1.0, 0.0) * widen(end, expand)[7:8, :]
    core = (first // ROWS) % 2
    left, right = slice(0, HALF), slice(HALF, HP)
    for ref, wanted in ((keep_ref, 0), (send_ref, 1)):
        store_run(
            ref,
            jnp.where(core == wanted, state[:, left], state[:, right]),
            jnp.where(core == wanted, through[:, left], through[:, right]),
        )


def store_run(ref, state, through):
    high = through.astype(jnp.bfloat16).astype(jnp.float32)
    low = through - high
    sub = iota((16, 1), 0)
    ref[:SN, :] = state.astype(jnp.bfloat16)
    ref[SN:, :] = jnp.where(sub == 0, high, jnp.where(sub == 1, low, 0.0)).astype(jnp.bfloat16)


def load_run(ref):
    tail = ref[SN:, :].astype(jnp.float32)
    return ref[:SN, :].astype(jnp.float32), tail[0:1, :] + tail[1:2, :]


def pick(cond, one, other):
    return jnp.where(cond, one[0], other[0]), jnp.where(cond, one[1], other[1])


def after(earlier, later):
    return later[0] + later[1] * earlier[0], earlier[1] * later[1]


def chip_kernel(first_ref, mine_ref, other_ref, out_ref):
    core = (first_ref[0] // ROWS) % 2
    mine, other = load_run(mine_ref), load_run(other_ref)
    store_run(out_ref, *after(pick(core == 0, mine, other), pick(core == 0, other, mine)))


def row_kernel(first_ref, mine_ref, below_ref, above_ref, across_ref, prefix_ref, total_ref):
    y = (first_ref[0] // (2 * ROWS)) % 4
    by_distance = [load_run(ref) for ref in (mine_ref, below_ref, across_ref, above_ref)]
    run = (jnp.zeros((SN, HALF), jnp.float32), jnp.ones((1, HALF), jnp.float32))
    prefix = run
    for place in range(4):
        distance = (y - place) % 4
        piece = by_distance[0]
        for d in range(1, 4):
            piece = pick(distance == d, by_distance[d], piece)
        prefix = pick(y == place, run, prefix)
        run = after(run, piece)
    store_run(prefix_ref, *prefix)
    store_run(total_ref, *run)


def carry_kernel(first_ref, row3_ref, row2_ref, row1_ref, prefix_ref, mine_ref, other_ref, keep_ref, send_ref):
    core = (first_ref[0] // ROWS) % 2
    run = load_run(row3_ref)
    for ref in (row2_ref, row1_ref, prefix_ref):
        run = after(run, load_run(ref))
    behind = after(run, pick(core == 0, load_run(mine_ref), load_run(other_ref)))
    keep_ref[...] = jnp.where(core == 0, run[0], behind[0]).astype(jnp.bfloat16)
    send_ref[...] = jnp.where(core == 0, behind[0], run[0]).astype(jnp.bfloat16)


def gate_kernel(first_ref, y_ref, z_ref, maps_ref, fac_ref, keep_ref, got_ref, act_ref):
    core = (first_ref[0] // ROWS) % 2
    keep, got = keep_ref[...], got_ref[...]
    state = jnp.concatenate([jnp.where(core == 0, keep, got), jnp.where(core == 0, got, keep)], axis=1)
    reads = jnp.dot(maps_ref[:, SN:], state, preferred_element_type=jnp.float32)
    y = y_ref[...] + reads * widen(fac_ref[...], spread())
    z = z_ref[...].astype(jnp.float32)
    act_ref[...] = (y * (z / (1.0 + jnp.exp(-z)))).astype(jnp.bfloat16)


class Attention:
    def __init__(self, len_ref, first_ref, q_ref, fetched, other, q_scr, kv_scr, kv_sem, near_only=False):
        self.first = first_ref[0]
        self.ends = ends_of(len_ref)
        self.mine = self.first // CHUNK
        self.low = start_of(self.first, self.ends) // CHUNK
        self.last_start = start_of(self.first + ROWS - 1, self.ends)
        self.arrays = (fetched, other)
        self.near_only, self.every = near_only, False
        self.q_scr, self.kv_scr, self.kv_sem = q_scr, kv_scr, kv_sem
        for g in range(2):
            rows = slice(g * ROWS, (g + 1) * ROWS)
            scaled = q_ref[:, g * HD : (g + 1) * HD].astype(jnp.float32) * (LOG2E * HD**-0.5)
            high = scaled.astype(jnp.bfloat16)
            q_scr[rows, :HD] = high
            q_scr[rows, HD:] = (scaled - high.astype(jnp.float32)).astype(jnp.bfloat16)

    def count(self, far):
        return 4 if self.near_only else (self.mine - far - self.low) // 2 + 1

    def block(self, far, i):
        if not self.near_only:
            return self.mine - far - 2 * i
        core = self.mine % 2
        step = jnp.where(core == far, 2, 8)
        return self.mine + jnp.where(core == 0, far, -far) - step * i

    def in_line(self, far, i):
        block = self.block(far, i)
        row = block // 8 == self.mine // 8
        column = (block // 2) % 4 == (self.mine // 2) % 4
        return jnp.where(block % 2 == 0, row, column)

    def wanted(self, far, i):
        block = self.block(far, i)
        if self.near_only:
            return (block >= self.low) & (block <= self.mine) & self.in_line(far, i)
        return self.every | jnp.logical_not(self.in_line(far, i))

    def copy(self, far, i):
        block = self.block(far, i)
        x, y, even = block // 8, (block // 2) % 4, block % 2 == 0
        my_x, my_y = self.mine // 8, (self.mine // 2) % 4
        distance = jnp.where(even, (my_y - y) % 4, (my_x - x) % 4)
        slot = distance ^ (distance >> 1)
        if not self.near_only:
            slot = slot + 4 * jnp.where(even, x, y)
        rows = pl.ds(pl.multiple_of(slot * CHUNK, CHUNK), CHUNK)
        to = far * (SLOTS // 2) + i
        return pltpu.make_async_copy(self.arrays[far].at[rows], self.kv_scr.at[to], self.kv_sem.at[to])

    def fetch(self, far):
        def one_chunk(i, _):
            pl.when(self.wanted(far, i))(lambda: self.copy(far, i).start())
            return 0

        lax.fori_loop(0, self.count(far), one_chunk, 0)

    def arrive(self, far):
        def one_chunk(i, _):
            pl.when(self.wanted(far, i))(lambda: self.copy(far, i).wait())
            return 0

        lax.fori_loop(0, self.count(far), one_chunk, 0)

    def scores(self, far, i, rows, masked):
        k = self.kv_scr[far * (SLOTS // 2) + i, :, :HD]
        s = lax.dot_general(
            self.q_scr[rows, :],
            jnp.concatenate([k, k], axis=1),
            (((1,), (1,)), ((), ())),
            preferred_element_type=jnp.float32,
        )
        if masked:
            pos = self.first + rows.start % ROWS + iota((rows.stop - rows.start, 1), 0)
            key = self.block(far, i) * CHUNK + iota((1, CHUNK), 1)
            s = jnp.where((key >= start_of(pos, self.ends)) & (key <= pos), s, LOW)
        return s

    def values(self, far, i):
        return jnp.concatenate([self.kv_scr[far * (SLOTS // 2) + i, :, HD:], jnp.ones((CHUNK, HD), jnp.bfloat16)], axis=1)

    def over_chunks(self, far, step, wait):
        def one_chunk(i, _):
            wanted = self.wanted(far, i)
            if wait:
                pl.when(wanted)(lambda: self.copy(far, i).wait())
            block = self.block(far, i)
            masked = (block == self.mine) | (block * CHUNK < self.last_start)
            pl.when(wanted & masked)(lambda: step(far, i, True))
            pl.when(wanted & jnp.logical_not(masked))(lambda: step(far, i, False))
            return 0

        lax.fori_loop(0, self.count(far), one_chunk, 0)

    def add(self, far, acc):
        def step(far, i, masked):
            v = self.values(far, i)
            for r in range(2 * ROWS // TILE):
                rows = slice(r * TILE, (r + 1) * TILE)
                p = jnp.exp2(self.scores(far, i, rows, masked)).astype(jnp.bfloat16)
                acc[rows, :] += jnp.dot(p, v, preferred_element_type=jnp.float32)

        self.over_chunks(far, step, True)

    def add_shifted(self, far, acc, m_scr):
        def step(far, i, masked):
            v = self.values(far, i)
            for r in range(2 * ROWS // TILE):
                rows = slice(r * TILE, (r + 1) * TILE)
                s = self.scores(far, i, rows, masked)
                old = m_scr[rows, :]
                m = jnp.maximum(old, jnp.max(s, axis=1, keepdims=True))
                alpha = jnp.exp2(old - m)
                p = jnp.exp2(s - jnp.concatenate([m] * (CHUNK // 128), axis=1)).astype(jnp.bfloat16)
                out = jnp.dot(p, v, preferred_element_type=jnp.float32)
                acc[rows, :] = acc[rows, :] * jnp.concatenate([alpha, alpha], axis=1) + out
                m_scr[rows, :] = m

        self.over_chunks(far, step, False)


def line_kernel(len_ref, first_ref, q_ref, line, line_got, acc_ref, q_scr, kv_scr, kv_sem):
    attention = Attention(len_ref, first_ref, q_ref, line, line_got, q_scr, kv_scr, kv_sem, near_only=True)
    attention.fetch(0)
    attention.fetch(1)
    acc_ref[...] = jnp.zeros_like(acc_ref)
    attention.add(0, acc_ref)
    attention.add(1, acc_ref)


def part_kernel(len_ref, first_ref, q_ref, before_ref, fetched, acc_ref, q_scr, kv_scr, kv_sem):
    attention = Attention(len_ref, first_ref, q_ref, fetched, None, q_scr, kv_scr, kv_sem)
    attention.fetch(0)
    acc_ref[...] = before_ref[...]
    attention.add(0, acc_ref)


def mix_kernel(
    len_ref,
    first_ref,
    q_ref,
    act_ref,
    acc_ref,
    fetched,
    other,
    wa_hbm,
    ws_hbm,
    o_hbm,
    q_scr,
    kv_scr,
    kv_sem,
    acc_scr,
    m_scr,
    w_scr,
    in_scr,
    o_scr,
    w_sem,
    o_sem,
):
    attention = Attention(len_ref, first_ref, q_ref, fetched, other, q_scr, kv_scr, kv_sem)
    attention.fetch(1)
    weights = [
        pltpu.make_async_copy(wa_hbm, w_scr.at[pl.ds(0, 2 * HD)], w_sem.at[0]),
        pltpu.make_async_copy(ws_hbm, w_scr.at[pl.ds(2 * HD, HP)], w_sem.at[1]),
    ]
    for copy in weights:
        copy.start()

    acc_scr[...] = acc_ref[...]
    attention.add(1, acc_scr)
    total = acc_scr[:, HD:]
    fine = (jnp.min(total) > 2.0**-60) & (jnp.max(total) < 2.0**110)

    @pl.when(jnp.logical_not(fine))
    def _():
        attention.every = True
        for far in range(2):
            attention.fetch(far)
            attention.arrive(far)
        acc_scr[...] = jnp.zeros_like(acc_scr)
        m_scr[...] = jnp.full(m_scr.shape, LOW, jnp.float32)
        attention.add_shifted(0, acc_scr, m_scr)
        attention.add_shifted(1, acc_scr, m_scr)

    for g in range(2):
        rows = slice(g * ROWS, (g + 1) * ROWS)
        in_scr[:, g * HD : (g + 1) * HD] = (acc_scr[rows, :HD] / acc_scr[rows, HD:]).astype(jnp.bfloat16)
    in_scr[:, 2 * HD :] = act_ref[...]
    for copy in weights:
        copy.wait()

    def out_copy(i):
        cols = pl.ds(i * COLS, COLS)
        return pltpu.make_async_copy(o_scr.at[:, cols], o_hbm.at[:, cols], o_sem.at[i])

    for i in range(DM // COLS):
        cols = slice(i * COLS, (i + 1) * COLS)
        o_scr[:, cols] = jnp.dot(in_scr[...], w_scr[:, cols], preferred_element_type=jnp.float32).astype(jnp.bfloat16)
        out_copy(i).start()
    for i in range(DM // COLS):
        out_copy(i).wait()


def big(**more):
    return pltpu.CompilerParams(vmem_limit_bytes=56 * 2**20, **more)


def moved(block, route0, route1):
    pairs = []
    for x in range(4):
        for y in range(4):
            for core, route in enumerate((route0, route1)):
                to = route(x, y)
                if to is not None:
                    pairs.append((x * 8 + y * 2 + core, to[0] * 8 + to[1] * 2 + core))
    return lax.ppermute(block, "pack", pairs)


def lines():
    columns = [[x * 8 + y * 2 for x in range(4)] for y in range(4)]
    rows = [[x * 8 + y * 2 + 1 for y in range(4)] for x in range(4)]
    return columns + rows


def along_x(distance):
    return lambda x, y: (x + distance, y) if x + distance < 4 else None


def along_y(distance):
    return lambda x, y: (x, (y + distance) % 4)


def swapped(block):
    return lax.ppermute(block, "pack", [(i, i ^ 1) for i in range(32)])


def call(kernel, shapes, ins, *args):
    return pl.pallas_call(
        kernel,
        out_shape=tuple(jax.ShapeDtypeStruct(shape, jnp.bfloat16) for shape in shapes),
        in_specs=[SMEM] + [VMEM] * ins,
        out_specs=(VMEM,) * len(shapes),
        compiler_params=big(),
        cost_estimate=pl.CostEstimate(flops=10**6, bytes_accessed=10**6, transcendentals=0),
    )(*args)


def local(
    queries,
    keys_values,
    ssm_values,
    ssm_gates,
    ssm_maps,
    step_size,
    decay_log,
    skip_gain,
    attn_out_weight,
    ssd_out_weight,
    lengths,
):
    first = jnp.reshape(lax.axis_index("pack") * ROWS, (1,)).astype(jnp.int32)
    kv = keys_values.reshape(ROWS, 2 * HD)
    nowhere = lambda x, y: None
    below = moved(kv, along_y(1), along_x(1))
    above = moved(kv, along_y(3), along_x(3))
    across = moved(kv, along_y(2), along_x(2))
    y_local, run_keep, run_send, fac = pl.pallas_call(
        ssd_kernel,
        out_shape=(
            jax.ShapeDtypeStruct((ROWS, HP), jnp.float32),
            jax.ShapeDtypeStruct((STATE_ROWS, HALF), jnp.bfloat16),
            jax.ShapeDtypeStruct((STATE_ROWS, HALF), jnp.bfloat16),
            jax.ShapeDtypeStruct((ROWS, HEADS), jnp.float32),
        ),
        in_specs=[SMEM] * 4 + [VMEM] * 3,
        out_specs=(VMEM, VMEM, VMEM, VMEM),
        compiler_params=big(),
        cost_estimate=pl.CostEstimate(flops=10**9, bytes_accessed=4 * 10**6, transcendentals=10**6),
        name="ssd_local",
    )(lengths, decay_log, skip_gain, first, ssm_values, ssm_maps, step_size.T)

    below, above, across = lax.optimization_barrier((below, above, across, fac))[:3]
    line = jnp.concatenate([kv, below, above, across], axis=0)
    fetched = lax.all_gather(line, "pack", axis=0, tiled=True, axis_index_groups=lines())
    line_got = swapped(line)

    run = (STATE_ROWS, HALF)
    run_got = swapped(run_send)
    (chip,) = call(chip_kernel, [run], 2, first, run_keep, run_got)
    chips = [moved(chip, along_y(d), along_y(d)) for d in (1, 3, 2)]
    prefix, total = call(row_kernel, [run, run], 4, first, chip, *chips)
    rows = [moved(total, along_x(d), along_x(d)) for d in (3, 2, 1)]
    line_got = lax.optimization_barrier((line_got, prefix))[0]
    scores_scratch = [
        pltpu.VMEM((2 * ROWS, 2 * HD), jnp.bfloat16),
        pltpu.VMEM((SLOTS, CHUNK, 2 * HD), jnp.bfloat16),
        pltpu.SemaphoreType.DMA((SLOTS,)),
    ]
    attention_out = jax.ShapeDtypeStruct((2 * ROWS, 2 * HD), jnp.float32)
    near = pl.pallas_call(
        line_kernel,
        out_shape=attention_out,
        in_specs=[SMEM] * 2 + [VMEM] + [ANY] * 2,
        out_specs=VMEM,
        scratch_shapes=scores_scratch,
        compiler_params=big(),
        cost_estimate=pl.CostEstimate(flops=4 * 10**9, bytes_accessed=5 * 10**6, transcendentals=5 * 10**6),
        name="line",
    )(lengths, first, queries, line, line_got)
    rows = lax.optimization_barrier((*rows, near))[:3]
    keep, send = call(carry_kernel, [(SN, HALF)] * 2, 6, first, *rows, prefix, run_keep, run_got)
    got = swapped(send)
    act = pl.pallas_call(
        gate_kernel,
        out_shape=jax.ShapeDtypeStruct((ROWS, HP), jnp.bfloat16),
        in_specs=[SMEM] + [VMEM] * 6,
        out_specs=VMEM,
        compiler_params=big(),
        cost_estimate=pl.CostEstimate(flops=10**8, bytes_accessed=3 * 10**6, transcendentals=3 * 10**5),
        name="gate",
    )(first, y_local, ssm_gates, ssm_maps, fac, keep, got)

    fetched = lax.optimization_barrier((fetched, act))[0]
    other = swapped(fetched)
    partial = pl.pallas_call(
        part_kernel,
        out_shape=attention_out,
        in_specs=[SMEM] * 2 + [VMEM] * 2 + [ANY],
        out_specs=VMEM,
        scratch_shapes=scores_scratch,
        compiler_params=big(),
        cost_estimate=pl.CostEstimate(flops=9 * 10**9, bytes_accessed=5 * 10**6, transcendentals=5 * 10**6),
        name="part",
    )(lengths, first, queries, near, fetched)

    terms = pl.pallas_call(
        mix_kernel,
        out_shape=jax.ShapeDtypeStruct((ROWS, DM), jnp.bfloat16),
        in_specs=[SMEM] * 2 + [VMEM] * 3 + [ANY] * 4,
        out_specs=ANY,
        scratch_shapes=scores_scratch
        + [
            pltpu.VMEM((2 * ROWS, 2 * HD), jnp.float32),
            pltpu.VMEM((2 * ROWS, HD), jnp.float32),
            pltpu.VMEM((2 * HD + HP, DM), jnp.bfloat16),
            pltpu.VMEM((ROWS, 2 * HD + HP), jnp.bfloat16),
            pltpu.VMEM((ROWS, DM), jnp.bfloat16),
            pltpu.SemaphoreType.DMA((2,)),
            pltpu.SemaphoreType.DMA((DM // COLS,)),
        ],
        compiler_params=big(),
        cost_estimate=pl.CostEstimate(flops=9 * 10**9, bytes_accessed=25 * 10**6, transcendentals=9 * 10**6),
        name="mix",
    )(lengths, first, queries, act, partial, fetched, other, attn_out_weight, ssd_out_weight)
    return lax.psum_scatter(terms, "tp", scatter_dimension=0, tiled=True)


def solution(mesh):
    return jax.shard_map(
        local,
        mesh=mesh,
        in_specs=(
            P("pack", "tp"),
            P("pack", "tp", None),
            P("pack", "tp"),
            P("pack", "tp"),
            P("pack", None),
            P("pack", "tp"),
            P("tp"),
            P("tp"),
            P("tp", None),
            P("tp", None),
            P(),
        ),
        out_specs=P(("pack", "tp"), None),
        check_vma=False,
    )
```

```python
import jax
import jax.numpy as jnp
from jax import lax
from jax.experimental import pallas as pl
from jax.experimental.pallas import tpu as pltpu
from jax.sharding import PartitionSpec as P

ROWS = 512
BLOCK = 256
HD = 128
HEADS = 8
HP = 512
SN = 256
DM = 5120
CHUNK = 512
SLOTS = 18
TILE = 256
COLS = 1280
LOW = -1e30
LOG2E = 1.4426950408889634
HIGH = lax.Precision.HIGHEST
LIMIT = 62 * 2**20
HALF = HP // 2
STATE_ROWS = SN + 16
VMEM = pl.BlockSpec(memory_space=pltpu.VMEM)
SMEM = pl.BlockSpec(memory_space=pltpu.SMEM)
ANY = pl.BlockSpec(memory_space=pl.ANY)


def iota(shape, dim):
    return lax.broadcasted_iota(jnp.int32, shape, dim)


def ends_of(len_ref):
    e0 = len_ref[0]
    e1 = e0 + len_ref[1]
    return e0, e1, e1 + len_ref[2]


def start_of(pos, ends):
    e0, e1, e2 = ends
    zero = jnp.zeros_like(pos)
    out = jnp.where(pos >= e0, zero + e0, zero)
    out = jnp.where(pos >= e1, zero + e1, out)
    return jnp.where(pos >= e2, zero + e2, out)


def spread():
    return (iota((HEADS, HP), 1) // (HP // HEADS) == iota((HEADS, HP), 0)).astype(jnp.float32)


def widen(a, expand):
    return jnp.dot(a, expand, precision=HIGH, preferred_element_type=jnp.float32)


def ssd_kernel(len_ref, dl_ref, skip_ref, first_ref, x_ref, maps_ref, step_ref, y_ref, keep_ref, send_ref, fac_ref):
    first = first_ref[0]
    ends = ends_of(len_ref)
    expand = spread()
    head_sub = iota((HEADS, 1), 0)
    wide_lane = iota((1, HP), 1) // (HP // HEADS)
    rate = jnp.zeros((HEADS, 1), jnp.float32)
    skip = jnp.zeros((1, HP), jnp.float32)
    for h in range(HEADS):
        rate = jnp.where(head_sub == h, dl_ref[h], rate)
        skip = jnp.where(wide_lane == h, skip_ref[h], skip)
    rate = -jnp.exp(rate)
    row = iota((BLOCK, 1), 0)
    col = iota((1, BLOCK), 1)
    tri = (row >= col).astype(jnp.float32)
    half = iota((1, 128), 1) < 64
    state = None
    before = None
    for n in range(ROWS // BLOCK):
        rows = slice(n * BLOCK, (n + 1) * BLOCK)
        base = first + n * BLOCK
        start_col = start_of(base + row, ends)
        last_start = start_of(base + (BLOCK - 1), ends)
        cum_t = lax.dot_general(
            rate * step_ref[:, rows], tri, (((1,), (1,)), ((), ())), precision=HIGH, preferred_element_type=jnp.float32
        )
        cum = cum_t.T
        write = maps_ref[rows, :SN]
        read = maps_ref[rows, SN:]
        prod = lax.dot_general(read, write, (((1,), (1,)), ((), ())), preferred_element_type=jnp.float32)
        allowed = (base + col >= start_col) & (col <= row)
        for pair in range(HEADS // 2):
            lanes = slice(pair * 128, (pair + 1) * 128)
            x = x_ref[rows, lanes]
            total = skip[:, lanes] * x.astype(jnp.float32)
            for which in range(2):
                h = pair * 2 + which
                gap = jnp.where(allowed, cum[:, h : h + 1] - cum_t[h : h + 1, :], LOW)
                weights = (jnp.exp(gap) * prod).astype(jnp.bfloat16)
                part = jnp.where(half if which == 0 else ~half, x, jnp.zeros_like(x))
                total = total + jnp.dot(weights, part, preferred_element_type=jnp.float32)
            y_ref[rows, lanes] = total
        ecum = jnp.exp(cum)
        if state is not None:
            local = widen(jnp.where(start_col < base, ecum, 0.0), expand)
            reads = jnp.dot(read, state.astype(jnp.bfloat16), preferred_element_type=jnp.float32)
            y_ref[rows, :] += reads * local
        carry = jnp.where(start_col < first, ecum, 0.0)
        if before is not None:
            carry = carry * before
        fac_ref[rows, :] = carry
        tail = jnp.exp(cum[BLOCK - 1 : BLOCK, :] - cum)
        tail = widen(jnp.where(base + row >= last_start, tail, 0.0), expand)
        weighted = (x_ref[rows, :].astype(jnp.float32) * tail).astype(jnp.bfloat16)
        new = lax.dot_general(write, weighted, (((0,), (0,)), ((), ())), preferred_element_type=jnp.float32)
        end = ecum[BLOCK - 8 :, :]
        if state is not None:
            keep = jnp.where(last_start < base, 1.0, 0.0)
            new = new + (keep * widen(end, expand)[7:8, :]) * state
            end = end * before
        state = new
        before = end[7:8, :]
    through = jnp.where(last_start < first, 1.0, 0.0) * widen(end, expand)[7:8, :]
    core = (first // ROWS) % 2
    left, right = slice(0, HALF), slice(HALF, HP)
    for ref, wanted in ((keep_ref, 0), (send_ref, 1)):
        store_run(
            ref,
            jnp.where(core == wanted, state[:, left], state[:, right]),
            jnp.where(core == wanted, through[:, left], through[:, right]),
        )


def store_run(ref, state, through):
    high = through.astype(jnp.bfloat16).astype(jnp.float32)
    low = through - high
    sub = iota((16, 1), 0)
    ref[:SN, :] = state.astype(jnp.bfloat16)
    ref[SN:, :] = jnp.where(sub == 0, high, jnp.where(sub == 1, low, 0.0)).astype(jnp.bfloat16)


def load_run(ref):
    tail = ref[SN:, :].astype(jnp.float32)
    return ref[:SN, :].astype(jnp.float32), tail[0:1, :] + tail[1:2, :]


def pick(cond, one, other):
    return jnp.where(cond, one[0], other[0]), jnp.where(cond, one[1], other[1])


def after(earlier, later):
    return later[0] + later[1] * earlier[0], earlier[1] * later[1]


def chip_kernel(first_ref, mine_ref, other_ref, out_ref):
    core = (first_ref[0] // ROWS) % 2
    mine, other = load_run(mine_ref), load_run(other_ref)
    store_run(out_ref, *after(pick(core == 0, mine, other), pick(core == 0, other, mine)))


def row_kernel(first_ref, mine_ref, below_ref, above_ref, across_ref, prefix_ref, total_ref):
    y = (first_ref[0] // (2 * ROWS)) % 4
    by_distance = [load_run(ref) for ref in (mine_ref, below_ref, across_ref, above_ref)]
    run = (jnp.zeros((SN, HALF), jnp.float32), jnp.ones((1, HALF), jnp.float32))
    prefix = run
    for place in range(4):
        distance = (y - place) % 4
        piece = by_distance[0]
        for d in range(1, 4):
            piece = pick(distance == d, by_distance[d], piece)
        prefix = pick(y == place, run, prefix)
        run = after(run, piece)
    store_run(prefix_ref, *prefix)
    store_run(total_ref, *run)


def carry_kernel(first_ref, row3_ref, row2_ref, row1_ref, prefix_ref, mine_ref, other_ref, keep_ref, send_ref):
    core = (first_ref[0] // ROWS) % 2
    run = load_run(row3_ref)
    for ref in (row2_ref, row1_ref, prefix_ref):
        run = after(run, load_run(ref))
    behind = after(run, pick(core == 0, load_run(mine_ref), load_run(other_ref)))
    keep_ref[...] = jnp.where(core == 0, run[0], behind[0]).astype(jnp.bfloat16)
    send_ref[...] = jnp.where(core == 0, behind[0], run[0]).astype(jnp.bfloat16)


def gate_kernel(first_ref, y_ref, z_ref, read_ref, fac_ref, keep_ref, got_ref, act_ref):
    core = (first_ref[0] // ROWS) % 2
    keep, got = keep_ref[...], got_ref[...]
    state = jnp.concatenate([jnp.where(core == 0, keep, got), jnp.where(core == 0, got, keep)], axis=1)
    reads = jnp.dot(read_ref[...], state, preferred_element_type=jnp.float32)
    y = y_ref[...] + reads * widen(fac_ref[...], spread())
    z = z_ref[...].astype(jnp.float32)
    act_ref[...] = (y * (z / (1.0 + jnp.exp(-z)))).astype(jnp.bfloat16)


class Attention:
    def __init__(self, len_ref, first_ref, fetched, other, q_scr, kv_scr, ids, kv_sem, near_only=False):
        self.first = first_ref[0]
        self.ends = ends_of(len_ref)
        self.mine = self.first // CHUNK
        self.low = start_of(self.first, self.ends) // CHUNK
        self.last_start = start_of(self.first + ROWS - 1, self.ends)
        self.arrays = (fetched, other)
        self.near_only = near_only
        self.q_scr, self.kv_scr, self.ids, self.kv_sem = q_scr, kv_scr, ids, kv_sem

    def count(self, far):
        return 4 if self.near_only else (self.mine - far - self.low) // 2 + 1

    def block(self, far, i):
        if not self.near_only:
            return self.mine - far - 2 * i
        core = self.mine % 2
        step = jnp.where(core == far, 2, 8)
        return self.mine + jnp.where(core == 0, far, -far) - step * i

    def in_line(self, block):
        row = block // 8 == self.mine // 8
        column = (block // 2) % 4 == (self.mine // 2) % 4
        return jnp.where(block % 2 == 0, row, column)

    def place(self, block):
        x, y, even = block // 8, (block // 2) % 4, block % 2 == 0
        my_x, my_y = self.mine // 8, (self.mine // 2) % 4
        distance = jnp.where(even, (my_y - y) % 4, (my_x - x) % 4)
        place = distance ^ (distance >> 1)
        if not self.near_only:
            place = place + 4 * jnp.where(even, x, y)
        return place

    def copy(self, far, place, slot):
        rows = pl.ds(pl.multiple_of(place * CHUNK, CHUNK), CHUNK)
        to = pl.ds(pl.multiple_of(slot * CHUNK, CHUNK), CHUNK)
        return pltpu.make_async_copy(self.arrays[far].at[rows], self.kv_scr.at[to], self.kv_sem.at[slot])

    def fetch(self, fars, every=False):
        def one_chunk(far, i, carry):
            plain, masked = carry
            block = self.block(far, i)
            if self.near_only:
                wanted = (block >= self.low) & (block <= self.mine) & self.in_line(block)
            elif every:
                wanted = block >= self.low
            else:
                wanted = jnp.logical_not(self.in_line(block))
            mask = (block == self.mine) | (block * CHUNK < self.last_start)
            slot = jnp.where(mask, SLOTS - 1 - masked, plain)

            @pl.when(wanted)
            def _():
                self.ids[slot] = block
                self.copy(far, self.place(block), slot).start()

            new = wanted.astype(jnp.int32)
            return plain + jnp.where(mask, 0, new), masked + jnp.where(mask, new, 0)

        carry = (jnp.int32(0), jnp.int32(0))
        for far in fars:
            carry = lax.fori_loop(0, self.count(far), lambda i, c, far=far: one_chunk(far, i, c), carry)
        self.plain, self.masked = carry

    def wait(self, slot):
        self.copy(0, 0, slot).wait()

    def keys(self, slot, chunks):
        return pl.ds(pl.multiple_of(slot * CHUNK, CHUNK), chunks * CHUNK)

    def scores(self, slot, chunks, r, masked):
        rows = slice(r * TILE, (r + 1) * TILE)
        k = self.kv_scr[self.keys(slot, chunks), :HD]
        s = lax.dot_general(
            self.q_scr[rows, :],
            jnp.concatenate([k, k], axis=1),
            (((1,), (1,)), ((), ())),
            preferred_element_type=jnp.float32,
        )
        if masked:
            pos = self.first + rows.start % ROWS + iota((TILE, 1), 0)
            key = self.ids[slot] * CHUNK + iota((1, CHUNK), 1)
            s = jnp.where((key >= start_of(pos, self.ends)) & (key <= pos), s, LOW)
        return s

    def values(self, slot, chunks):
        v = self.kv_scr[self.keys(slot, chunks), HD:]
        return jnp.concatenate([v, jnp.ones((chunks * CHUNK, HD), jnp.bfloat16)], axis=1)

    def step(self, acc, slot, chunks, masked):
        v = self.values(slot, chunks)
        tiles = 2 * ROWS // TILE
        s = self.scores(slot, chunks, 0, masked)
        for r in range(tiles):
            following = self.scores(slot, chunks, r + 1, masked) if r + 1 < tiles else None
            p = jnp.exp2(s).astype(jnp.bfloat16)
            acc[r * TILE : (r + 1) * TILE, :] += jnp.dot(p, v, preferred_element_type=jnp.float32)
            s = following

    def add(self, acc):
        def one_masked(j, _):
            self.wait(SLOTS - 1 - j)
            self.step(acc, SLOTS - 1 - j, 1, True)
            return 0

        def two_plain(j, _):
            self.wait(2 * j)
            self.wait(2 * j + 1)
            self.step(acc, 2 * j, 2, False)
            return 0

        lax.fori_loop(0, self.masked, one_masked, 0)
        lax.fori_loop(0, self.plain // 2, two_plain, 0)

        @pl.when(self.plain % 2 == 1)
        def _():
            self.wait(self.plain - 1)
            self.step(acc, self.plain - 1, 1, False)

    def add_shifted(self, acc, m_scr):
        def one_chunk(j, _):
            slot = jnp.where(j < self.plain, j, SLOTS - 1 - (j - self.plain))
            self.wait(slot)
            v = self.values(slot, 1)
            for r in range(2 * ROWS // TILE):
                rows = slice(r * TILE, (r + 1) * TILE)
                s = self.scores(slot, 1, r, True)
                old = m_scr[rows, :]
                m = jnp.maximum(old, jnp.max(s, axis=1, keepdims=True))
                alpha = jnp.exp2(old - m)
                p = jnp.exp2(s - jnp.concatenate([m] * (CHUNK // 128), axis=1)).astype(jnp.bfloat16)
                out = jnp.dot(p, v, preferred_element_type=jnp.float32)
                acc[rows, :] = acc[rows, :] * jnp.concatenate([alpha, alpha], axis=1) + out
                m_scr[rows, :] = m
            return 0

        lax.fori_loop(0, self.plain + self.masked, one_chunk, 0)


def own_line_kernel(len_ref, first_ref, q_ref, line, acc_ref, split_ref, kv_scr, ids, kv_sem):
    attention = Attention(len_ref, first_ref, line, None, split_ref, kv_scr, ids, kv_sem, near_only=True)
    attention.fetch((0,))
    for g in range(2):
        rows = slice(g * ROWS, (g + 1) * ROWS)
        scaled = q_ref[:, g * HD : (g + 1) * HD].astype(jnp.float32) * (LOG2E * HD**-0.5)
        high = scaled.astype(jnp.bfloat16)
        split_ref[rows, :HD] = high
        split_ref[rows, HD:] = (scaled - high.astype(jnp.float32)).astype(jnp.bfloat16)
    acc_ref[...] = jnp.zeros_like(acc_ref)
    attention.add(acc_ref)


def other_line_kernel(len_ref, first_ref, split_ref, before_ref, line_got, acc_ref, kv_scr, ids, kv_sem):
    attention = Attention(len_ref, first_ref, line_got, line_got, split_ref, kv_scr, ids, kv_sem, near_only=True)
    attention.fetch((1,))
    acc_ref[...] = before_ref[...]
    attention.add(acc_ref)


def part_kernel(len_ref, first_ref, split_ref, before_ref, fetched, acc_ref, kv_scr, ids, kv_sem):
    attention = Attention(len_ref, first_ref, fetched, None, split_ref, kv_scr, ids, kv_sem)
    attention.fetch((0,))
    acc_ref[...] = before_ref[...]
    attention.add(acc_ref)


def mix_kernel(
    len_ref,
    first_ref,
    split_hbm,
    act_hbm,
    before_hbm,
    fetched,
    other,
    wa_hbm,
    ws_hbm,
    o_hbm,
    kv_scr,
    ids,
    kv_sem,
    q_scr,
    acc_scr,
    m_scr,
    w_scr,
    in_scr,
    o_scr,
    in_sem,
    w_sem,
    o_sem,
):
    attention = Attention(len_ref, first_ref, fetched, other, q_scr, kv_scr, ids, kv_sem)
    inputs = [
        pltpu.make_async_copy(split_hbm, q_scr, in_sem.at[0]),
        pltpu.make_async_copy(before_hbm, acc_scr, in_sem.at[1]),
        pltpu.make_async_copy(act_hbm, in_scr.at[:, pl.ds(2 * HD, HP)], in_sem.at[2]),
    ]
    for copy in inputs[:2]:
        copy.start()
    attention.fetch((1,))
    weights = []
    for i in range(DM // COLS):
        cols = pl.ds(i * COLS, COLS)
        weights.append(
            (
                pltpu.make_async_copy(wa_hbm.at[:, cols], w_scr.at[pl.ds(0, 2 * HD), cols], w_sem.at[2 * i]),
                pltpu.make_async_copy(ws_hbm.at[:, cols], w_scr.at[pl.ds(2 * HD, HP), cols], w_sem.at[2 * i + 1]),
            )
        )
    inputs[2].start()
    for pair in weights:
        for copy in pair:
            copy.start()
    for copy in inputs[:2]:
        copy.wait()

    attention.add(acc_scr)
    total = acc_scr[:, HD:]
    fine = (jnp.min(total) > 2.0**-60) & (jnp.max(total) < 2.0**110)

    @pl.when(jnp.logical_not(fine))
    def _():
        attention.fetch((0, 1), every=True)
        acc_scr[...] = jnp.zeros_like(acc_scr)
        m_scr[...] = jnp.full(m_scr.shape, LOW, jnp.float32)
        attention.add_shifted(acc_scr, m_scr)

    for g in range(2):
        rows = slice(g * ROWS, (g + 1) * ROWS)
        in_scr[:, g * HD : (g + 1) * HD] = (acc_scr[rows, :HD] / acc_scr[rows, HD:]).astype(jnp.bfloat16)
    inputs[2].wait()

    def out_copy(i):
        cols = pl.ds(i * COLS, COLS)
        return pltpu.make_async_copy(o_scr.at[:, cols], o_hbm.at[:, cols], o_sem.at[i])

    for i in range(DM // COLS):
        cols = slice(i * COLS, (i + 1) * COLS)
        for copy in weights[i]:
            copy.wait()
        o_scr[:, cols] = jnp.dot(in_scr[...], w_scr[:, cols], preferred_element_type=jnp.float32).astype(jnp.bfloat16)
        out_copy(i).start()
    for i in range(DM // COLS):
        out_copy(i).wait()


def big(**more):
    return pltpu.CompilerParams(vmem_limit_bytes=LIMIT, **more)


def moved(block, route0, route1):
    pairs = []
    for x in range(4):
        for y in range(4):
            for core, route in enumerate((route0, route1)):
                to = route(x, y)
                if to is not None:
                    pairs.append((x * 8 + y * 2 + core, to[0] * 8 + to[1] * 2 + core))
    return lax.ppermute(block, "pack", pairs)


def lines():
    columns = [[x * 8 + y * 2 for x in range(4)] for y in range(4)]
    rows = [[x * 8 + y * 2 + 1 for y in range(4)] for x in range(4)]
    return columns + rows


def along_x(distance):
    return lambda x, y: (x + distance, y) if x + distance < 4 else None


def along_y(distance):
    return lambda x, y: (x, (y + distance) % 4)


def swapped(block):
    return lax.ppermute(block, "pack", [(i, i ^ 1) for i in range(32)])


def call(kernel, shapes, ins, *args):
    return pl.pallas_call(
        kernel,
        out_shape=tuple(jax.ShapeDtypeStruct(shape, jnp.bfloat16) for shape in shapes),
        in_specs=[SMEM] + [VMEM] * ins,
        out_specs=(VMEM,) * len(shapes),
        compiler_params=big(),
        cost_estimate=pl.CostEstimate(flops=10**6, bytes_accessed=10**6, transcendentals=0),
    )(*args)


def local(
    queries,
    keys_values,
    ssm_values,
    ssm_gates,
    ssm_maps,
    step_size,
    decay_log,
    skip_gain,
    attn_out_weight,
    ssd_out_weight,
    lengths,
):
    first = jnp.reshape(lax.axis_index("pack") * ROWS, (1,)).astype(jnp.int32)
    kv = keys_values.reshape(ROWS, 2 * HD)
    nowhere = lambda x, y: None
    below = moved(kv, along_y(1), along_x(1))
    above = moved(kv, along_y(3), along_x(3))
    across = moved(kv, along_y(2), along_x(2))
    y_local, run_keep, run_send, fac = pl.pallas_call(
        ssd_kernel,
        out_shape=(
            jax.ShapeDtypeStruct((ROWS, HP), jnp.float32),
            jax.ShapeDtypeStruct((STATE_ROWS, HALF), jnp.bfloat16),
            jax.ShapeDtypeStruct((STATE_ROWS, HALF), jnp.bfloat16),
            jax.ShapeDtypeStruct((ROWS, HEADS), jnp.float32),
        ),
        in_specs=[SMEM] * 4 + [VMEM] * 3,
        out_specs=(VMEM, VMEM, VMEM, VMEM),
        compiler_params=big(),
        cost_estimate=pl.CostEstimate(flops=10**9, bytes_accessed=4 * 10**6, transcendentals=10**6),
        name="ssd_local",
    )(lengths, decay_log, skip_gain, first, ssm_values, ssm_maps, step_size.T)

    below, above, across = lax.optimization_barrier((below, above, across, fac))[:3]
    line = jnp.concatenate([kv, below, above, across], axis=0)
    fetched = lax.all_gather(line, "pack", axis=0, tiled=True, axis_index_groups=lines())
    line_got = swapped(line)

    run = (STATE_ROWS, HALF)
    run_got = swapped(run_send)
    (chip,) = call(chip_kernel, [run], 2, first, run_keep, run_got)
    chips = [moved(chip, along_y(d), along_y(d)) for d in (1, 3, 2)]
    chunks_scratch = [
        pltpu.VMEM((SLOTS * CHUNK, 2 * HD), jnp.bfloat16),
        pltpu.SMEM((SLOTS,), jnp.int32),
        pltpu.SemaphoreType.DMA((SLOTS,)),
    ]
    sums = jax.ShapeDtypeStruct((2 * ROWS, 2 * HD), jnp.float32)
    split = jax.ShapeDtypeStruct((2 * ROWS, 2 * HD), jnp.bfloat16)

    def attend(kernel, name, shapes, vmem, *args):
        out = pl.pallas_call(
            kernel,
            out_shape=shapes,
            in_specs=[SMEM] * 2 + [VMEM] * vmem + [ANY],
            out_specs=(VMEM,) * len(shapes),
            scratch_shapes=chunks_scratch,
            compiler_params=big(),
            cost_estimate=pl.CostEstimate(flops=3 * 10**9, bytes_accessed=5 * 10**6, transcendentals=5 * 10**6),
            name=name,
        )(lengths, first, *args)
        return out

    line = lax.optimization_barrier((line, chip))[0]
    acc, queries_split = attend(own_line_kernel, "own_line", (sums, split), 1, queries, line)
    chips = lax.optimization_barrier((*chips, acc))[:3]
    prefix, total = call(row_kernel, [run, run], 4, first, chip, *chips)
    rows = [moved(total, along_x(d), along_x(d)) for d in (3, 2, 1)]
    line_got = lax.optimization_barrier((line_got, prefix))[0]
    (acc,) = attend(other_line_kernel, "other_line", (sums,), 2, queries_split, acc, line_got)
    rows = lax.optimization_barrier((*rows, acc))[:3]
    keep, send = call(carry_kernel, [(SN, HALF)] * 2, 6, first, *rows, prefix, run_keep, run_got)
    got = swapped(send)
    act = pl.pallas_call(
        gate_kernel,
        out_shape=jax.ShapeDtypeStruct((ROWS, HP), jnp.bfloat16),
        grid=(2,),
        in_specs=[
            SMEM,
            pl.BlockSpec((ROWS // 2, HP), lambda i: (i, 0)),
            pl.BlockSpec((ROWS // 2, HP), lambda i: (i, 0)),
            pl.BlockSpec((ROWS // 2, SN), lambda i: (i, 1)),
            pl.BlockSpec((ROWS // 2, HEADS), lambda i: (i, 0)),
            pl.BlockSpec((SN, HALF), lambda i: (0, 0)),
            pl.BlockSpec((SN, HALF), lambda i: (0, 0)),
        ],
        out_specs=pl.BlockSpec((ROWS // 2, HP), lambda i: (i, 0)),
        compiler_params=big(),
        cost_estimate=pl.CostEstimate(flops=10**8, bytes_accessed=3 * 10**6, transcendentals=3 * 10**5),
        name="gate",
    )(first, y_local, ssm_gates, ssm_maps, fac, keep, got)

    fetched = lax.optimization_barrier((fetched, act))[0]
    other = swapped(fetched)
    (acc,) = attend(part_kernel, "part", (sums,), 2, queries_split, acc, fetched)

    terms = pl.pallas_call(
        mix_kernel,
        out_shape=jax.ShapeDtypeStruct((ROWS, DM), jnp.bfloat16),
        in_specs=[SMEM] * 2 + [ANY] * 7,
        out_specs=ANY,
        scratch_shapes=chunks_scratch
        + [
            pltpu.VMEM((2 * ROWS, 2 * HD), jnp.bfloat16),
            pltpu.VMEM((2 * ROWS, 2 * HD), jnp.float32),
            pltpu.VMEM((2 * ROWS, HD), jnp.float32),
            pltpu.VMEM((2 * HD + HP, DM), jnp.bfloat16),
            pltpu.VMEM((ROWS, 2 * HD + HP), jnp.bfloat16),
            pltpu.VMEM((ROWS, DM), jnp.bfloat16),
            pltpu.SemaphoreType.DMA((3,)),
            pltpu.SemaphoreType.DMA((2 * (DM // COLS),)),
            pltpu.SemaphoreType.DMA((DM // COLS,)),
        ],
        compiler_params=big(),
        cost_estimate=pl.CostEstimate(flops=9 * 10**9, bytes_accessed=25 * 10**6, transcendentals=9 * 10**6),
        name="mix",
    )(lengths, first, queries_split, act, acc, fetched, other, attn_out_weight, ssd_out_weight)
    return lax.psum_scatter(terms, "tp", scatter_dimension=0, tiled=True)


def solution(mesh):
    return jax.shard_map(
        local,
        mesh=mesh,
        in_specs=(
            P("pack", "tp"),
            P("pack", "tp", None),
            P("pack", "tp"),
            P("pack", "tp"),
            P("pack", None),
            P("pack", "tp"),
            P("tp"),
            P("tp"),
            P("tp", None),
            P("tp", None),
            P(),
        ),
        out_specs=P(("pack", "tp"), None),
        check_vma=False,
    )
```

```python
import jax
import jax.numpy as jnp
from jax import lax
from jax.experimental import pallas as pl
from jax.experimental.pallas import tpu as pltpu
from jax.sharding import PartitionSpec as P

ROWS = 512
BLOCK = 256
HD = 128
HEADS = 8
HP = 512
SN = 256
DM = 5120
CHUNK = 512
SLOTS = 18
TILE = 256
COLS = 1280
LOW = -1e30
LOG2E = 1.4426950408889634
HIGH = lax.Precision.HIGHEST
LIMIT = 62 * 2**20
HALF = HP // 2
STATE_ROWS = SN + 16
VMEM = pl.BlockSpec(memory_space=pltpu.VMEM)
SMEM = pl.BlockSpec(memory_space=pltpu.SMEM)
ANY = pl.BlockSpec(memory_space=pl.ANY)


def iota(shape, dim):
    return lax.broadcasted_iota(jnp.int32, shape, dim)


def ends_of(len_ref):
    e0 = len_ref[0]
    e1 = e0 + len_ref[1]
    return e0, e1, e1 + len_ref[2]


def start_of(pos, ends):
    e0, e1, e2 = ends
    zero = jnp.zeros_like(pos)
    out = jnp.where(pos >= e0, zero + e0, zero)
    out = jnp.where(pos >= e1, zero + e1, out)
    return jnp.where(pos >= e2, zero + e2, out)


def spread():
    return (iota((HEADS, HP), 1) // (HP // HEADS) == iota((HEADS, HP), 0)).astype(jnp.float32)


def widen(a, expand):
    return jnp.dot(a, expand, precision=HIGH, preferred_element_type=jnp.float32)


def ssd_kernel(len_ref, dl_ref, skip_ref, first_ref, x_ref, maps_ref, step_ref, y_ref, keep_ref, send_ref, fac_ref):
    first = first_ref[0]
    ends = ends_of(len_ref)
    expand = spread()
    head_sub = iota((HEADS, 1), 0)
    wide_lane = iota((1, HP), 1) // (HP // HEADS)
    rate = jnp.zeros((HEADS, 1), jnp.float32)
    skip = jnp.zeros((1, HP), jnp.float32)
    for h in range(HEADS):
        rate = jnp.where(head_sub == h, dl_ref[h], rate)
        skip = jnp.where(wide_lane == h, skip_ref[h], skip)
    rate = -jnp.exp(rate)
    row = iota((BLOCK, 1), 0)
    col = iota((1, BLOCK), 1)
    tri = (row >= col).astype(jnp.float32)
    half = iota((1, 128), 1) < 64
    state = None
    before = None
    for n in range(ROWS // BLOCK):
        rows = slice(n * BLOCK, (n + 1) * BLOCK)
        base = first + n * BLOCK
        start_col = start_of(base + row, ends)
        last_start = start_of(base + (BLOCK - 1), ends)
        cum_t = lax.dot_general(
            rate * step_ref[:, rows], tri, (((1,), (1,)), ((), ())), precision=HIGH, preferred_element_type=jnp.float32
        )
        cum = cum_t.T
        write = maps_ref[rows, :SN]
        read = maps_ref[rows, SN:]
        prod = lax.dot_general(read, write, (((1,), (1,)), ((), ())), preferred_element_type=jnp.float32)
        allowed = (base + col >= start_col) & (col <= row)
        for pair in range(HEADS // 2):
            lanes = slice(pair * 128, (pair + 1) * 128)
            x = x_ref[rows, lanes]
            total = skip[:, lanes] * x.astype(jnp.float32)
            for which in range(2):
                h = pair * 2 + which
                gap = jnp.where(allowed, cum[:, h : h + 1] - cum_t[h : h + 1, :], LOW)
                weights = (jnp.exp(gap) * prod).astype(jnp.bfloat16)
                part = jnp.where(half if which == 0 else ~half, x, jnp.zeros_like(x))
                total = total + jnp.dot(weights, part, preferred_element_type=jnp.float32)
            y_ref[rows, lanes] = total
        ecum = jnp.exp(cum)
        if state is not None:
            local = widen(jnp.where(start_col < base, ecum, 0.0), expand)
            reads = jnp.dot(read, state.astype(jnp.bfloat16), preferred_element_type=jnp.float32)
            y_ref[rows, :] += reads * local
        carry = jnp.where(start_col < first, ecum, 0.0)
        if before is not None:
            carry = carry * before
        fac_ref[rows, :] = carry
        tail = jnp.exp(cum[BLOCK - 1 : BLOCK, :] - cum)
        tail = widen(jnp.where(base + row >= last_start, tail, 0.0), expand)
        weighted = (x_ref[rows, :].astype(jnp.float32) * tail).astype(jnp.bfloat16)
        new = lax.dot_general(write, weighted, (((0,), (0,)), ((), ())), preferred_element_type=jnp.float32)
        end = ecum[BLOCK - 8 :, :]
        if state is not None:
            keep = jnp.where(last_start < base, 1.0, 0.0)
            new = new + (keep * widen(end, expand)[7:8, :]) * state
            end = end * before
        state = new
        before = end[7:8, :]
    through = jnp.where(last_start < first, 1.0, 0.0) * widen(end, expand)[7:8, :]
    core = (first // ROWS) % 2
    left, right = slice(0, HALF), slice(HALF, HP)
    for ref, wanted in ((keep_ref, 0), (send_ref, 1)):
        store_run(
            ref,
            jnp.where(core == wanted, state[:, left], state[:, right]),
            jnp.where(core == wanted, through[:, left], through[:, right]),
        )


def store_run(ref, state, through):
    high = through.astype(jnp.bfloat16).astype(jnp.float32)
    low = through - high
    sub = iota((16, 1), 0)
    ref[:SN, :] = state.astype(jnp.bfloat16)
    ref[SN:, :] = jnp.where(sub == 0, high, jnp.where(sub == 1, low, 0.0)).astype(jnp.bfloat16)


def load_run(ref):
    tail = ref[SN:, :].astype(jnp.float32)
    return ref[:SN, :].astype(jnp.float32), tail[0:1, :] + tail[1:2, :]


def pick(cond, one, other):
    return jnp.where(cond, one[0], other[0]), jnp.where(cond, one[1], other[1])


def after(earlier, later):
    return later[0] + later[1] * earlier[0], earlier[1] * later[1]


def chip_kernel(first_ref, mine_ref, other_ref, out_ref):
    core = (first_ref[0] // ROWS) % 2
    mine, other = load_run(mine_ref), load_run(other_ref)
    store_run(out_ref, *after(pick(core == 0, mine, other), pick(core == 0, other, mine)))


def row_kernel(first_ref, mine_ref, below_ref, above_ref, across_ref, prefix_ref, total_ref):
    y = (first_ref[0] // (2 * ROWS)) % 4
    by_distance = [load_run(ref) for ref in (mine_ref, below_ref, across_ref, above_ref)]
    run = (jnp.zeros((SN, HALF), jnp.float32), jnp.ones((1, HALF), jnp.float32))
    prefix = run
    for place in range(4):
        distance = (y - place) % 4
        piece = by_distance[0]
        for d in range(1, 4):
            piece = pick(distance == d, by_distance[d], piece)
        prefix = pick(y == place, run, prefix)
        run = after(run, piece)
    store_run(prefix_ref, *prefix)
    store_run(total_ref, *run)


def carry_kernel(first_ref, row3_ref, row2_ref, row1_ref, prefix_ref, mine_ref, other_ref, keep_ref, send_ref):
    core = (first_ref[0] // ROWS) % 2
    run = load_run(row3_ref)
    for ref in (row2_ref, row1_ref, prefix_ref):
        run = after(run, load_run(ref))
    behind = after(run, pick(core == 0, load_run(mine_ref), load_run(other_ref)))
    keep_ref[...] = jnp.where(core == 0, run[0], behind[0]).astype(jnp.bfloat16)
    send_ref[...] = jnp.where(core == 0, behind[0], run[0]).astype(jnp.bfloat16)


def gate_kernel(first_ref, y_ref, z_ref, read_ref, fac_ref, keep_ref, got_ref, act_ref):
    core = (first_ref[0] // ROWS) % 2
    keep, got = keep_ref[...], got_ref[...]
    state = jnp.concatenate([jnp.where(core == 0, keep, got), jnp.where(core == 0, got, keep)], axis=1)
    reads = jnp.dot(read_ref[...], state, preferred_element_type=jnp.float32)
    y = y_ref[...] + reads * widen(fac_ref[...], spread())
    z = z_ref[...].astype(jnp.float32)
    act_ref[...] = (y * (z / (1.0 + jnp.exp(-z)))).astype(jnp.bfloat16)


class Attention:
    def __init__(self, len_ref, first_ref, fetched, other, q_scr, kv_scr, ids, kv_sem, near_only=False):
        self.first = first_ref[0]
        self.ends = ends_of(len_ref)
        self.mine = self.first // CHUNK
        self.low = start_of(self.first, self.ends) // CHUNK
        self.last_start = start_of(self.first + ROWS - 1, self.ends)
        self.arrays = (fetched, other)
        self.near_only = near_only
        self.q_scr, self.kv_scr, self.ids, self.kv_sem = q_scr, kv_scr, ids, kv_sem

    def count(self, far):
        return (self.mine - far - self.low) // 2 + 1

    def block(self, far, i):
        if not self.near_only:
            return self.mine - far - 2 * i
        core = self.mine % 2
        step = jnp.where(core == far, 2, 8)
        return self.mine + jnp.where(core == 0, far, -far) - step * i

    def in_line(self, block):
        row = block // 8 == self.mine // 8
        column = (block // 2) % 4 == (self.mine // 2) % 4
        return jnp.where(block % 2 == 0, row, column)

    def copy(self, far, i, slot):
        if self.near_only:
            source = self.arrays[far][i ^ (i >> 1)]
        else:
            chip = self.block(far, i) // 2
            source = self.arrays[far].at[pl.ds(pl.multiple_of(chip * CHUNK, CHUNK), CHUNK)]
        to = pl.ds(pl.multiple_of(slot * CHUNK, CHUNK), CHUNK)
        return pltpu.make_async_copy(source, self.kv_scr.at[to], self.kv_sem.at[slot])

    def fetch(self, fars, every=False):
        def one_chunk(far, i, carry):
            plain, masked = carry
            block = self.block(far, i)
            if self.near_only:
                wanted = (block >= self.low) & (block <= self.mine) & self.in_line(block)
            elif every:
                wanted = block >= self.low
            else:
                wanted = jnp.logical_not(self.in_line(block))
            mask = (block == self.mine) | (block * CHUNK < self.last_start)
            slot = jnp.where(mask, SLOTS - 1 - masked, plain)

            @pl.when(wanted)
            def _():
                self.ids[slot] = block
                self.copy(far, i, slot).start()

            new = wanted.astype(jnp.int32)
            return plain + jnp.where(mask, 0, new), masked + jnp.where(mask, new, 0)

        carry = (jnp.int32(0), jnp.int32(0))
        for far in fars:
            if self.near_only:
                for i in range(4):
                    carry = one_chunk(far, i, carry)
            else:
                carry = lax.fori_loop(0, self.count(far), lambda i, c, far=far: one_chunk(far, i, c), carry)
        self.plain, self.masked = carry

    def wait(self, slot):
        to = self.kv_scr.at[self.keys(slot, 1)]
        pltpu.make_async_copy(to, to, self.kv_sem.at[slot]).wait()

    def keys(self, slot, chunks):
        return pl.ds(pl.multiple_of(slot * CHUNK, CHUNK), chunks * CHUNK)

    def scores(self, slot, chunks, r, masked):
        rows = slice(r * TILE, (r + 1) * TILE)
        k = self.kv_scr[self.keys(slot, chunks), :HD]
        s = lax.dot_general(
            self.q_scr[rows, :],
            jnp.concatenate([k, k], axis=1),
            (((1,), (1,)), ((), ())),
            preferred_element_type=jnp.float32,
        )
        if masked:
            pos = self.first + rows.start % ROWS + iota((TILE, 1), 0)
            key = self.ids[slot] * CHUNK + iota((1, CHUNK), 1)
            s = jnp.where((key >= start_of(pos, self.ends)) & (key <= pos), s, LOW)
        return s

    def values(self, slot, chunks):
        v = self.kv_scr[self.keys(slot, chunks), HD:]
        return jnp.concatenate([v, jnp.ones((chunks * CHUNK, HD), jnp.bfloat16)], axis=1)

    def step(self, acc, slot, chunks, masked):
        v = self.values(slot, chunks)
        tiles = 2 * ROWS // TILE
        s = self.scores(slot, chunks, 0, masked)
        for r in range(tiles):
            following = self.scores(slot, chunks, r + 1, masked) if r + 1 < tiles else None
            p = jnp.exp2(s).astype(jnp.bfloat16)
            acc[r * TILE : (r + 1) * TILE, :] += jnp.dot(p, v, preferred_element_type=jnp.float32)
            s = following

    def add(self, acc):
        def one_masked(j, _):
            self.wait(SLOTS - 1 - j)
            self.step(acc, SLOTS - 1 - j, 1, True)
            return 0

        def two_plain(j, _):
            self.wait(2 * j)
            self.wait(2 * j + 1)
            self.step(acc, 2 * j, 2, False)
            return 0

        lax.fori_loop(0, self.masked, one_masked, 0)
        lax.fori_loop(0, self.plain // 2, two_plain, 0)

        @pl.when(self.plain % 2 == 1)
        def _():
            self.wait(self.plain - 1)
            self.step(acc, self.plain - 1, 1, False)

    def add_shifted(self, acc, m_scr):
        def one_chunk(j, _):
            slot = jnp.where(j < self.plain, j, SLOTS - 1 - (j - self.plain))
            self.wait(slot)
            v = self.values(slot, 1)
            for r in range(2 * ROWS // TILE):
                rows = slice(r * TILE, (r + 1) * TILE)
                s = self.scores(slot, 1, r, True)
                old = m_scr[rows, :]
                m = jnp.maximum(old, jnp.max(s, axis=1, keepdims=True))
                alpha = jnp.exp2(old - m)
                p = jnp.exp2(s - jnp.concatenate([m] * (CHUNK // 128), axis=1)).astype(jnp.bfloat16)
                out = jnp.dot(p, v, preferred_element_type=jnp.float32)
                acc[rows, :] = acc[rows, :] * jnp.concatenate([alpha, alpha], axis=1) + out
                m_scr[rows, :] = m
            return 0

        lax.fori_loop(0, self.plain + self.masked, one_chunk, 0)


def stack_kernel(kv, below, above, across, _, line, sem):
    copies = [
        pltpu.make_async_copy(piece, line.at[pl.ds(i * CHUNK, CHUNK)], sem.at[i])
        for i, piece in enumerate((kv, below, above, across))
    ]
    for copy in copies:
        copy.start()
    for copy in copies:
        copy.wait()


def own_line_kernel(len_ref, first_ref, q_ref, line, acc_ref, split_ref, kv_scr, ids, kv_sem):
    pieces = [line.at[pl.ds(i * CHUNK, CHUNK)] for i in range(4)]
    attention = Attention(len_ref, first_ref, pieces, None, split_ref, kv_scr, ids, kv_sem, near_only=True)
    attention.fetch((0,))
    for g in range(2):
        rows = slice(g * ROWS, (g + 1) * ROWS)
        scaled = q_ref[:, g * HD : (g + 1) * HD].astype(jnp.float32) * (LOG2E * HD**-0.5)
        high = scaled.astype(jnp.bfloat16)
        split_ref[rows, :HD] = high
        split_ref[rows, HD:] = (scaled - high.astype(jnp.float32)).astype(jnp.bfloat16)
    acc_ref[...] = jnp.zeros_like(acc_ref)
    attention.add(acc_ref)


def other_line_kernel(len_ref, first_ref, split_ref, before_ref, line_got, acc_ref, kv_scr, ids, kv_sem):
    pieces = [line_got.at[pl.ds(i * CHUNK, CHUNK)] for i in range(4)]
    attention = Attention(len_ref, first_ref, None, pieces, split_ref, kv_scr, ids, kv_sem, near_only=True)
    attention.fetch((1,))
    acc_ref[...] = before_ref[...]
    attention.add(acc_ref)


def part_kernel(len_ref, first_ref, split_ref, before_ref, fetched, acc_ref, kv_scr, ids, kv_sem):
    attention = Attention(len_ref, first_ref, fetched, None, split_ref, kv_scr, ids, kv_sem)
    attention.fetch((0,))
    acc_ref[...] = before_ref[...]
    attention.add(acc_ref)


def mix_kernel(
    len_ref,
    first_ref,
    split_hbm,
    act_hbm,
    before_hbm,
    fetched,
    other,
    wa_hbm,
    ws_hbm,
    o_hbm,
    kv_scr,
    ids,
    kv_sem,
    q_scr,
    acc_scr,
    m_scr,
    w_scr,
    in_scr,
    o_scr,
    in_sem,
    w_sem,
    o_sem,
):
    attention = Attention(len_ref, first_ref, fetched, other, q_scr, kv_scr, ids, kv_sem)
    inputs = [
        pltpu.make_async_copy(split_hbm, q_scr, in_sem.at[0]),
        pltpu.make_async_copy(before_hbm, acc_scr, in_sem.at[1]),
        pltpu.make_async_copy(act_hbm, in_scr.at[:, pl.ds(2 * HD, HP)], in_sem.at[2]),
    ]
    for copy in inputs[:2]:
        copy.start()
    attention.fetch((1,))
    weights = []
    for i in range(DM // COLS):
        cols = pl.ds(i * COLS, COLS)
        weights.append(
            (
                pltpu.make_async_copy(wa_hbm.at[:, cols], w_scr.at[pl.ds(0, 2 * HD), cols], w_sem.at[2 * i]),
                pltpu.make_async_copy(ws_hbm.at[:, cols], w_scr.at[pl.ds(2 * HD, HP), cols], w_sem.at[2 * i + 1]),
            )
        )
    inputs[2].start()
    for pair in weights:
        for copy in pair:
            copy.start()
    for copy in inputs[:2]:
        copy.wait()

    attention.add(acc_scr)
    total = acc_scr[:, HD:]
    fine = (jnp.min(total) > 2.0**-60) & (jnp.max(total) < 2.0**110)

    @pl.when(jnp.logical_not(fine))
    def _():
        attention.fetch((0, 1), every=True)
        acc_scr[...] = jnp.zeros_like(acc_scr)
        m_scr[...] = jnp.full(m_scr.shape, LOW, jnp.float32)
        attention.add_shifted(acc_scr, m_scr)

    for g in range(2):
        rows = slice(g * ROWS, (g + 1) * ROWS)
        in_scr[:, g * HD : (g + 1) * HD] = (acc_scr[rows, :HD] / acc_scr[rows, HD:]).astype(jnp.bfloat16)
    inputs[2].wait()

    def out_copy(i):
        cols = pl.ds(i * COLS, COLS)
        return pltpu.make_async_copy(o_scr.at[:, cols], o_hbm.at[:, cols], o_sem.at[i])

    for i in range(DM // COLS):
        cols = slice(i * COLS, (i + 1) * COLS)
        for copy in weights[i]:
            copy.wait()
        o_scr[:, cols] = jnp.dot(in_scr[...], w_scr[:, cols], preferred_element_type=jnp.float32).astype(jnp.bfloat16)
        out_copy(i).start()
    for i in range(DM // COLS):
        out_copy(i).wait()


def big(**more):
    return pltpu.CompilerParams(vmem_limit_bytes=LIMIT, **more)


def moved(block, route0, route1):
    pairs = []
    for x in range(4):
        for y in range(4):
            for core, route in enumerate((route0, route1)):
                to = route(x, y)
                if to is not None:
                    pairs.append((x * 8 + y * 2 + core, to[0] * 8 + to[1] * 2 + core))
    return lax.ppermute(block, "pack", pairs)


def parities():
    return [list(range(core, 32, 2)) for core in range(2)]


def along_x(distance):
    return lambda x, y: (x + distance, y) if x + distance < 4 else None


def along_y(distance):
    return lambda x, y: (x, (y + distance) % 4)


def swapped(block):
    return lax.ppermute(block, "pack", [(i, i ^ 1) for i in range(32)])


def call(kernel, shapes, ins, *args):
    return pl.pallas_call(
        kernel,
        out_shape=tuple(jax.ShapeDtypeStruct(shape, jnp.bfloat16) for shape in shapes),
        in_specs=[SMEM] + [VMEM] * ins,
        out_specs=(VMEM,) * len(shapes),
        compiler_params=big(),
        cost_estimate=pl.CostEstimate(flops=10**6, bytes_accessed=10**6, transcendentals=0),
    )(*args)


def local(
    queries,
    keys_values,
    ssm_values,
    ssm_gates,
    ssm_maps,
    step_size,
    decay_log,
    skip_gain,
    attn_out_weight,
    ssd_out_weight,
    lengths,
):
    first = jnp.reshape(lax.axis_index("pack") * ROWS, (1,)).astype(jnp.int32)
    kv = keys_values.reshape(ROWS, 2 * HD)
    nowhere = lambda x, y: None
    fetched = lax.all_gather(kv, "pack", axis=0, tiled=True, axis_index_groups=parities())

    y_local, run_keep, run_send, fac = pl.pallas_call(
        ssd_kernel,
        out_shape=(
            jax.ShapeDtypeStruct((ROWS, HP), jnp.float32),
            jax.ShapeDtypeStruct((STATE_ROWS, HALF), jnp.bfloat16),
            jax.ShapeDtypeStruct((STATE_ROWS, HALF), jnp.bfloat16),
            jax.ShapeDtypeStruct((ROWS, HEADS), jnp.float32),
        ),
        in_specs=[SMEM] * 4 + [VMEM] * 3,
        out_specs=(VMEM, VMEM, VMEM, VMEM),
        compiler_params=big(),
        cost_estimate=pl.CostEstimate(flops=10**9, bytes_accessed=4 * 10**6, transcendentals=10**6),
        name="ssd_local",
    )(lengths, decay_log, skip_gain, first, ssm_values, ssm_maps, step_size.T)

    kv = lax.optimization_barrier((kv, fac))[0]
    below = moved(kv, along_y(1), along_x(1))
    above = moved(kv, along_y(3), along_x(3))
    across = moved(kv, along_y(2), along_x(2))

    run = (STATE_ROWS, HALF)
    run_got = swapped(run_send)
    (chip,) = call(chip_kernel, [run], 2, first, run_keep, run_got)
    chips = [moved(chip, along_y(d), along_y(d)) for d in (1, 3, 2)]
    chunks_scratch = [
        pltpu.VMEM((SLOTS * CHUNK, 2 * HD), jnp.bfloat16),
        pltpu.SMEM((SLOTS,), jnp.int32),
        pltpu.SemaphoreType.DMA((SLOTS,)),
    ]
    sums = jax.ShapeDtypeStruct((2 * ROWS, 2 * HD), jnp.float32)
    split = jax.ShapeDtypeStruct((2 * ROWS, 2 * HD), jnp.bfloat16)

    def attend(kernel, name, shapes, vmem, *args):
        out = pl.pallas_call(
            kernel,
            out_shape=shapes,
            in_specs=[SMEM] * 2 + [VMEM] * vmem + [ANY],
            out_specs=(VMEM,) * len(shapes),
            scratch_shapes=chunks_scratch,
            compiler_params=big(),
            cost_estimate=pl.CostEstimate(flops=3 * 10**9, bytes_accessed=5 * 10**6, transcendentals=5 * 10**6),
            name=name,
        )(lengths, first, *args)
        return out

    line = pl.pallas_call(
        stack_kernel,
        out_shape=jax.ShapeDtypeStruct((4 * CHUNK, 2 * HD), jnp.bfloat16),
        in_specs=[ANY] * 5,
        out_specs=ANY,
        scratch_shapes=[pltpu.SemaphoreType.DMA((4,))],
        compiler_params=big(),
        name="stack",
    )(kv, below, above, across, chip)
    line_got = swapped(line)
    acc, queries_split = attend(own_line_kernel, "own_line", (sums, split), 1, queries, line)
    chips = lax.optimization_barrier((*chips, acc))[:3]
    prefix, total = call(row_kernel, [run, run], 4, first, chip, *chips)
    rows = [moved(total, along_x(d), along_x(d)) for d in (3, 2, 1)]
    line_got = lax.optimization_barrier((line_got, prefix))[0]
    (acc,) = attend(other_line_kernel, "other_line", (sums,), 2, queries_split, acc, line_got)
    rows = lax.optimization_barrier((*rows, acc))[:3]
    keep, send = call(carry_kernel, [(SN, HALF)] * 2, 6, first, *rows, prefix, run_keep, run_got)
    got = swapped(send)
    act = pl.pallas_call(
        gate_kernel,
        out_shape=jax.ShapeDtypeStruct((ROWS, HP), jnp.bfloat16),
        grid=(2,),
        in_specs=[
            SMEM,
            pl.BlockSpec((ROWS // 2, HP), lambda i: (i, 0)),
            pl.BlockSpec((ROWS // 2, HP), lambda i: (i, 0)),
            pl.BlockSpec((ROWS // 2, SN), lambda i: (i, 1)),
            pl.BlockSpec((ROWS // 2, HEADS), lambda i: (i, 0)),
            pl.BlockSpec((SN, HALF), lambda i: (0, 0)),
            pl.BlockSpec((SN, HALF), lambda i: (0, 0)),
        ],
        out_specs=pl.BlockSpec((ROWS // 2, HP), lambda i: (i, 0)),
        compiler_params=big(),
        cost_estimate=pl.CostEstimate(flops=10**8, bytes_accessed=3 * 10**6, transcendentals=3 * 10**5),
        name="gate",
    )(first, y_local, ssm_gates, ssm_maps, fac, keep, got)

    fetched = lax.optimization_barrier((fetched, act))[0]
    other = swapped(fetched)
    (acc,) = attend(part_kernel, "part", (sums,), 2, queries_split, acc, fetched)

    terms = pl.pallas_call(
        mix_kernel,
        out_shape=jax.ShapeDtypeStruct((ROWS, DM), jnp.bfloat16),
        in_specs=[SMEM] * 2 + [ANY] * 7,
        out_specs=ANY,
        scratch_shapes=chunks_scratch
        + [
            pltpu.VMEM((2 * ROWS, 2 * HD), jnp.bfloat16),
            pltpu.VMEM((2 * ROWS, 2 * HD), jnp.float32),
            pltpu.VMEM((2 * ROWS, HD), jnp.float32),
            pltpu.VMEM((2 * HD + HP, DM), jnp.bfloat16),
            pltpu.VMEM((ROWS, 2 * HD + HP), jnp.bfloat16),
            pltpu.VMEM((ROWS, DM), jnp.bfloat16),
            pltpu.SemaphoreType.DMA((3,)),
            pltpu.SemaphoreType.DMA((2 * (DM // COLS),)),
            pltpu.SemaphoreType.DMA((DM // COLS,)),
        ],
        compiler_params=big(),
        cost_estimate=pl.CostEstimate(flops=9 * 10**9, bytes_accessed=25 * 10**6, transcendentals=9 * 10**6),
        name="mix",
    )(lengths, first, queries_split, act, acc, fetched, other, attn_out_weight, ssd_out_weight)
    return lax.psum_scatter(terms, "tp", scatter_dimension=0, tiled=True)


def solution(mesh):
    return jax.shard_map(
        local,
        mesh=mesh,
        in_specs=(
            P("pack", "tp"),
            P("pack", "tp", None),
            P("pack", "tp"),
            P("pack", "tp"),
            P("pack", None),
            P("pack", "tp"),
            P("tp"),
            P("tp"),
            P("tp", None),
            P("tp", None),
            P(),
        ),
        out_specs=P(("pack", "tp"), None),
        check_vma=False,
    )
```

```python
import jax
import jax.numpy as jnp
from jax import lax
from jax.experimental import pallas as pl
from jax.experimental.pallas import tpu as pltpu
from jax.sharding import PartitionSpec as P

ROWS = 512
BLOCK = 256
HD = 128
HEADS = 8
HP = 512
SN = 256
DM = 5120
CHUNK = 512
SLOTS = 18
TILE = 256
COLS = 1280
LOW = -1e30
LOG2E = 1.4426950408889634
HIGH = lax.Precision.HIGHEST
LIMIT = 64 * 2**20 - 2**16
HALF = HP // 2
STATE_ROWS = SN + 16
VMEM = pl.BlockSpec(memory_space=pltpu.VMEM)
SMEM = pl.BlockSpec(memory_space=pltpu.SMEM)
ANY = pl.BlockSpec(memory_space=pl.ANY)


def iota(shape, dim):
    return lax.broadcasted_iota(jnp.int32, shape, dim)


def ends_of(len_ref):
    e0 = len_ref[0]
    e1 = e0 + len_ref[1]
    return e0, e1, e1 + len_ref[2]


def start_of(pos, ends):
    e0, e1, e2 = ends
    zero = jnp.zeros_like(pos)
    out = jnp.where(pos >= e0, zero + e0, zero)
    out = jnp.where(pos >= e1, zero + e1, out)
    return jnp.where(pos >= e2, zero + e2, out)


def spread():
    return (iota((HEADS, HP), 1) // (HP // HEADS) == iota((HEADS, HP), 0)).astype(jnp.float32)


def widen(a, expand):
    return jnp.dot(a, expand, precision=HIGH, preferred_element_type=jnp.float32)


def ssd_kernel(len_ref, dl_ref, skip_ref, first_ref, x_ref, maps_ref, step_ref, y_ref, keep_ref, send_ref, fac_ref):
    first = first_ref[0]
    ends = ends_of(len_ref)
    expand = spread()
    head_sub = iota((HEADS, 1), 0)
    wide_lane = iota((1, HP), 1) // (HP // HEADS)
    rate = jnp.zeros((HEADS, 1), jnp.float32)
    skip = jnp.zeros((1, HP), jnp.float32)
    for h in range(HEADS):
        rate = jnp.where(head_sub == h, dl_ref[h], rate)
        skip = jnp.where(wide_lane == h, skip_ref[h], skip)
    rate = -jnp.exp(rate)
    row = iota((BLOCK, 1), 0)
    col = iota((1, BLOCK), 1)
    tri = (row >= col).astype(jnp.float32)
    half = iota((1, 128), 1) < 64
    state = None
    before = None
    for n in range(ROWS // BLOCK):
        rows = slice(n * BLOCK, (n + 1) * BLOCK)
        base = first + n * BLOCK
        start_col = start_of(base + row, ends)
        last_start = start_of(base + (BLOCK - 1), ends)
        cum_t = lax.dot_general(
            rate * step_ref[:, rows], tri, (((1,), (1,)), ((), ())), precision=HIGH, preferred_element_type=jnp.float32
        )
        cum = cum_t.T
        write = maps_ref[rows, :SN]
        read = maps_ref[rows, SN:]
        prod = lax.dot_general(read, write, (((1,), (1,)), ((), ())), preferred_element_type=jnp.float32)
        allowed = (base + col >= start_col) & (col <= row)
        for pair in range(HEADS // 2):
            lanes = slice(pair * 128, (pair + 1) * 128)
            x = x_ref[rows, lanes]
            total = skip[:, lanes] * x.astype(jnp.float32)
            for which in range(2):
                h = pair * 2 + which
                gap = jnp.where(allowed, cum[:, h : h + 1] - cum_t[h : h + 1, :], LOW)
                weights = (jnp.exp(gap) * prod).astype(jnp.bfloat16)
                part = jnp.where(half if which == 0 else ~half, x, jnp.zeros_like(x))
                total = total + jnp.dot(weights, part, preferred_element_type=jnp.float32)
            y_ref[rows, lanes] = total
        ecum = jnp.exp(cum)
        if state is not None:
            local = widen(jnp.where(start_col < base, ecum, 0.0), expand)
            reads = jnp.dot(read, state.astype(jnp.bfloat16), preferred_element_type=jnp.float32)
            y_ref[rows, :] += reads * local
        carry = jnp.where(start_col < first, ecum, 0.0)
        if before is not None:
            carry = carry * before
        fac_ref[rows, :] = carry
        tail = jnp.exp(cum[BLOCK - 1 : BLOCK, :] - cum)
        tail = widen(jnp.where(base + row >= last_start, tail, 0.0), expand)
        weighted = (x_ref[rows, :].astype(jnp.float32) * tail).astype(jnp.bfloat16)
        new = lax.dot_general(write, weighted, (((0,), (0,)), ((), ())), preferred_element_type=jnp.float32)
        end = ecum[BLOCK - 8 :, :]
        if state is not None:
            keep = jnp.where(last_start < base, 1.0, 0.0)
            new = new + (keep * widen(end, expand)[7:8, :]) * state
            end = end * before
        state = new
        before = end[7:8, :]
    through = jnp.where(last_start < first, 1.0, 0.0) * widen(end, expand)[7:8, :]
    core = (first // ROWS) % 2
    left, right = slice(0, HALF), slice(HALF, HP)
    for ref, wanted in ((keep_ref, 0), (send_ref, 1)):
        store_run(
            ref,
            jnp.where(core == wanted, state[:, left], state[:, right]),
            jnp.where(core == wanted, through[:, left], through[:, right]),
        )


def store_run(ref, state, through):
    high = through.astype(jnp.bfloat16).astype(jnp.float32)
    low = through - high
    sub = iota((16, 1), 0)
    ref[:SN, :] = state.astype(jnp.bfloat16)
    ref[SN:, :] = jnp.where(sub == 0, high, jnp.where(sub == 1, low, 0.0)).astype(jnp.bfloat16)


def load_run(ref):
    tail = ref[SN:, :].astype(jnp.float32)
    return ref[:SN, :].astype(jnp.float32), tail[0:1, :] + tail[1:2, :]


def pick(cond, one, other):
    return jnp.where(cond, one[0], other[0]), jnp.where(cond, one[1], other[1])


def after(earlier, later):
    return later[0] + later[1] * earlier[0], earlier[1] * later[1]


def chip_kernel(first_ref, mine_ref, other_ref, out_ref):
    core = (first_ref[0] // ROWS) % 2
    mine, other = load_run(mine_ref), load_run(other_ref)
    store_run(out_ref, *after(pick(core == 0, mine, other), pick(core == 0, other, mine)))


def row_kernel(first_ref, mine_ref, below_ref, above_ref, across_ref, prefix_ref, total_ref):
    y = (first_ref[0] // (2 * ROWS)) % 4
    by_distance = [load_run(ref) for ref in (mine_ref, below_ref, across_ref, above_ref)]
    run = (jnp.zeros((SN, HALF), jnp.float32), jnp.ones((1, HALF), jnp.float32))
    prefix = run
    for place in range(4):
        distance = (y - place) % 4
        piece = by_distance[0]
        for d in range(1, 4):
            piece = pick(distance == d, by_distance[d], piece)
        prefix = pick(y == place, run, prefix)
        run = after(run, piece)
    store_run(prefix_ref, *prefix)
    store_run(total_ref, *run)


def carry_kernel(first_ref, row3_ref, row2_ref, row1_ref, prefix_ref, mine_ref, other_ref, keep_ref, send_ref):
    core = (first_ref[0] // ROWS) % 2
    run = load_run(row3_ref)
    for ref in (row2_ref, row1_ref, prefix_ref):
        run = after(run, load_run(ref))
    behind = after(run, pick(core == 0, load_run(mine_ref), load_run(other_ref)))
    keep_ref[...] = jnp.where(core == 0, run[0], behind[0]).astype(jnp.bfloat16)
    send_ref[...] = jnp.where(core == 0, behind[0], run[0]).astype(jnp.bfloat16)


def gate_kernel(first_ref, y_ref, z_ref, read_ref, fac_ref, keep_ref, got_ref, act_ref):
    core = (first_ref[0] // ROWS) % 2
    keep, got = keep_ref[...], got_ref[...]
    state = jnp.concatenate([jnp.where(core == 0, keep, got), jnp.where(core == 0, got, keep)], axis=1)
    reads = jnp.dot(read_ref[...], state, preferred_element_type=jnp.float32)
    y = y_ref[...] + reads * widen(fac_ref[...], spread())
    z = z_ref[...].astype(jnp.float32)
    act_ref[...] = (y * (z / (1.0 + jnp.exp(-z)))).astype(jnp.bfloat16)


class Attention:
    def __init__(self, len_ref, first_ref, fetched, other, q_scr, kv_scr, ids, kinds, kv_sem, near_only=False):
        self.first = first_ref[0]
        self.ends = ends_of(len_ref)
        self.mine = self.first // CHUNK
        self.low = start_of(self.first, self.ends) // CHUNK
        self.last_start = start_of(self.first + ROWS - 1, self.ends)
        self.arrays = (fetched, other)
        self.near_only = near_only
        self.q_scr, self.kv_scr, self.ids, self.kinds, self.kv_sem = q_scr, kv_scr, ids, kinds, kv_sem

    def count(self, far):
        return 4 if self.near_only else (self.mine - far - self.low) // 2 + 1

    def block(self, far, i):
        if not self.near_only:
            return self.mine - far - 2 * i
        core = self.mine % 2
        step = jnp.where(core == far, 2, 8)
        return self.mine + jnp.where(core == 0, far, -far) - step * i

    def in_line(self, block):
        row = block // 8 == self.mine // 8
        column = (block // 2) % 4 == (self.mine // 2) % 4
        return jnp.where(block % 2 == 0, row, column)

    def place(self, block):
        x, y, even = block // 8, (block // 2) % 4, block % 2 == 0
        my_x, my_y = self.mine // 8, (self.mine // 2) % 4
        distance = jnp.where(even, (my_y - y) % 4, (my_x - x) % 4)
        place = distance ^ (distance >> 1)
        if not self.near_only:
            place = place + 4 * jnp.where(even, x, y)
        return place

    def copy(self, far, place, slot):
        rows = pl.ds(pl.multiple_of(place * CHUNK, CHUNK), CHUNK)
        to = pl.ds(pl.multiple_of(slot * CHUNK, CHUNK), CHUNK)
        return pltpu.make_async_copy(self.arrays[far].at[rows], self.kv_scr.at[to], self.kv_sem.at[slot])

    def fetch(self, fars, every=False):
        def one_chunk(far, i, carry):
            plain, masked = carry
            block = self.block(far, i)
            if self.near_only:
                wanted = (block >= self.low) & (block <= self.mine) & self.in_line(block)
            elif every:
                wanted = block >= self.low
            else:
                wanted = jnp.logical_not(self.in_line(block))
            mask = (block == self.mine) | (block * CHUNK < self.last_start)
            slot = jnp.where(mask, SLOTS - 1 - masked, plain)

            @pl.when(wanted)
            def _():
                self.ids[slot] = block
                inside = start_of(block * CHUNK + (CHUNK - 1), self.ends) > block * CHUNK
                self.kinds[slot] = jnp.where((block == self.mine) | inside, 1, 0)
                self.copy(far, self.place(block), slot).start()

            new = wanted.astype(jnp.int32)
            return plain + jnp.where(mask, 0, new), masked + jnp.where(mask, new, 0)

        carry = (jnp.int32(0), jnp.int32(0))
        for far in fars:
            carry = lax.fori_loop(0, self.count(far), lambda i, c, far=far: one_chunk(far, i, c), carry)
        self.plain, self.masked = carry

    def wait(self, slot):
        self.copy(0, 0, slot).wait()

    def keys(self, slot, chunks):
        return pl.ds(pl.multiple_of(slot * CHUNK, CHUNK), chunks * CHUNK)

    def scores(self, slot, chunks, r, masked):
        rows = slice(r * TILE, (r + 1) * TILE)
        k = self.kv_scr[self.keys(slot, chunks), :HD]
        s = lax.dot_general(
            self.q_scr[rows, :],
            jnp.concatenate([k, k], axis=1),
            (((1,), (1,)), ((), ())),
            preferred_element_type=jnp.float32,
        )
        if masked:
            pos = self.first + rows.start % ROWS + iota((TILE, 1), 0)
            key = self.ids[slot] * CHUNK + iota((1, CHUNK), 1)
            s = jnp.where((key >= start_of(pos, self.ends)) & (key <= pos), s, LOW)
        return s

    def values(self, slot, chunks):
        v = self.kv_scr[self.keys(slot, chunks), HD:]
        return jnp.concatenate([v, jnp.ones((chunks * CHUNK, HD), jnp.bfloat16)], axis=1)

    def step(self, acc, slot, chunks, masked, by_row=False):
        v = self.values(slot, chunks)
        tiles = 2 * ROWS // TILE
        s = self.scores(slot, chunks, 0, masked)
        for r in range(tiles):
            following = self.scores(slot, chunks, r + 1, masked) if r + 1 < tiles else None
            p = jnp.exp2(s).astype(jnp.bfloat16)
            out = jnp.dot(p, v, preferred_element_type=jnp.float32)
            if by_row:
                pos = self.first + (r * TILE) % ROWS + iota((TILE, 1), 0)
                out = jnp.where(start_of(pos, self.ends) <= self.ids[slot] * CHUNK, out, 0.0)
            acc[r * TILE : (r + 1) * TILE, :] += out
            s = following

    def add(self, acc):
        def one_masked(j, _):
            slot = SLOTS - 1 - j
            self.wait(slot)
            pl.when(self.kinds[slot] == 0)(lambda: self.step(acc, slot, 1, False, by_row=True))
            pl.when(self.kinds[slot] == 1)(lambda: self.step(acc, slot, 1, True))
            return 0

        def two_plain(j, _):
            self.wait(2 * j)
            self.wait(2 * j + 1)
            self.step(acc, 2 * j, 2, False)
            return 0

        lax.fori_loop(0, self.masked, one_masked, 0)
        lax.fori_loop(0, self.plain // 2, two_plain, 0)

        @pl.when(self.plain % 2 == 1)
        def _():
            self.wait(self.plain - 1)
            self.step(acc, self.plain - 1, 1, False)

    def add_shifted(self, acc, m_scr):
        def one_chunk(j, _):
            slot = jnp.where(j < self.plain, j, SLOTS - 1 - (j - self.plain))
            self.wait(slot)
            v = self.values(slot, 1)
            for r in range(2 * ROWS // TILE):
                rows = slice(r * TILE, (r + 1) * TILE)
                s = self.scores(slot, 1, r, True)
                old = m_scr[rows, :]
                m = jnp.maximum(old, jnp.max(s, axis=1, keepdims=True))
                alpha = jnp.exp2(old - m)
                p = jnp.exp2(s - jnp.concatenate([m] * (CHUNK // 128), axis=1)).astype(jnp.bfloat16)
                out = jnp.dot(p, v, preferred_element_type=jnp.float32)
                acc[rows, :] = acc[rows, :] * jnp.concatenate([alpha, alpha], axis=1) + out
                m_scr[rows, :] = m
            return 0

        lax.fori_loop(0, self.plain + self.masked, one_chunk, 0)


def own_line_kernel(len_ref, first_ref, q_ref, line, acc_ref, split_ref, kv_scr, ids, kinds, kv_sem):
    attention = Attention(len_ref, first_ref, line, None, split_ref, kv_scr, ids, kinds, kv_sem, near_only=True)
    attention.fetch((0,))
    for g in range(2):
        rows = slice(g * ROWS, (g + 1) * ROWS)
        scaled = q_ref[:, g * HD : (g + 1) * HD].astype(jnp.float32) * (LOG2E * HD**-0.5)
        high = scaled.astype(jnp.bfloat16)
        split_ref[rows, :HD] = high
        split_ref[rows, HD:] = (scaled - high.astype(jnp.float32)).astype(jnp.bfloat16)
    acc_ref[...] = jnp.zeros_like(acc_ref)
    attention.add(acc_ref)


def other_line_kernel(len_ref, first_ref, split_ref, before_ref, line_got, acc_ref, kv_scr, ids, kinds, kv_sem):
    attention = Attention(len_ref, first_ref, line_got, line_got, split_ref, kv_scr, ids, kinds, kv_sem, near_only=True)
    attention.fetch((1,))
    acc_ref[...] = before_ref[...]
    attention.add(acc_ref)


def part_kernel(len_ref, first_ref, split_ref, before_ref, fetched, acc_ref, kv_scr, ids, kinds, kv_sem):
    attention = Attention(len_ref, first_ref, fetched, None, split_ref, kv_scr, ids, kinds, kv_sem)
    attention.fetch((0,))
    acc_ref[...] = before_ref[...]
    attention.add(acc_ref)


def mix_kernel(
    len_ref,
    first_ref,
    split_hbm,
    act_hbm,
    before_hbm,
    fetched,
    other,
    wa_hbm,
    ws_hbm,
    o_hbm,
    kv_scr,
    ids,
    kinds,
    kv_sem,
    q_scr,
    acc_scr,
    m_scr,
    w_scr,
    in_scr,
    o_scr,
    in_sem,
    w_sem,
    o_sem,
):
    attention = Attention(len_ref, first_ref, fetched, other, q_scr, kv_scr, ids, kinds, kv_sem)
    inputs = [
        pltpu.make_async_copy(split_hbm, q_scr, in_sem.at[0]),
        pltpu.make_async_copy(before_hbm, acc_scr, in_sem.at[1]),
        pltpu.make_async_copy(act_hbm, in_scr.at[:, pl.ds(2 * HD, HP)], in_sem.at[2]),
    ]
    for copy in inputs[:2]:
        copy.start()
    attention.fetch((1,))
    weights = []
    for i in range(DM // COLS):
        cols = pl.ds(i * COLS, COLS)
        weights.append(
            (
                pltpu.make_async_copy(wa_hbm.at[:, cols], w_scr.at[pl.ds(0, 2 * HD), cols], w_sem.at[2 * i]),
                pltpu.make_async_copy(ws_hbm.at[:, cols], w_scr.at[pl.ds(2 * HD, HP), cols], w_sem.at[2 * i + 1]),
            )
        )
    inputs[2].start()
    for pair in weights:
        for copy in pair:
            copy.start()
    for copy in inputs[:2]:
        copy.wait()

    attention.add(acc_scr)
    total = acc_scr[:, HD:]
    fine = (jnp.min(total) > 2.0**-60) & (jnp.max(total) < 2.0**110)

    @pl.when(jnp.logical_not(fine))
    def _():
        attention.fetch((0, 1), every=True)
        acc_scr[...] = jnp.zeros_like(acc_scr)
        m_scr[...] = jnp.full(m_scr.shape, LOW, jnp.float32)
        attention.add_shifted(acc_scr, m_scr)

    for g in range(2):
        rows = slice(g * ROWS, (g + 1) * ROWS)
        in_scr[:, g * HD : (g + 1) * HD] = (acc_scr[rows, :HD] / acc_scr[rows, HD:]).astype(jnp.bfloat16)
    inputs[2].wait()

    def out_copy(i):
        cols = pl.ds(i * COLS, COLS)
        return pltpu.make_async_copy(o_scr.at[:, cols], o_hbm.at[:, cols], o_sem.at[i])

    for i in range(DM // COLS):
        cols = slice(i * COLS, (i + 1) * COLS)
        for copy in weights[i]:
            copy.wait()
        o_scr[:, cols] = jnp.dot(in_scr[...], w_scr[:, cols], preferred_element_type=jnp.float32).astype(jnp.bfloat16)
        out_copy(i).start()
    for i in range(DM // COLS):
        out_copy(i).wait()


def big(**more):
    return pltpu.CompilerParams(vmem_limit_bytes=LIMIT, **more)


def moved(block, route0, route1):
    pairs = []
    for x in range(4):
        for y in range(4):
            for core, route in enumerate((route0, route1)):
                to = route(x, y)
                if to is not None:
                    pairs.append((x * 8 + y * 2 + core, to[0] * 8 + to[1] * 2 + core))
    return lax.ppermute(block, "pack", pairs)


def lines():
    columns = [[x * 8 + y * 2 for x in range(4)] for y in range(4)]
    rows = [[x * 8 + y * 2 + 1 for y in range(4)] for x in range(4)]
    return columns + rows


def along_x(distance):
    return lambda x, y: (x + distance, y) if x + distance < 4 else None


def along_y(distance):
    return lambda x, y: (x, (y + distance) % 4)


def swapped(block):
    return lax.ppermute(block, "pack", [(i, i ^ 1) for i in range(32)])


def call(kernel, shapes, ins, *args):
    return pl.pallas_call(
        kernel,
        out_shape=tuple(jax.ShapeDtypeStruct(shape, jnp.bfloat16) for shape in shapes),
        in_specs=[SMEM] + [VMEM] * ins,
        out_specs=(VMEM,) * len(shapes),
        compiler_params=big(),
        cost_estimate=pl.CostEstimate(flops=10**6, bytes_accessed=10**6, transcendentals=0),
    )(*args)


def local(
    queries,
    keys_values,
    ssm_values,
    ssm_gates,
    ssm_maps,
    step_size,
    decay_log,
    skip_gain,
    attn_out_weight,
    ssd_out_weight,
    lengths,
):
    first = jnp.reshape(lax.axis_index("pack") * ROWS, (1,)).astype(jnp.int32)
    kv = keys_values.reshape(ROWS, 2 * HD)
    nowhere = lambda x, y: None
    below = moved(kv, along_y(1), along_x(1))
    above = moved(kv, along_y(3), along_x(3))
    across = moved(kv, along_y(2), along_x(2))
    y_local, run_keep, run_send, fac = pl.pallas_call(
        ssd_kernel,
        out_shape=(
            jax.ShapeDtypeStruct((ROWS, HP), jnp.float32),
            jax.ShapeDtypeStruct((STATE_ROWS, HALF), jnp.bfloat16),
            jax.ShapeDtypeStruct((STATE_ROWS, HALF), jnp.bfloat16),
            jax.ShapeDtypeStruct((ROWS, HEADS), jnp.float32),
        ),
        in_specs=[SMEM] * 4 + [VMEM] * 3,
        out_specs=(VMEM, VMEM, VMEM, VMEM),
        compiler_params=big(),
        cost_estimate=pl.CostEstimate(flops=10**9, bytes_accessed=4 * 10**6, transcendentals=10**6),
        name="ssd_local",
    )(lengths, decay_log, skip_gain, first, ssm_values, ssm_maps, step_size.T)

    below, above, across = lax.optimization_barrier((below, above, across, fac))[:3]
    line = jnp.concatenate([kv, below, above, across], axis=0)
    fetched = lax.all_gather(line, "pack", axis=0, tiled=True, axis_index_groups=lines())
    line_got = swapped(line)

    run = (STATE_ROWS, HALF)
    run_got = swapped(run_send)
    (chip,) = call(chip_kernel, [run], 2, first, run_keep, run_got)
    chips = [moved(chip, along_y(d), along_y(d)) for d in (1, 3, 2)]
    chunks_scratch = [
        pltpu.VMEM((SLOTS * CHUNK, 2 * HD), jnp.bfloat16),
        pltpu.SMEM((SLOTS,), jnp.int32),
        pltpu.SMEM((SLOTS,), jnp.int32),
        pltpu.SemaphoreType.DMA((SLOTS,)),
    ]
    sums = jax.ShapeDtypeStruct((2 * ROWS, 2 * HD), jnp.float32)
    split = jax.ShapeDtypeStruct((2 * ROWS, 2 * HD), jnp.bfloat16)

    def attend(kernel, name, shapes, vmem, *args):
        out = pl.pallas_call(
            kernel,
            out_shape=shapes,
            in_specs=[SMEM] * 2 + [VMEM] * vmem + [ANY],
            out_specs=(VMEM,) * len(shapes),
            scratch_shapes=chunks_scratch,
            compiler_params=big(),
            cost_estimate=pl.CostEstimate(flops=3 * 10**9, bytes_accessed=5 * 10**6, transcendentals=5 * 10**6),
            name=name,
        )(lengths, first, *args)
        return out

    line = lax.optimization_barrier((line, chip))[0]
    acc, queries_split = attend(own_line_kernel, "own_line", (sums, split), 1, queries, line)
    chips = lax.optimization_barrier((*chips, acc))[:3]
    prefix, total = call(row_kernel, [run, run], 4, first, chip, *chips)
    rows = [moved(total, along_x(d), along_x(d)) for d in (3, 2, 1)]
    line_got = lax.optimization_barrier((line_got, prefix))[0]
    (acc,) = attend(other_line_kernel, "other_line", (sums,), 2, queries_split, acc, line_got)
    rows = lax.optimization_barrier((*rows, acc))[:3]
    keep, send = call(carry_kernel, [(SN, HALF)] * 2, 6, first, *rows, prefix, run_keep, run_got)
    got = swapped(send)
    act = pl.pallas_call(
        gate_kernel,
        out_shape=jax.ShapeDtypeStruct((ROWS, HP), jnp.bfloat16),
        grid=(2,),
        in_specs=[
            SMEM,
            pl.BlockSpec((ROWS // 2, HP), lambda i: (i, 0)),
            pl.BlockSpec((ROWS // 2, HP), lambda i: (i, 0)),
            pl.BlockSpec((ROWS // 2, SN), lambda i: (i, 1)),
            pl.BlockSpec((ROWS // 2, HEADS), lambda i: (i, 0)),
            pl.BlockSpec((SN, HALF), lambda i: (0, 0)),
            pl.BlockSpec((SN, HALF), lambda i: (0, 0)),
        ],
        out_specs=pl.BlockSpec((ROWS // 2, HP), lambda i: (i, 0)),
        compiler_params=big(),
        cost_estimate=pl.CostEstimate(flops=10**8, bytes_accessed=3 * 10**6, transcendentals=3 * 10**5),
        name="gate",
    )(first, y_local, ssm_gates, ssm_maps, fac, keep, got)

    fetched = lax.optimization_barrier((fetched, act))[0]
    other = swapped(fetched)
    (acc,) = attend(part_kernel, "part", (sums,), 2, queries_split, acc, fetched)

    terms = pl.pallas_call(
        mix_kernel,
        out_shape=jax.ShapeDtypeStruct((ROWS, DM), jnp.bfloat16),
        in_specs=[SMEM] * 2 + [ANY] * 7,
        out_specs=ANY,
        scratch_shapes=chunks_scratch
        + [
            pltpu.VMEM((2 * ROWS, 2 * HD), jnp.bfloat16),
            pltpu.VMEM((2 * ROWS, 2 * HD), jnp.float32),
            pltpu.VMEM((2 * ROWS, HD), jnp.float32),
            pltpu.VMEM((2 * HD + HP, DM), jnp.bfloat16),
            pltpu.VMEM((ROWS, 2 * HD + HP), jnp.bfloat16),
            pltpu.VMEM((ROWS, DM), jnp.bfloat16),
            pltpu.SemaphoreType.DMA((3,)),
            pltpu.SemaphoreType.DMA((2 * (DM // COLS),)),
            pltpu.SemaphoreType.DMA((DM // COLS,)),
        ],
        compiler_params=big(),
        cost_estimate=pl.CostEstimate(flops=9 * 10**9, bytes_accessed=25 * 10**6, transcendentals=9 * 10**6),
        name="mix",
    )(lengths, first, queries_split, act, acc, fetched, other, attn_out_weight, ssd_out_weight)
    return lax.psum_scatter(terms, "tp", scatter_dimension=0, tiled=True)


def solution(mesh):
    return jax.shard_map(
        local,
        mesh=mesh,
        in_specs=(
            P("pack", "tp"),
            P("pack", "tp", None),
            P("pack", "tp"),
            P("pack", "tp"),
            P("pack", None),
            P("pack", "tp"),
            P("tp"),
            P("tp"),
            P("tp", None),
            P("tp", None),
            P(),
        ),
        out_specs=P(("pack", "tp"), None),
        check_vma=False,
    )
```

```python
import jax
import jax.numpy as jnp
from jax import lax
from jax.experimental import pallas as pl
from jax.experimental.pallas import tpu as pltpu
from jax.sharding import PartitionSpec as P

ROWS = 512
BLOCK = 256
HD = 128
HEADS = 8
HP = 512
SN = 256
DM = 5120
CHUNK = 512
SLOTS = 18
TILE = 256
COLS = 1280
LOW = -1e30
LOG2E = 1.4426950408889634
HIGH = lax.Precision.HIGHEST
LIMIT = 64 * 2**20 - 2**16
HALF = HP // 2
STATE_ROWS = SN + 16
VMEM = pl.BlockSpec(memory_space=pltpu.VMEM)
SMEM = pl.BlockSpec(memory_space=pltpu.SMEM)
ANY = pl.BlockSpec(memory_space=pl.ANY)


def iota(shape, dim):
    return lax.broadcasted_iota(jnp.int32, shape, dim)


def ends_of(len_ref):
    e0 = len_ref[0]
    e1 = e0 + len_ref[1]
    return e0, e1, e1 + len_ref[2]


def start_of(pos, ends):
    e0, e1, e2 = ends
    zero = jnp.zeros_like(pos)
    out = jnp.where(pos >= e0, zero + e0, zero)
    out = jnp.where(pos >= e1, zero + e1, out)
    return jnp.where(pos >= e2, zero + e2, out)


def spread():
    return (iota((HEADS, HP), 1) // (HP // HEADS) == iota((HEADS, HP), 0)).astype(jnp.float32)


def widen(a, expand):
    return jnp.dot(a, expand, precision=HIGH, preferred_element_type=jnp.float32)


def ssd_kernel(len_ref, dl_ref, skip_ref, first_ref, x_ref, maps_ref, step_ref, y_ref, keep_ref, send_ref, fac_ref):
    first = first_ref[0]
    ends = ends_of(len_ref)
    expand = spread()
    head_sub = iota((HEADS, 1), 0)
    wide_lane = iota((1, HP), 1) // (HP // HEADS)
    rate = jnp.zeros((HEADS, 1), jnp.float32)
    skip = jnp.zeros((1, HP), jnp.float32)
    for h in range(HEADS):
        rate = jnp.where(head_sub == h, dl_ref[h], rate)
        skip = jnp.where(wide_lane == h, skip_ref[h], skip)
    rate = -jnp.exp(rate)
    row = iota((BLOCK, 1), 0)
    col = iota((1, BLOCK), 1)
    tri = (row >= col).astype(jnp.float32)
    half = iota((1, 128), 1) < 64
    state = None
    before = None
    for n in range(ROWS // BLOCK):
        rows = slice(n * BLOCK, (n + 1) * BLOCK)
        base = first + n * BLOCK
        start_col = start_of(base + row, ends)
        last_start = start_of(base + (BLOCK - 1), ends)
        cum_t = lax.dot_general(
            rate * step_ref[:, rows], tri, (((1,), (1,)), ((), ())), precision=HIGH, preferred_element_type=jnp.float32
        )
        cum = cum_t.T
        write = maps_ref[rows, :SN]
        read = maps_ref[rows, SN:]
        prod = lax.dot_general(read, write, (((1,), (1,)), ((), ())), preferred_element_type=jnp.float32)
        allowed = (base + col >= start_col) & (col <= row)
        for pair in range(HEADS // 2):
            lanes = slice(pair * 128, (pair + 1) * 128)
            x = x_ref[rows, lanes]
            total = skip[:, lanes] * x.astype(jnp.float32)
            for which in range(2):
                h = pair * 2 + which
                gap = jnp.where(allowed, cum[:, h : h + 1] - cum_t[h : h + 1, :], LOW)
                weights = (jnp.exp(gap) * prod).astype(jnp.bfloat16)
                part = jnp.where(half if which == 0 else ~half, x, jnp.zeros_like(x))
                total = total + jnp.dot(weights, part, preferred_element_type=jnp.float32)
            y_ref[rows, lanes] = total
        ecum = jnp.exp(cum)
        if state is not None:
            local = widen(jnp.where(start_col < base, ecum, 0.0), expand)
            reads = jnp.dot(read, state.astype(jnp.bfloat16), preferred_element_type=jnp.float32)
            y_ref[rows, :] += reads * local
        carry = jnp.where(start_col < first, ecum, 0.0)
        if before is not None:
            carry = carry * before
        fac_ref[rows, :] = carry
        tail = jnp.exp(cum[BLOCK - 1 : BLOCK, :] - cum)
        tail = widen(jnp.where(base + row >= last_start, tail, 0.0), expand)
        weighted = (x_ref[rows, :].astype(jnp.float32) * tail).astype(jnp.bfloat16)
        new = lax.dot_general(write, weighted, (((0,), (0,)), ((), ())), preferred_element_type=jnp.float32)
        end = ecum[BLOCK - 8 :, :]
        if state is not None:
            keep = jnp.where(last_start < base, 1.0, 0.0)
            new = new + (keep * widen(end, expand)[7:8, :]) * state
            end = end * before
        state = new
        before = end[7:8, :]
    through = jnp.where(last_start < first, 1.0, 0.0) * widen(end, expand)[7:8, :]
    core = (first // ROWS) % 2
    left, right = slice(0, HALF), slice(HALF, HP)
    for ref, wanted in ((keep_ref, 0), (send_ref, 1)):
        store_run(
            ref,
            jnp.where(core == wanted, state[:, left], state[:, right]),
            jnp.where(core == wanted, through[:, left], through[:, right]),
        )


def store_run(ref, state, through):
    high = through.astype(jnp.bfloat16).astype(jnp.float32)
    low = through - high
    sub = iota((16, 1), 0)
    ref[:SN, :] = state.astype(jnp.bfloat16)
    ref[SN:, :] = jnp.where(sub == 0, high, jnp.where(sub == 1, low, 0.0)).astype(jnp.bfloat16)


def load_run(ref):
    tail = ref[SN:, :].astype(jnp.float32)
    return ref[:SN, :].astype(jnp.float32), tail[0:1, :] + tail[1:2, :]


def pick(cond, one, other):
    return jnp.where(cond, one[0], other[0]), jnp.where(cond, one[1], other[1])


def after(earlier, later):
    return later[0] + later[1] * earlier[0], earlier[1] * later[1]


def chip_kernel(first_ref, mine_ref, other_ref, out_ref):
    core = (first_ref[0] // ROWS) % 2
    mine, other = load_run(mine_ref), load_run(other_ref)
    store_run(out_ref, *after(pick(core == 0, mine, other), pick(core == 0, other, mine)))


def row_kernel(first_ref, mine_ref, below_ref, above_ref, across_ref, prefix_ref, total_ref):
    y = (first_ref[0] // (2 * ROWS)) % 4
    by_distance = [load_run(ref) for ref in (mine_ref, below_ref, across_ref, above_ref)]
    run = (jnp.zeros((SN, HALF), jnp.float32), jnp.ones((1, HALF), jnp.float32))
    prefix = run
    for place in range(4):
        distance = (y - place) % 4
        piece = by_distance[0]
        for d in range(1, 4):
            piece = pick(distance == d, by_distance[d], piece)
        prefix = pick(y == place, run, prefix)
        run = after(run, piece)
    store_run(prefix_ref, *prefix)
    store_run(total_ref, *run)


def carry_kernel(first_ref, row3_ref, row2_ref, row1_ref, prefix_ref, mine_ref, other_ref, keep_ref, send_ref):
    core = (first_ref[0] // ROWS) % 2
    run = load_run(row3_ref)
    for ref in (row2_ref, row1_ref, prefix_ref):
        run = after(run, load_run(ref))
    behind = after(run, pick(core == 0, load_run(mine_ref), load_run(other_ref)))
    keep_ref[...] = jnp.where(core == 0, run[0], behind[0]).astype(jnp.bfloat16)
    send_ref[...] = jnp.where(core == 0, behind[0], run[0]).astype(jnp.bfloat16)


def gate_kernel(first_ref, y_ref, z_ref, read_ref, fac_ref, keep_ref, got_ref, act_ref):
    core = (first_ref[0] // ROWS) % 2
    keep, got = keep_ref[...], got_ref[...]
    state = jnp.concatenate([jnp.where(core == 0, keep, got), jnp.where(core == 0, got, keep)], axis=1)
    reads = jnp.dot(read_ref[...], state, preferred_element_type=jnp.float32)
    y = y_ref[...] + reads * widen(fac_ref[...], spread())
    z = z_ref[...].astype(jnp.float32)
    act_ref[...] = (y * (z / (1.0 + jnp.exp(-z)))).astype(jnp.bfloat16)


class Attention:
    def __init__(self, len_ref, first_ref, fetched, other, q_scr, kv_scr, ids, kinds, kv_sem, near_only=False):
        self.first = first_ref[0]
        self.ends = ends_of(len_ref)
        self.mine = self.first // CHUNK
        self.low = start_of(self.first, self.ends) // CHUNK
        self.last_start = start_of(self.first + ROWS - 1, self.ends)
        self.arrays = (fetched, other)
        self.near_only = near_only
        self.q_scr, self.kv_scr, self.ids, self.kinds, self.kv_sem = q_scr, kv_scr, ids, kinds, kv_sem

    def count(self, far):
        return 4 if self.near_only else (self.mine - far - self.low) // 2 + 1

    def block(self, far, i):
        if not self.near_only:
            return self.mine - far - 2 * i
        core = self.mine % 2
        step = jnp.where(core == far, 2, 8)
        return self.mine + jnp.where(core == 0, far, -far) - step * i

    def in_line(self, block):
        row = self.mine // 2 - block // 2 <= 3
        column = (block // 2) % 4 == (self.mine // 2) % 4
        return jnp.where(block % 2 == 0, row, column)

    def place(self, block):
        chip, even = block // 2, block % 2 == 0
        my_x, my_y = self.mine // 8, (self.mine // 2) % 4
        distance = jnp.where(even, (my_y - chip) % 4, (my_x - chip // 4) % 4)
        place = distance ^ (distance >> 1)
        if not self.near_only:
            place = place + 4 * jnp.where(even, (chip + distance) // 4, chip % 4)
        return place

    def copy(self, far, place, slot):
        rows = pl.ds(pl.multiple_of(place * CHUNK, CHUNK), CHUNK)
        to = pl.ds(pl.multiple_of(slot * CHUNK, CHUNK), CHUNK)
        return pltpu.make_async_copy(self.arrays[far].at[rows], self.kv_scr.at[to], self.kv_sem.at[slot])

    def fetch(self, fars, every=False):
        def one_chunk(far, i, carry):
            plain, masked = carry
            block = self.block(far, i)
            if self.near_only:
                wanted = (block >= self.low) & (block <= self.mine)
            elif every:
                wanted = block >= self.low
            else:
                wanted = jnp.logical_not(self.in_line(block))
            mask = (block == self.mine) | (block * CHUNK < self.last_start)
            slot = jnp.where(mask, SLOTS - 1 - masked, plain)

            @pl.when(wanted)
            def _():
                self.ids[slot] = block
                inside = start_of(block * CHUNK + (CHUNK - 1), self.ends) > block * CHUNK
                self.kinds[slot] = jnp.where((block == self.mine) | inside, 1, 0)
                self.copy(far, self.place(block), slot).start()

            new = wanted.astype(jnp.int32)
            return plain + jnp.where(mask, 0, new), masked + jnp.where(mask, new, 0)

        carry = (jnp.int32(0), jnp.int32(0))
        for far in fars:
            carry = lax.fori_loop(0, self.count(far), lambda i, c, far=far: one_chunk(far, i, c), carry)
        self.plain, self.masked = carry

    def wait(self, slot):
        self.copy(0, 0, slot).wait()

    def keys(self, slot, chunks):
        return pl.ds(pl.multiple_of(slot * CHUNK, CHUNK), chunks * CHUNK)

    def scores(self, slot, chunks, r, masked):
        rows = slice(r * TILE, (r + 1) * TILE)
        k = self.kv_scr[self.keys(slot, chunks), :HD]
        s = lax.dot_general(
            self.q_scr[rows, :],
            jnp.concatenate([k, k], axis=1),
            (((1,), (1,)), ((), ())),
            preferred_element_type=jnp.float32,
        )
        if masked:
            pos = self.first + rows.start % ROWS + iota((TILE, 1), 0)
            key = self.ids[slot] * CHUNK + iota((1, CHUNK), 1)
            s = jnp.where((key >= start_of(pos, self.ends)) & (key <= pos), s, LOW)
        return s

    def values(self, slot, chunks):
        v = self.kv_scr[self.keys(slot, chunks), HD:]
        return jnp.concatenate([v, jnp.ones((chunks * CHUNK, HD), jnp.bfloat16)], axis=1)

    def step(self, acc, slot, chunks, masked, by_row=False):
        v = self.values(slot, chunks)
        tiles = 2 * ROWS // TILE
        s = self.scores(slot, chunks, 0, masked)
        for r in range(tiles):
            following = self.scores(slot, chunks, r + 1, masked) if r + 1 < tiles else None
            p = jnp.exp2(s).astype(jnp.bfloat16)
            out = jnp.dot(p, v, preferred_element_type=jnp.float32)
            if by_row:
                pos = self.first + (r * TILE) % ROWS + iota((TILE, 1), 0)
                out = jnp.where(start_of(pos, self.ends) <= self.ids[slot] * CHUNK, out, 0.0)
            acc[r * TILE : (r + 1) * TILE, :] += out
            s = following

    def add(self, acc):
        def one_masked(j, _):
            slot = SLOTS - 1 - j
            self.wait(slot)
            pl.when(self.kinds[slot] == 0)(lambda: self.step(acc, slot, 1, False, by_row=True))
            pl.when(self.kinds[slot] == 1)(lambda: self.step(acc, slot, 1, True))
            return 0

        def two_plain(j, _):
            self.wait(2 * j)
            self.wait(2 * j + 1)
            self.step(acc, 2 * j, 2, False)
            return 0

        lax.fori_loop(0, self.masked, one_masked, 0)
        lax.fori_loop(0, self.plain // 2, two_plain, 0)

        @pl.when(self.plain % 2 == 1)
        def _():
            self.wait(self.plain - 1)
            self.step(acc, self.plain - 1, 1, False)

    def add_shifted(self, acc, m_scr):
        def one_chunk(j, _):
            slot = jnp.where(j < self.plain, j, SLOTS - 1 - (j - self.plain))
            self.wait(slot)
            v = self.values(slot, 1)
            for r in range(2 * ROWS // TILE):
                rows = slice(r * TILE, (r + 1) * TILE)
                s = self.scores(slot, 1, r, True)
                old = m_scr[rows, :]
                m = jnp.maximum(old, jnp.max(s, axis=1, keepdims=True))
                alpha = jnp.exp2(old - m)
                p = jnp.exp2(s - jnp.concatenate([m] * (CHUNK // 128), axis=1)).astype(jnp.bfloat16)
                out = jnp.dot(p, v, preferred_element_type=jnp.float32)
                acc[rows, :] = acc[rows, :] * jnp.concatenate([alpha, alpha], axis=1) + out
                m_scr[rows, :] = m
            return 0

        lax.fori_loop(0, self.plain + self.masked, one_chunk, 0)


def own_line_kernel(len_ref, first_ref, q_ref, line, acc_ref, split_ref, kv_scr, ids, kinds, kv_sem):
    attention = Attention(len_ref, first_ref, line, None, split_ref, kv_scr, ids, kinds, kv_sem, near_only=True)
    attention.fetch((0,))
    for g in range(2):
        rows = slice(g * ROWS, (g + 1) * ROWS)
        scaled = q_ref[:, g * HD : (g + 1) * HD].astype(jnp.float32) * (LOG2E * HD**-0.5)
        high = scaled.astype(jnp.bfloat16)
        split_ref[rows, :HD] = high
        split_ref[rows, HD:] = (scaled - high.astype(jnp.float32)).astype(jnp.bfloat16)
    acc_ref[...] = jnp.zeros_like(acc_ref)
    attention.add(acc_ref)


def other_line_kernel(len_ref, first_ref, split_ref, before_ref, line_got, acc_ref, kv_scr, ids, kinds, kv_sem):
    attention = Attention(len_ref, first_ref, line_got, line_got, split_ref, kv_scr, ids, kinds, kv_sem, near_only=True)
    attention.fetch((1,))
    acc_ref[...] = before_ref[...]
    attention.add(acc_ref)


def part_kernel(
    len_ref, first_ref, split_hbm, before_hbm, fetched, acc_ref, kv_scr, ids, kinds, kv_sem, q_scr, in_sem
):
    attention = Attention(len_ref, first_ref, fetched, None, q_scr, kv_scr, ids, kinds, kv_sem)
    inputs = [
        pltpu.make_async_copy(split_hbm, q_scr, in_sem.at[0]),
        pltpu.make_async_copy(before_hbm, acc_ref, in_sem.at[1]),
    ]
    for copy in inputs:
        copy.start()
    attention.fetch((0,))
    for copy in inputs:
        copy.wait()
    attention.add(acc_ref)


def mix_kernel(
    len_ref,
    first_ref,
    split_hbm,
    act_hbm,
    before_hbm,
    fetched,
    other,
    wa_hbm,
    ws_hbm,
    o_hbm,
    kv_scr,
    ids,
    kinds,
    kv_sem,
    q_scr,
    acc_scr,
    m_scr,
    w_scr,
    in_scr,
    o_scr,
    in_sem,
    w_sem,
    o_sem,
):
    attention = Attention(len_ref, first_ref, fetched, other, q_scr, kv_scr, ids, kinds, kv_sem)
    inputs = [
        pltpu.make_async_copy(split_hbm, q_scr, in_sem.at[0]),
        pltpu.make_async_copy(before_hbm, acc_scr, in_sem.at[1]),
        pltpu.make_async_copy(act_hbm, in_scr.at[:, pl.ds(2 * HD, HP)], in_sem.at[2]),
    ]
    for copy in inputs[:2]:
        copy.start()
    attention.fetch((1,))
    weights = []
    for i in range(DM // COLS):
        cols = pl.ds(i * COLS, COLS)
        weights.append(
            (
                pltpu.make_async_copy(wa_hbm.at[:, cols], w_scr.at[pl.ds(0, 2 * HD), cols], w_sem.at[2 * i]),
                pltpu.make_async_copy(ws_hbm.at[:, cols], w_scr.at[pl.ds(2 * HD, HP), cols], w_sem.at[2 * i + 1]),
            )
        )
    for copy in inputs[:2]:
        copy.wait()
    inputs[2].start()
    for pair in weights:
        for copy in pair:
            copy.start()

    attention.add(acc_scr)
    total = acc_scr[:, HD:]
    fine = (jnp.min(total) > 2.0**-60) & (jnp.max(total) < 2.0**110)

    @pl.when(jnp.logical_not(fine))
    def _():
        attention.fetch((0, 1), every=True)
        acc_scr[...] = jnp.zeros_like(acc_scr)
        m_scr[...] = jnp.full(m_scr.shape, LOW, jnp.float32)
        attention.add_shifted(acc_scr, m_scr)

    for g in range(2):
        rows = slice(g * ROWS, (g + 1) * ROWS)
        in_scr[:, g * HD : (g + 1) * HD] = (acc_scr[rows, :HD] / acc_scr[rows, HD:]).astype(jnp.bfloat16)
    inputs[2].wait()

    def out_copy(i):
        cols = pl.ds(i * COLS, COLS)
        return pltpu.make_async_copy(o_scr.at[:, cols], o_hbm.at[:, cols], o_sem.at[i])

    for i in range(DM // COLS):
        cols = slice(i * COLS, (i + 1) * COLS)
        for copy in weights[i]:
            copy.wait()
        o_scr[:, cols] = jnp.dot(in_scr[...], w_scr[:, cols], preferred_element_type=jnp.float32).astype(jnp.bfloat16)
        out_copy(i).start()
    for i in range(DM // COLS):
        out_copy(i).wait()


def big(limit=LIMIT):
    return pltpu.CompilerParams(vmem_limit_bytes=limit)


def moved(block, route0, route1):
    pairs = []
    for x in range(4):
        for y in range(4):
            for core, route in enumerate((route0, route1)):
                to = route(x, y)
                if to is not None:
                    pairs.append((x * 8 + y * 2 + core, to[0] * 8 + to[1] * 2 + core))
    return lax.ppermute(block, "pack", pairs)


def lines():
    columns = [[x * 8 + y * 2 for x in range(4)] for y in range(4)]
    rows = [[x * 8 + y * 2 + 1 for y in range(4)] for x in range(4)]
    return columns + rows


def along_x(distance):
    return lambda x, y: (x + distance, y) if x + distance < 4 else None


def along_tokens(distance):
    def to(x, y):
        chip = 4 * x + y + distance
        return (chip // 4, chip % 4) if chip < 16 else None

    return to


def along_y(distance):
    return lambda x, y: (x, (y + distance) % 4)


def swapped(block):
    return lax.ppermute(block, "pack", [(i, i ^ 1) for i in range(32)])


def call(kernel, shapes, ins, *args):
    return pl.pallas_call(
        kernel,
        out_shape=tuple(jax.ShapeDtypeStruct(shape, jnp.bfloat16) for shape in shapes),
        in_specs=[SMEM] + [VMEM] * ins,
        out_specs=(VMEM,) * len(shapes),
        compiler_params=big(),
        cost_estimate=pl.CostEstimate(flops=10**6, bytes_accessed=10**6, transcendentals=0),
    )(*args)


def local(
    queries,
    keys_values,
    ssm_values,
    ssm_gates,
    ssm_maps,
    step_size,
    decay_log,
    skip_gain,
    attn_out_weight,
    ssd_out_weight,
    lengths,
):
    first = jnp.reshape(lax.axis_index("pack") * ROWS, (1,)).astype(jnp.int32)
    kv = keys_values.reshape(ROWS, 2 * HD)
    nowhere = lambda x, y: None
    one, three, two = [moved(kv, along_tokens(d), along_x(d)) for d in (1, 3, 2)]
    y_local, run_keep, run_send, fac = pl.pallas_call(
        ssd_kernel,
        out_shape=(
            jax.ShapeDtypeStruct((ROWS, HP), jnp.float32),
            jax.ShapeDtypeStruct((STATE_ROWS, HALF), jnp.bfloat16),
            jax.ShapeDtypeStruct((STATE_ROWS, HALF), jnp.bfloat16),
            jax.ShapeDtypeStruct((ROWS, HEADS), jnp.float32),
        ),
        in_specs=[SMEM] * 4 + [VMEM] * 3,
        out_specs=(VMEM, VMEM, VMEM, VMEM),
        compiler_params=big(62 * 2**20),
        cost_estimate=pl.CostEstimate(flops=10**9, bytes_accessed=4 * 10**6, transcendentals=10**6),
        name="ssd_local",
    )(lengths, decay_log, skip_gain, first, ssm_values, ssm_maps, step_size.T)

    one, three, two = lax.optimization_barrier((one, three, two, fac))[:3]
    line = jnp.concatenate([kv, one, three, two], axis=0)
    fetched = lax.all_gather(line, "pack", axis=0, tiled=True, axis_index_groups=lines())
    line_got = swapped(line)

    run = (STATE_ROWS, HALF)
    run_got = swapped(run_send)
    (chip,) = call(chip_kernel, [run], 2, first, run_keep, run_got)
    chips = [moved(chip, along_y(d), along_y(d)) for d in (1, 3, 2)]
    chunks_scratch = [
        pltpu.VMEM((SLOTS * CHUNK, 2 * HD), jnp.bfloat16),
        pltpu.SMEM((SLOTS,), jnp.int32),
        pltpu.SMEM((SLOTS,), jnp.int32),
        pltpu.SemaphoreType.DMA((SLOTS,)),
    ]
    sums = jax.ShapeDtypeStruct((2 * ROWS, 2 * HD), jnp.float32)
    split = jax.ShapeDtypeStruct((2 * ROWS, 2 * HD), jnp.bfloat16)

    def attend(kernel, name, shapes, vmem, *args, scratch=()):
        out = pl.pallas_call(
            kernel,
            out_shape=shapes,
            in_specs=[SMEM] * 2 + [VMEM] * vmem + [ANY] * (len(args) - vmem),
            out_specs=(VMEM,) * len(shapes),
            scratch_shapes=chunks_scratch + list(scratch),
            compiler_params=big(),
            cost_estimate=pl.CostEstimate(flops=3 * 10**9, bytes_accessed=5 * 10**6, transcendentals=5 * 10**6),
            name=name,
        )(lengths, first, *args)
        return out

    line = lax.optimization_barrier((line, chip))[0]
    acc, queries_split = attend(own_line_kernel, "own_line", (sums, split), 1, queries, line)
    chips = lax.optimization_barrier((*chips, acc))[:3]
    prefix, total = call(row_kernel, [run, run], 4, first, chip, *chips)
    rows = [moved(total, along_x(d), along_x(d)) for d in (3, 2, 1)]
    line_got = lax.optimization_barrier((line_got, prefix))[0]
    (acc,) = attend(other_line_kernel, "other_line", (sums,), 2, queries_split, acc, line_got)
    rows = lax.optimization_barrier((*rows, acc))[:3]
    keep, send = call(carry_kernel, [(SN, HALF)] * 2, 6, first, *rows, prefix, run_keep, run_got)
    got = swapped(send)
    act = pl.pallas_call(
        gate_kernel,
        out_shape=jax.ShapeDtypeStruct((ROWS, HP), jnp.bfloat16),
        grid=(2,),
        in_specs=[
            SMEM,
            pl.BlockSpec((ROWS // 2, HP), lambda i: (i, 0)),
            pl.BlockSpec((ROWS // 2, HP), lambda i: (i, 0)),
            pl.BlockSpec((ROWS // 2, SN), lambda i: (i, 1)),
            pl.BlockSpec((ROWS // 2, HEADS), lambda i: (i, 0)),
            pl.BlockSpec((SN, HALF), lambda i: (0, 0)),
            pl.BlockSpec((SN, HALF), lambda i: (0, 0)),
        ],
        out_specs=pl.BlockSpec((ROWS // 2, HP), lambda i: (i, 0)),
        compiler_params=big(),
        cost_estimate=pl.CostEstimate(flops=10**8, bytes_accessed=3 * 10**6, transcendentals=3 * 10**5),
        name="gate",
    )(first, y_local, ssm_gates, ssm_maps, fac, keep, got)

    fetched = lax.optimization_barrier((fetched, act))[0]
    other = swapped(fetched)
    (acc,) = attend(
        part_kernel,
        "part",
        (sums,),
        0,
        queries_split,
        acc,
        fetched,
        scratch=[pltpu.VMEM((2 * ROWS, 2 * HD), jnp.bfloat16), pltpu.SemaphoreType.DMA((2,))],
    )

    terms = pl.pallas_call(
        mix_kernel,
        out_shape=jax.ShapeDtypeStruct((ROWS, DM), jnp.bfloat16),
        in_specs=[SMEM] * 2 + [ANY] * 7,
        out_specs=ANY,
        scratch_shapes=chunks_scratch
        + [
            pltpu.VMEM((2 * ROWS, 2 * HD), jnp.bfloat16),
            pltpu.VMEM((2 * ROWS, 2 * HD), jnp.float32),
            pltpu.VMEM((2 * ROWS, HD), jnp.float32),
            pltpu.VMEM((2 * HD + HP, DM), jnp.bfloat16),
            pltpu.VMEM((ROWS, 2 * HD + HP), jnp.bfloat16),
            pltpu.VMEM((ROWS, DM), jnp.bfloat16),
            pltpu.SemaphoreType.DMA((3,)),
            pltpu.SemaphoreType.DMA((2 * (DM // COLS),)),
            pltpu.SemaphoreType.DMA((DM // COLS,)),
        ],
        compiler_params=big(),
        cost_estimate=pl.CostEstimate(flops=9 * 10**9, bytes_accessed=25 * 10**6, transcendentals=9 * 10**6),
        name="mix",
    )(lengths, first, queries_split, act, acc, fetched, other, attn_out_weight, ssd_out_weight)
    return lax.psum_scatter(terms, "tp", scatter_dimension=0, tiled=True)


def solution(mesh):
    return jax.shard_map(
        local,
        mesh=mesh,
        in_specs=(
            P("pack", "tp"),
            P("pack", "tp", None),
            P("pack", "tp"),
            P("pack", "tp"),
            P("pack", None),
            P("pack", "tp"),
            P("tp"),
            P("tp"),
            P("tp", None),
            P("tp", None),
            P(),
        ),
        out_specs=P(("pack", "tp"), None),
        check_vma=False,
    )
```

```python
import jax
import jax.numpy as jnp
from jax import lax
from jax.experimental import pallas as pl
from jax.experimental.pallas import tpu as pltpu
from jax.sharding import PartitionSpec as P

ROWS = 512
BLOCK = 256
HD = 128
HEADS = 8
HP = 512
SN = 256
DM = 5120
CHUNK = 512
SLOTS = 18
TILE = 256
COLS = 1024
LOW = -1e30
LOG2E = 1.4426950408889634
HIGH = lax.Precision.HIGHEST
LIMIT = 64 * 2**20 - 2**16
HALF = HP // 2
STATE_ROWS = SN + 16
VMEM = pl.BlockSpec(memory_space=pltpu.VMEM)
SMEM = pl.BlockSpec(memory_space=pltpu.SMEM)
ANY = pl.BlockSpec(memory_space=pl.ANY)


def iota(shape, dim):
    return lax.broadcasted_iota(jnp.int32, shape, dim)


def ends_of(len_ref):
    e0 = len_ref[0]
    e1 = e0 + len_ref[1]
    return e0, e1, e1 + len_ref[2]


def start_of(pos, ends):
    e0, e1, e2 = ends
    zero = jnp.zeros_like(pos)
    out = jnp.where(pos >= e0, zero + e0, zero)
    out = jnp.where(pos >= e1, zero + e1, out)
    return jnp.where(pos >= e2, zero + e2, out)


def spread():
    return (iota((HEADS, HP), 1) // (HP // HEADS) == iota((HEADS, HP), 0)).astype(jnp.float32)


def widen(a, expand):
    return jnp.dot(a, expand, precision=HIGH, preferred_element_type=jnp.float32)


def ssd_kernel(len_ref, dl_ref, skip_ref, first_ref, x_ref, maps_ref, step_ref, y_ref, keep_ref, send_ref, fac_ref):
    first = first_ref[0]
    ends = ends_of(len_ref)
    expand = spread()
    head_sub = iota((HEADS, 1), 0)
    wide_lane = iota((1, HP), 1) // (HP // HEADS)
    rate = jnp.zeros((HEADS, 1), jnp.float32)
    skip = jnp.zeros((1, HP), jnp.float32)
    for h in range(HEADS):
        rate = jnp.where(head_sub == h, dl_ref[h], rate)
        skip = jnp.where(wide_lane == h, skip_ref[h], skip)
    rate = -jnp.exp(rate)
    row = iota((BLOCK, 1), 0)
    col = iota((1, BLOCK), 1)
    tri = (row >= col).astype(jnp.float32)
    half = iota((1, 128), 1) < 64
    state = None
    before = None
    for n in range(ROWS // BLOCK):
        rows = slice(n * BLOCK, (n + 1) * BLOCK)
        base = first + n * BLOCK
        start_col = start_of(base + row, ends)
        last_start = start_of(base + (BLOCK - 1), ends)
        cum_t = lax.dot_general(
            rate * step_ref[:, rows], tri, (((1,), (1,)), ((), ())), precision=HIGH, preferred_element_type=jnp.float32
        )
        cum = cum_t.T
        write = maps_ref[rows, :SN]
        read = maps_ref[rows, SN:]
        prod = lax.dot_general(read, write, (((1,), (1,)), ((), ())), preferred_element_type=jnp.float32)
        allowed = (base + col >= start_col) & (col <= row)
        for pair in range(HEADS // 2):
            lanes = slice(pair * 128, (pair + 1) * 128)
            x = x_ref[rows, lanes]
            total = skip[:, lanes] * x.astype(jnp.float32)
            for which in range(2):
                h = pair * 2 + which
                gap = jnp.where(allowed, cum[:, h : h + 1] - cum_t[h : h + 1, :], LOW)
                weights = (jnp.exp(gap) * prod).astype(jnp.bfloat16)
                part = jnp.where(half if which == 0 else ~half, x, jnp.zeros_like(x))
                total = total + jnp.dot(weights, part, preferred_element_type=jnp.float32)
            y_ref[rows, lanes] = total
        ecum = jnp.exp(cum)
        if state is not None:
            local = widen(jnp.where(start_col < base, ecum, 0.0), expand)
            reads = jnp.dot(read, state.astype(jnp.bfloat16), preferred_element_type=jnp.float32)
            y_ref[rows, :] += reads * local
        carry = jnp.where(start_col < first, ecum, 0.0)
        if before is not None:
            carry = carry * before
        fac_ref[rows, :] = carry
        tail = jnp.exp(cum[BLOCK - 1 : BLOCK, :] - cum)
        tail = widen(jnp.where(base + row >= last_start, tail, 0.0), expand)
        weighted = (x_ref[rows, :].astype(jnp.float32) * tail).astype(jnp.bfloat16)
        new = lax.dot_general(write, weighted, (((0,), (0,)), ((), ())), preferred_element_type=jnp.float32)
        end = ecum[BLOCK - 8 :, :]
        if state is not None:
            keep = jnp.where(last_start < base, 1.0, 0.0)
            new = new + (keep * widen(end, expand)[7:8, :]) * state
            end = end * before
        state = new
        before = end[7:8, :]
    through = jnp.where(last_start < first, 1.0, 0.0) * widen(end, expand)[7:8, :]
    core = (first // ROWS) % 2
    left, right = slice(0, HALF), slice(HALF, HP)
    for ref, wanted in ((keep_ref, 0), (send_ref, 1)):
        store_run(
            ref,
            jnp.where(core == wanted, state[:, left], state[:, right]),
            jnp.where(core == wanted, through[:, left], through[:, right]),
        )


def store_run(ref, state, through):
    high = through.astype(jnp.bfloat16).astype(jnp.float32)
    low = through - high
    sub = iota((16, 1), 0)
    ref[:SN, :] = state.astype(jnp.bfloat16)
    ref[SN:, :] = jnp.where(sub == 0, high, jnp.where(sub == 1, low, 0.0)).astype(jnp.bfloat16)


def load_run(ref):
    tail = ref[SN:, :].astype(jnp.float32)
    return ref[:SN, :].astype(jnp.float32), tail[0:1, :] + tail[1:2, :]


def pick(cond, one, other):
    return jnp.where(cond, one[0], other[0]), jnp.where(cond, one[1], other[1])


def after(earlier, later):
    return later[0] + later[1] * earlier[0], earlier[1] * later[1]


def chip_kernel(first_ref, mine_ref, other_ref, out_ref):
    core = (first_ref[0] // ROWS) % 2
    mine, other = load_run(mine_ref), load_run(other_ref)
    store_run(out_ref, *after(pick(core == 0, mine, other), pick(core == 0, other, mine)))


def row_kernel(first_ref, mine_ref, below_ref, above_ref, across_ref, prefix_ref, total_ref):
    y = (first_ref[0] // (2 * ROWS)) % 4
    by_distance = [load_run(ref) for ref in (mine_ref, below_ref, across_ref, above_ref)]
    run = (jnp.zeros((SN, HALF), jnp.float32), jnp.ones((1, HALF), jnp.float32))
    prefix = run
    for place in range(4):
        distance = (y - place) % 4
        piece = by_distance[0]
        for d in range(1, 4):
            piece = pick(distance == d, by_distance[d], piece)
        prefix = pick(y == place, run, prefix)
        run = after(run, piece)
    store_run(prefix_ref, *prefix)
    store_run(total_ref, *run)


def carry_kernel(first_ref, row3_ref, row2_ref, row1_ref, prefix_ref, mine_ref, other_ref, keep_ref, send_ref):
    core = (first_ref[0] // ROWS) % 2
    run = load_run(row3_ref)
    for ref in (row2_ref, row1_ref, prefix_ref):
        run = after(run, load_run(ref))
    behind = after(run, pick(core == 0, load_run(mine_ref), load_run(other_ref)))
    keep_ref[...] = jnp.where(core == 0, run[0], behind[0]).astype(jnp.bfloat16)
    send_ref[...] = jnp.where(core == 0, behind[0], run[0]).astype(jnp.bfloat16)


def gate_kernel(first_ref, y_ref, z_ref, read_ref, fac_ref, keep_ref, got_ref, act_ref):
    core = (first_ref[0] // ROWS) % 2
    keep, got = keep_ref[...], got_ref[...]
    state = jnp.concatenate([jnp.where(core == 0, keep, got), jnp.where(core == 0, got, keep)], axis=1)
    reads = jnp.dot(read_ref[...], state, preferred_element_type=jnp.float32)
    y = y_ref[...] + reads * widen(fac_ref[...], spread())
    z = z_ref[...].astype(jnp.float32)
    act_ref[...] = (y * (z / (1.0 + jnp.exp(-z)))).astype(jnp.bfloat16)


class Attention:
    def __init__(self, len_ref, first_ref, fetched, other, q_scr, kv_scr, ids, kinds, kv_sem, near_only=False):
        self.first = first_ref[0]
        self.ends = ends_of(len_ref)
        self.mine = self.first // CHUNK
        self.low = start_of(self.first, self.ends) // CHUNK
        self.last_start = start_of(self.first + ROWS - 1, self.ends)
        self.arrays = (fetched, other)
        self.near_only = near_only
        self.q_scr, self.kv_scr, self.ids, self.kinds, self.kv_sem = q_scr, kv_scr, ids, kinds, kv_sem

    def count(self, far):
        return 4 if self.near_only else (self.mine - far - self.low) // 2 + 1

    def block(self, far, i):
        if not self.near_only:
            return self.mine - far - 2 * i
        core = self.mine % 2
        step = jnp.where(core == far, 2, 8)
        return self.mine + jnp.where(core == 0, far, -far) - step * i

    def in_line(self, block):
        row = block // 8 == self.mine // 8
        column = (block // 2) % 4 == (self.mine // 2) % 4
        return jnp.where(block % 2 == 0, row, column)

    def place(self, block):
        x, y, even = block // 8, (block // 2) % 4, block % 2 == 0
        my_x, my_y = self.mine // 8, (self.mine // 2) % 4
        distance = jnp.where(even, (my_y - y) % 4, (my_x - x) % 4)
        place = distance ^ (distance >> 1)
        if not self.near_only:
            place = place + 4 * jnp.where(even, x, y)
        return place

    def copy(self, far, place, slot):
        rows = pl.ds(pl.multiple_of(place * CHUNK, CHUNK), CHUNK)
        to = pl.ds(pl.multiple_of(slot * CHUNK, CHUNK), CHUNK)
        return pltpu.make_async_copy(self.arrays[far].at[rows], self.kv_scr.at[to], self.kv_sem.at[slot])

    def fetch(self, fars, every=False):
        def one_chunk(far, i, carry):
            plain, masked = carry
            block = self.block(far, i)
            if self.near_only:
                wanted = (block >= self.low) & (block <= self.mine) & self.in_line(block)
            elif every:
                wanted = block >= self.low
            else:
                wanted = jnp.logical_not(self.in_line(block))
            mask = (block == self.mine) | (block * CHUNK < self.last_start)
            slot = jnp.where(mask, SLOTS - 1 - masked, plain)

            @pl.when(wanted)
            def _():
                self.ids[slot] = block
                inside = start_of(block * CHUNK + (CHUNK - 1), self.ends) > block * CHUNK
                self.kinds[slot] = jnp.where((block == self.mine) | inside, 1, 0)
                self.copy(far, self.place(block), slot).start()

            new = wanted.astype(jnp.int32)
            return plain + jnp.where(mask, 0, new), masked + jnp.where(mask, new, 0)

        carry = (jnp.int32(0), jnp.int32(0))
        for far in fars:
            carry = lax.fori_loop(0, self.count(far), lambda i, c, far=far: one_chunk(far, i, c), carry)
        self.plain, self.masked = carry

    def wait(self, slot):
        self.copy(0, 0, slot).wait()

    def keys(self, slot, chunks):
        return pl.ds(pl.multiple_of(slot * CHUNK, CHUNK), chunks * CHUNK)

    def scores(self, slot, chunks, r, masked):
        rows = slice(r * TILE, (r + 1) * TILE)
        k = self.kv_scr[self.keys(slot, chunks), :HD]
        s = lax.dot_general(
            self.q_scr[rows, :],
            jnp.concatenate([k, k], axis=1),
            (((1,), (1,)), ((), ())),
            preferred_element_type=jnp.float32,
        )
        if masked:
            pos = self.first + rows.start % ROWS + iota((TILE, 1), 0)
            key = self.ids[slot] * CHUNK + iota((1, CHUNK), 1)
            s = jnp.where((key >= start_of(pos, self.ends)) & (key <= pos), s, LOW)
        return s

    def values(self, slot, chunks):
        v = self.kv_scr[self.keys(slot, chunks), HD:]
        return jnp.concatenate([v, jnp.ones((chunks * CHUNK, HD), jnp.bfloat16)], axis=1)

    def step(self, acc, slot, chunks, masked, by_row=False):
        v = self.values(slot, chunks)
        tiles = 2 * ROWS // TILE
        s = self.scores(slot, chunks, 0, masked)
        for r in range(tiles):
            following = self.scores(slot, chunks, r + 1, masked) if r + 1 < tiles else None
            p = jnp.exp2(s).astype(jnp.bfloat16)
            out = jnp.dot(p, v, preferred_element_type=jnp.float32)
            if by_row:
                pos = self.first + (r * TILE) % ROWS + iota((TILE, 1), 0)
                out = jnp.where(start_of(pos, self.ends) <= self.ids[slot] * CHUNK, out, 0.0)
            acc[r * TILE : (r + 1) * TILE, :] += out
            s = following

    def add(self, acc):
        def one_masked(j, _):
            slot = SLOTS - 1 - j
            self.wait(slot)
            pl.when(self.kinds[slot] == 0)(lambda: self.step(acc, slot, 1, False, by_row=True))
            pl.when(self.kinds[slot] == 1)(lambda: self.step(acc, slot, 1, True))
            return 0

        def two_plain(j, _):
            self.wait(2 * j)
            self.wait(2 * j + 1)
            self.step(acc, 2 * j, 2, False)
            return 0

        lax.fori_loop(0, self.masked, one_masked, 0)
        lax.fori_loop(0, self.plain // 2, two_plain, 0)

        @pl.when(self.plain % 2 == 1)
        def _():
            self.wait(self.plain - 1)
            self.step(acc, self.plain - 1, 1, False)

    def add_shifted(self, acc, m_scr):
        def one_chunk(j, _):
            slot = jnp.where(j < self.plain, j, SLOTS - 1 - (j - self.plain))
            self.wait(slot)
            v = self.values(slot, 1)
            for r in range(2 * ROWS // TILE):
                rows = slice(r * TILE, (r + 1) * TILE)
                s = self.scores(slot, 1, r, True)
                old = m_scr[rows, :]
                m = jnp.maximum(old, jnp.max(s, axis=1, keepdims=True))
                alpha = jnp.exp2(old - m)
                p = jnp.exp2(s - jnp.concatenate([m] * (CHUNK // 128), axis=1)).astype(jnp.bfloat16)
                out = jnp.dot(p, v, preferred_element_type=jnp.float32)
                acc[rows, :] = acc[rows, :] * jnp.concatenate([alpha, alpha], axis=1) + out
                m_scr[rows, :] = m
            return 0

        lax.fori_loop(0, self.plain + self.masked, one_chunk, 0)


def own_line_kernel(len_ref, first_ref, q_ref, line, acc_ref, split_ref, kv_scr, ids, kinds, kv_sem):
    attention = Attention(len_ref, first_ref, line, None, split_ref, kv_scr, ids, kinds, kv_sem, near_only=True)
    attention.fetch((0,))
    for g in range(2):
        rows = slice(g * ROWS, (g + 1) * ROWS)
        scaled = q_ref[:, g * HD : (g + 1) * HD].astype(jnp.float32) * (LOG2E * HD**-0.5)
        high = scaled.astype(jnp.bfloat16)
        split_ref[rows, :HD] = high
        split_ref[rows, HD:] = (scaled - high.astype(jnp.float32)).astype(jnp.bfloat16)
    acc_ref[...] = jnp.zeros_like(acc_ref)
    attention.add(acc_ref)


def other_line_kernel(len_ref, first_ref, split_ref, before_ref, line_got, acc_ref, kv_scr, ids, kinds, kv_sem):
    attention = Attention(len_ref, first_ref, line_got, line_got, split_ref, kv_scr, ids, kinds, kv_sem, near_only=True)
    attention.fetch((1,))
    acc_ref[...] = before_ref[...]
    attention.add(acc_ref)


def part_kernel(
    len_ref, first_ref, split_hbm, before_hbm, fetched, acc_ref, kv_scr, ids, kinds, kv_sem, q_scr, in_sem
):
    attention = Attention(len_ref, first_ref, fetched, None, q_scr, kv_scr, ids, kinds, kv_sem)
    inputs = [
        pltpu.make_async_copy(split_hbm, q_scr, in_sem.at[0]),
        pltpu.make_async_copy(before_hbm, acc_ref, in_sem.at[1]),
    ]
    for copy in inputs:
        copy.start()
    attention.fetch((0,))
    for copy in inputs:
        copy.wait()
    attention.add(acc_ref)


def mix_kernel(
    len_ref,
    first_ref,
    split_hbm,
    act_hbm,
    before_hbm,
    fetched,
    other,
    wa_hbm,
    ws_hbm,
    o_hbm,
    kv_scr,
    ids,
    kinds,
    kv_sem,
    q_scr,
    acc_scr,
    m_scr,
    w_scr,
    in_scr,
    o_scr,
    in_sem,
    w_sem,
    o_sem,
):
    attention = Attention(len_ref, first_ref, fetched, other, q_scr, kv_scr, ids, kinds, kv_sem)
    inputs = [
        pltpu.make_async_copy(split_hbm, q_scr, in_sem.at[0]),
        pltpu.make_async_copy(before_hbm, acc_scr, in_sem.at[1]),
        pltpu.make_async_copy(act_hbm, in_scr.at[:, pl.ds(2 * HD, HP)], in_sem.at[2]),
    ]
    for copy in inputs[:2]:
        copy.start()
    attention.fetch((1,))
    weights = []
    for i in range(DM // COLS):
        cols = pl.ds(i * COLS, COLS)
        weights.append(
            (
                pltpu.make_async_copy(wa_hbm.at[:, cols], w_scr.at[pl.ds(0, 2 * HD), cols], w_sem.at[2 * i]),
                pltpu.make_async_copy(ws_hbm.at[:, cols], w_scr.at[pl.ds(2 * HD, HP), cols], w_sem.at[2 * i + 1]),
            )
        )
    inputs[2].start()
    for pair in weights:
        for copy in pair:
            copy.start()
    for copy in inputs[:2]:
        copy.wait()

    attention.add(acc_scr)
    total = acc_scr[:, HD:]
    fine = (jnp.min(total) > 2.0**-60) & (jnp.max(total) < 2.0**110)

    @pl.when(jnp.logical_not(fine))
    def _():
        attention.fetch((0, 1), every=True)
        acc_scr[...] = jnp.zeros_like(acc_scr)
        m_scr[...] = jnp.full(m_scr.shape, LOW, jnp.float32)
        attention.add_shifted(acc_scr, m_scr)

    for g in range(2):
        rows = slice(g * ROWS, (g + 1) * ROWS)
        in_scr[:, g * HD : (g + 1) * HD] = (acc_scr[rows, :HD] / acc_scr[rows, HD:]).astype(jnp.bfloat16)
    inputs[2].wait()

    def out_copy(i):
        cols = pl.ds(i * COLS, COLS)
        return pltpu.make_async_copy(o_scr.at[:, cols], o_hbm.at[:, cols], o_sem.at[i])

    for i in range(DM // COLS):
        cols = slice(i * COLS, (i + 1) * COLS)
        for copy in weights[i]:
            copy.wait()
        o_scr[:, cols] = jnp.dot(in_scr[...], w_scr[:, cols], preferred_element_type=jnp.float32).astype(jnp.bfloat16)
        out_copy(i).start()
    for i in range(DM // COLS):
        out_copy(i).wait()


def big(limit=LIMIT):
    return pltpu.CompilerParams(vmem_limit_bytes=limit)


def moved(block, route0, route1):
    pairs = []
    for x in range(4):
        for y in range(4):
            for core, route in enumerate((route0, route1)):
                to = route(x, y)
                if to is not None:
                    pairs.append((x * 8 + y * 2 + core, to[0] * 8 + to[1] * 2 + core))
    return lax.ppermute(block, "pack", pairs)


def lines():
    columns = [[x * 8 + y * 2 for x in range(4)] for y in range(4)]
    rows = [[x * 8 + y * 2 + 1 for y in range(4)] for x in range(4)]
    return columns + rows


def along_x(distance):
    return lambda x, y: (x + distance, y) if x + distance < 4 else None


def along_y(distance):
    return lambda x, y: (x, (y + distance) % 4)


def swapped(block):
    return lax.ppermute(block, "pack", [(i, i ^ 1) for i in range(32)])


def call(kernel, shapes, ins, *args):
    return pl.pallas_call(
        kernel,
        out_shape=tuple(jax.ShapeDtypeStruct(shape, jnp.bfloat16) for shape in shapes),
        in_specs=[SMEM] + [VMEM] * ins,
        out_specs=(VMEM,) * len(shapes),
        compiler_params=big(),
        cost_estimate=pl.CostEstimate(flops=10**6, bytes_accessed=10**6, transcendentals=0),
    )(*args)


def local(
    queries,
    keys_values,
    ssm_values,
    ssm_gates,
    ssm_maps,
    step_size,
    decay_log,
    skip_gain,
    attn_out_weight,
    ssd_out_weight,
    lengths,
):
    first = jnp.reshape(lax.axis_index("pack") * ROWS, (1,)).astype(jnp.int32)
    kv = keys_values.reshape(ROWS, 2 * HD)
    nowhere = lambda x, y: None
    below = moved(kv, along_y(1), along_x(1))
    above = moved(kv, along_y(3), along_x(3))
    across = moved(kv, along_y(2), along_x(2))
    y_local, run_keep, run_send, fac = pl.pallas_call(
        ssd_kernel,
        out_shape=(
            jax.ShapeDtypeStruct((ROWS, HP), jnp.float32),
            jax.ShapeDtypeStruct((STATE_ROWS, HALF), jnp.bfloat16),
            jax.ShapeDtypeStruct((STATE_ROWS, HALF), jnp.bfloat16),
            jax.ShapeDtypeStruct((ROWS, HEADS), jnp.float32),
        ),
        in_specs=[SMEM] * 4 + [VMEM] * 3,
        out_specs=(VMEM, VMEM, VMEM, VMEM),
        compiler_params=big(62 * 2**20),
        cost_estimate=pl.CostEstimate(flops=10**9, bytes_accessed=4 * 10**6, transcendentals=10**6),
        name="ssd_local",
    )(lengths, decay_log, skip_gain, first, ssm_values, ssm_maps, step_size.T)

    below, above, across = lax.optimization_barrier((below, above, across, fac))[:3]
    line = jnp.concatenate([kv, below, above, across], axis=0)
    fetched = lax.all_gather(line, "pack", axis=0, tiled=True, axis_index_groups=lines())
    line_got = swapped(line)

    run = (STATE_ROWS, HALF)
    run_got = swapped(run_send)
    (chip,) = call(chip_kernel, [run], 2, first, run_keep, run_got)
    chips = [moved(chip, along_y(d), along_y(d)) for d in (1, 3, 2)]
    chunks_scratch = [
        pltpu.VMEM((SLOTS * CHUNK, 2 * HD), jnp.bfloat16),
        pltpu.SMEM((SLOTS,), jnp.int32),
        pltpu.SMEM((SLOTS,), jnp.int32),
        pltpu.SemaphoreType.DMA((SLOTS,)),
    ]
    sums = jax.ShapeDtypeStruct((2 * ROWS, 2 * HD), jnp.float32)
    split = jax.ShapeDtypeStruct((2 * ROWS, 2 * HD), jnp.bfloat16)

    def attend(kernel, name, shapes, vmem, *args, scratch=()):
        out = pl.pallas_call(
            kernel,
            out_shape=shapes,
            in_specs=[SMEM] * 2 + [VMEM] * vmem + [ANY] * (len(args) - vmem),
            out_specs=(VMEM,) * len(shapes),
            scratch_shapes=chunks_scratch + list(scratch),
            compiler_params=big(),
            cost_estimate=pl.CostEstimate(flops=3 * 10**9, bytes_accessed=5 * 10**6, transcendentals=5 * 10**6),
            name=name,
        )(lengths, first, *args)
        return out

    line = lax.optimization_barrier((line, chip))[0]
    acc, queries_split = attend(own_line_kernel, "own_line", (sums, split), 1, queries, line)
    chips = lax.optimization_barrier((*chips, acc))[:3]
    prefix, total = call(row_kernel, [run, run], 4, first, chip, *chips)
    rows = [moved(total, along_x(d), along_x(d)) for d in (3, 2, 1)]
    line_got = lax.optimization_barrier((line_got, prefix))[0]
    (acc,) = attend(other_line_kernel, "other_line", (sums,), 2, queries_split, acc, line_got)
    rows = lax.optimization_barrier((*rows, acc))[:3]
    keep, send = call(carry_kernel, [(SN, HALF)] * 2, 6, first, *rows, prefix, run_keep, run_got)
    got = swapped(send)
    act = pl.pallas_call(
        gate_kernel,
        out_shape=jax.ShapeDtypeStruct((ROWS, HP), jnp.bfloat16),
        grid=(2,),
        in_specs=[
            SMEM,
            pl.BlockSpec((ROWS // 2, HP), lambda i: (i, 0)),
            pl.BlockSpec((ROWS // 2, HP), lambda i: (i, 0)),
            pl.BlockSpec((ROWS // 2, SN), lambda i: (i, 1)),
            pl.BlockSpec((ROWS // 2, HEADS), lambda i: (i, 0)),
            pl.BlockSpec((SN, HALF), lambda i: (0, 0)),
            pl.BlockSpec((SN, HALF), lambda i: (0, 0)),
        ],
        out_specs=pl.BlockSpec((ROWS // 2, HP), lambda i: (i, 0)),
        compiler_params=big(),
        cost_estimate=pl.CostEstimate(flops=10**8, bytes_accessed=3 * 10**6, transcendentals=3 * 10**5),
        name="gate",
    )(first, y_local, ssm_gates, ssm_maps, fac, keep, got)

    fetched = lax.optimization_barrier((fetched, act))[0]
    other = swapped(fetched)
    (acc,) = attend(
        part_kernel,
        "part",
        (sums,),
        0,
        queries_split,
        acc,
        fetched,
        scratch=[pltpu.VMEM((2 * ROWS, 2 * HD), jnp.bfloat16), pltpu.SemaphoreType.DMA((2,))],
    )

    terms = pl.pallas_call(
        mix_kernel,
        out_shape=jax.ShapeDtypeStruct((ROWS, DM), jnp.bfloat16),
        in_specs=[SMEM] * 2 + [ANY] * 7,
        out_specs=ANY,
        scratch_shapes=chunks_scratch
        + [
            pltpu.VMEM((2 * ROWS, 2 * HD), jnp.bfloat16),
            pltpu.VMEM((2 * ROWS, 2 * HD), jnp.float32),
            pltpu.VMEM((2 * ROWS, HD), jnp.float32),
            pltpu.VMEM((2 * HD + HP, DM), jnp.bfloat16),
            pltpu.VMEM((ROWS, 2 * HD + HP), jnp.bfloat16),
            pltpu.VMEM((ROWS, DM), jnp.bfloat16),
            pltpu.SemaphoreType.DMA((3,)),
            pltpu.SemaphoreType.DMA((2 * (DM // COLS),)),
            pltpu.SemaphoreType.DMA((DM // COLS,)),
        ],
        compiler_params=big(),
        cost_estimate=pl.CostEstimate(flops=9 * 10**9, bytes_accessed=25 * 10**6, transcendentals=9 * 10**6),
        name="mix",
    )(lengths, first, queries_split, act, acc, fetched, other, attn_out_weight, ssd_out_weight)
    return lax.psum_scatter(terms, "tp", scatter_dimension=0, tiled=True)


def solution(mesh):
    return jax.shard_map(
        local,
        mesh=mesh,
        in_specs=(
            P("pack", "tp"),
            P("pack", "tp", None),
            P("pack", "tp"),
            P("pack", "tp"),
            P("pack", None),
            P("pack", "tp"),
            P("tp"),
            P("tp"),
            P("tp", None),
            P("tp", None),
            P(),
        ),
        out_specs=P(("pack", "tp"), None),
        check_vma=False,
    )
```

```python
import jax
import jax.numpy as jnp
from jax import lax
from jax.experimental import pallas as pl
from jax.experimental.pallas import tpu as pltpu
from jax.sharding import PartitionSpec as P

ROWS = 512
BLOCK = 256
HD = 128
HEADS = 8
HP = 512
SN = 256
DM = 5120
CHUNK = 512
SLOTS = 18
TILE = 256
COLS = 1024
LOW = -1e30
LOG2E = 1.4426950408889634
HIGH = lax.Precision.HIGHEST
LIMIT = 64 * 2**20 - 2**16
EARLY = 62 * 2**20
HALF = HP // 2
STATE_ROWS = SN + 16
VMEM = pl.BlockSpec(memory_space=pltpu.VMEM)
SMEM = pl.BlockSpec(memory_space=pltpu.SMEM)
ANY = pl.BlockSpec(memory_space=pl.ANY)


def iota(shape, dim):
    return lax.broadcasted_iota(jnp.int32, shape, dim)


def ends_of(len_ref):
    e0 = len_ref[0]
    e1 = e0 + len_ref[1]
    return e0, e1, e1 + len_ref[2]


def start_of(pos, ends):
    e0, e1, e2 = ends
    zero = jnp.zeros_like(pos)
    out = jnp.where(pos >= e0, zero + e0, zero)
    out = jnp.where(pos >= e1, zero + e1, out)
    return jnp.where(pos >= e2, zero + e2, out)


def spread():
    return (iota((HEADS, HP), 1) // (HP // HEADS) == iota((HEADS, HP), 0)).astype(jnp.float32)


def widen(a, expand):
    return jnp.dot(a, expand, precision=HIGH, preferred_element_type=jnp.float32)


def ssd_kernel(len_ref, dl_ref, skip_ref, first_ref, x_ref, maps_ref, step_ref, y_ref, keep_ref, send_ref, fac_ref):
    first = first_ref[0]
    ends = ends_of(len_ref)
    expand = spread()
    head_sub = iota((HEADS, 1), 0)
    wide_lane = iota((1, HP), 1) // (HP // HEADS)
    rate = jnp.zeros((HEADS, 1), jnp.float32)
    skip = jnp.zeros((1, HP), jnp.float32)
    for h in range(HEADS):
        rate = jnp.where(head_sub == h, dl_ref[h], rate)
        skip = jnp.where(wide_lane == h, skip_ref[h], skip)
    rate = -jnp.exp(rate)
    row = iota((BLOCK, 1), 0)
    col = iota((1, BLOCK), 1)
    tri = (row >= col).astype(jnp.float32)
    half = iota((1, 128), 1) < 64
    state = None
    before = None
    for n in range(ROWS // BLOCK):
        rows = slice(n * BLOCK, (n + 1) * BLOCK)
        base = first + n * BLOCK
        start_col = start_of(base + row, ends)
        last_start = start_of(base + (BLOCK - 1), ends)
        cum_t = lax.dot_general(
            rate * step_ref[:, rows], tri, (((1,), (1,)), ((), ())), precision=HIGH, preferred_element_type=jnp.float32
        )
        cum = cum_t.T
        write = maps_ref[rows, :SN]
        read = maps_ref[rows, SN:]
        prod = lax.dot_general(read, write, (((1,), (1,)), ((), ())), preferred_element_type=jnp.float32)
        allowed = (base + col >= start_col) & (col <= row)
        for pair in range(HEADS // 2):
            lanes = slice(pair * 128, (pair + 1) * 128)
            x = x_ref[rows, lanes]
            total = skip[:, lanes] * x.astype(jnp.float32)
            for which in range(2):
                h = pair * 2 + which
                gap = jnp.where(allowed, cum[:, h : h + 1] - cum_t[h : h + 1, :], LOW)
                weights = (jnp.exp(gap) * prod).astype(jnp.bfloat16)
                part = jnp.where(half if which == 0 else ~half, x, jnp.zeros_like(x))
                total = total + jnp.dot(weights, part, preferred_element_type=jnp.float32)
            y_ref[rows, lanes] = total
        ecum = jnp.exp(cum)
        if state is not None:
            local = widen(jnp.where(start_col < base, ecum, 0.0), expand)
            reads = jnp.dot(read, state.astype(jnp.bfloat16), preferred_element_type=jnp.float32)
            y_ref[rows, :] += reads * local
        carry = jnp.where(start_col < first, ecum, 0.0)
        if before is not None:
            carry = carry * before
        fac_ref[rows, :] = carry
        tail = jnp.exp(cum[BLOCK - 1 : BLOCK, :] - cum)
        tail = widen(jnp.where(base + row >= last_start, tail, 0.0), expand)
        weighted = (x_ref[rows, :].astype(jnp.float32) * tail).astype(jnp.bfloat16)
        new = lax.dot_general(write, weighted, (((0,), (0,)), ((), ())), preferred_element_type=jnp.float32)
        end = ecum[BLOCK - 8 :, :]
        if state is not None:
            keep = jnp.where(last_start < base, 1.0, 0.0)
            new = new + (keep * widen(end, expand)[7:8, :]) * state
            end = end * before
        state = new
        before = end[7:8, :]
    through = jnp.where(last_start < first, 1.0, 0.0) * widen(end, expand)[7:8, :]
    core = (first // ROWS) % 2
    left, right = slice(0, HALF), slice(HALF, HP)
    for ref, wanted in ((keep_ref, 0), (send_ref, 1)):
        store_run(
            ref,
            jnp.where(core == wanted, state[:, left], state[:, right]),
            jnp.where(core == wanted, through[:, left], through[:, right]),
        )


def store_run(ref, state, through):
    high = through.astype(jnp.bfloat16).astype(jnp.float32)
    low = through - high
    sub = iota((16, 1), 0)
    ref[:SN, :] = state.astype(jnp.bfloat16)
    ref[SN:, :] = jnp.where(sub == 0, high, jnp.where(sub == 1, low, 0.0)).astype(jnp.bfloat16)


def load_run(ref):
    tail = ref[SN:, :].astype(jnp.float32)
    return ref[:SN, :].astype(jnp.float32), tail[0:1, :] + tail[1:2, :]


def pick(cond, one, other):
    return jnp.where(cond, one[0], other[0]), jnp.where(cond, one[1], other[1])


def after(earlier, later):
    return later[0] + later[1] * earlier[0], earlier[1] * later[1]


def chip_kernel(first_ref, mine_ref, other_ref, out_ref, token_ref):
    core = (first_ref[0] // ROWS) % 2
    mine, other = load_run(mine_ref), load_run(other_ref)
    store_run(out_ref, *after(pick(core == 0, mine, other), pick(core == 0, other, mine)))
    token_ref[...] = jnp.zeros_like(token_ref)


def row_kernel(first_ref, mine_ref, below_ref, above_ref, across_ref, prefix_ref, total_ref):
    y = (first_ref[0] // (2 * ROWS)) % 4
    by_distance = [load_run(ref) for ref in (mine_ref, below_ref, across_ref, above_ref)]
    run = (jnp.zeros((SN, HALF), jnp.float32), jnp.ones((1, HALF), jnp.float32))
    prefix = run
    for place in range(4):
        distance = (y - place) % 4
        piece = by_distance[0]
        for d in range(1, 4):
            piece = pick(distance == d, by_distance[d], piece)
        prefix = pick(y == place, run, prefix)
        run = after(run, piece)
    store_run(prefix_ref, *prefix)
    store_run(total_ref, *run)


def carry_kernel(first_ref, row3_ref, row2_ref, row1_ref, prefix_ref, mine_ref, other_ref, keep_ref, send_ref):
    core = (first_ref[0] // ROWS) % 2
    run = load_run(row3_ref)
    for ref in (row2_ref, row1_ref, prefix_ref):
        run = after(run, load_run(ref))
    behind = after(run, pick(core == 0, load_run(mine_ref), load_run(other_ref)))
    keep_ref[...] = jnp.where(core == 0, run[0], behind[0]).astype(jnp.bfloat16)
    send_ref[...] = jnp.where(core == 0, behind[0], run[0]).astype(jnp.bfloat16)


def gate_kernel(first_ref, y_ref, z_ref, read_ref, fac_ref, keep_ref, got_ref, act_ref):
    core = (first_ref[0] // ROWS) % 2
    keep, got = keep_ref[...], got_ref[...]
    state = jnp.concatenate([jnp.where(core == 0, keep, got), jnp.where(core == 0, got, keep)], axis=1)
    reads = jnp.dot(read_ref[...], state, preferred_element_type=jnp.float32)
    y = y_ref[...] + reads * widen(fac_ref[...], spread())
    z = z_ref[...].astype(jnp.float32)
    act_ref[...] = (y * (z / (1.0 + jnp.exp(-z)))).astype(jnp.bfloat16)


class Attention:
    def __init__(self, len_ref, first_ref, fetched, other, q_scr, kv_scr, ids, kinds, kv_sem, near_only=False):
        self.first = first_ref[0]
        self.ends = ends_of(len_ref)
        self.mine = self.first // CHUNK
        self.low = start_of(self.first, self.ends) // CHUNK
        self.last_start = start_of(self.first + ROWS - 1, self.ends)
        self.arrays = (fetched, other)
        self.near_only = near_only
        self.q_scr, self.kv_scr, self.ids, self.kinds, self.kv_sem = q_scr, kv_scr, ids, kinds, kv_sem

    def count(self, far):
        return 4 if self.near_only else (self.mine - far - self.low) // 2 + 1

    def block(self, far, i):
        if not self.near_only:
            return self.mine - far - 2 * i
        core = self.mine % 2
        step = jnp.where(core == far, 2, 8)
        return self.mine + jnp.where(core == 0, far, -far) - step * i

    def in_line(self, block):
        row = block // 8 == self.mine // 8
        column = (block // 2) % 4 == (self.mine // 2) % 4
        return jnp.where(block % 2 == 0, row, column)

    def place(self, block):
        x, y, even = block // 8, (block // 2) % 4, block % 2 == 0
        my_x, my_y = self.mine // 8, (self.mine // 2) % 4
        distance = jnp.where(even, (my_y - y) % 4, (my_x - x) % 4)
        place = distance ^ (distance >> 1)
        if not self.near_only:
            place = place + 4 * jnp.where(even, x, y)
        return place

    def copy(self, far, place, slot):
        rows = pl.ds(pl.multiple_of(place * CHUNK, CHUNK), CHUNK)
        to = pl.ds(pl.multiple_of(slot * CHUNK, CHUNK), CHUNK)
        return pltpu.make_async_copy(self.arrays[far].at[rows], self.kv_scr.at[to], self.kv_sem.at[slot])

    def fetch(self, fars, every=False):
        def one_chunk(far, i, carry):
            plain, masked = carry
            block = self.block(far, i)
            if self.near_only:
                wanted = (block >= self.low) & (block <= self.mine) & self.in_line(block)
            elif every:
                wanted = block >= self.low
            else:
                wanted = jnp.logical_not(self.in_line(block))
            mask = (block == self.mine) | (block * CHUNK < self.last_start)
            slot = jnp.where(mask, SLOTS - 1 - masked, plain)

            @pl.when(wanted)
            def _():
                self.ids[slot] = block
                inside = start_of(block * CHUNK + (CHUNK - 1), self.ends) > block * CHUNK
                self.kinds[slot] = jnp.where((block == self.mine) | inside, 1, 0)
                self.copy(far, self.place(block), slot).start()

            new = wanted.astype(jnp.int32)
            return plain + jnp.where(mask, 0, new), masked + jnp.where(mask, new, 0)

        carry = (jnp.int32(0), jnp.int32(0))
        for far in fars:
            carry = lax.fori_loop(0, self.count(far), lambda i, c, far=far: one_chunk(far, i, c), carry)
        self.plain, self.masked = carry

    def wait(self, slot):
        self.copy(0, 0, slot).wait()

    def keys(self, slot, chunks):
        return pl.ds(pl.multiple_of(slot * CHUNK, CHUNK), chunks * CHUNK)

    def scores(self, slot, chunks, r, masked):
        rows = slice(r * TILE, (r + 1) * TILE)
        k = self.kv_scr[self.keys(slot, chunks), :HD]
        s = lax.dot_general(
            self.q_scr[rows, :],
            jnp.concatenate([k, k], axis=1),
            (((1,), (1,)), ((), ())),
            preferred_element_type=jnp.float32,
        )
        if masked:
            pos = self.first + rows.start % ROWS + iota((TILE, 1), 0)
            key = self.ids[slot] * CHUNK + iota((1, CHUNK), 1)
            s = jnp.where((key >= start_of(pos, self.ends)) & (key <= pos), s, LOW)
        return s

    def values(self, slot, chunks):
        v = self.kv_scr[self.keys(slot, chunks), HD:]
        return jnp.concatenate([v, jnp.ones((chunks * CHUNK, HD), jnp.bfloat16)], axis=1)

    def step(self, acc, slot, chunks, masked, by_row=False):
        v = self.values(slot, chunks)
        tiles = 2 * ROWS // TILE
        s = self.scores(slot, chunks, 0, masked)
        for r in range(tiles):
            following = self.scores(slot, chunks, r + 1, masked) if r + 1 < tiles else None
            p = jnp.exp2(s).astype(jnp.bfloat16)
            out = jnp.dot(p, v, preferred_element_type=jnp.float32)
            if by_row:
                pos = self.first + (r * TILE) % ROWS + iota((TILE, 1), 0)
                out = jnp.where(start_of(pos, self.ends) <= self.ids[slot] * CHUNK, out, 0.0)
            acc[r * TILE : (r + 1) * TILE, :] += out
            s = following

    def add(self, acc):
        def one_masked(j, _):
            slot = SLOTS - 1 - j
            self.wait(slot)
            pl.when(self.kinds[slot] == 0)(lambda: self.step(acc, slot, 1, False, by_row=True))
            pl.when(self.kinds[slot] == 1)(lambda: self.step(acc, slot, 1, True))
            return 0

        def two_plain(j, _):
            self.wait(2 * j)
            self.wait(2 * j + 1)
            self.step(acc, 2 * j, 2, False)
            return 0

        lax.fori_loop(0, self.masked, one_masked, 0)
        lax.fori_loop(0, self.plain // 2, two_plain, 0)

        @pl.when(self.plain % 2 == 1)
        def _():
            self.wait(self.plain - 1)
            self.step(acc, self.plain - 1, 1, False)

    def add_shifted(self, acc, m_scr):
        def one_chunk(j, _):
            slot = jnp.where(j < self.plain, j, SLOTS - 1 - (j - self.plain))
            self.wait(slot)
            v = self.values(slot, 1)
            for r in range(2 * ROWS // TILE):
                rows = slice(r * TILE, (r + 1) * TILE)
                s = self.scores(slot, 1, r, True)
                old = m_scr[rows, :]
                m = jnp.maximum(old, jnp.max(s, axis=1, keepdims=True))
                alpha = jnp.exp2(old - m)
                p = jnp.exp2(s - jnp.concatenate([m] * (CHUNK // 128), axis=1)).astype(jnp.bfloat16)
                out = jnp.dot(p, v, preferred_element_type=jnp.float32)
                acc[rows, :] = acc[rows, :] * jnp.concatenate([alpha, alpha], axis=1) + out
                m_scr[rows, :] = m
            return 0

        lax.fori_loop(0, self.plain + self.masked, one_chunk, 0)


def own_line_kernel(len_ref, first_ref, q_ref, line, _, acc_ref, split_ref, kv_scr, ids, kinds, kv_sem):
    attention = Attention(len_ref, first_ref, line, None, split_ref, kv_scr, ids, kinds, kv_sem, near_only=True)
    attention.fetch((0,))
    for g in range(2):
        rows = slice(g * ROWS, (g + 1) * ROWS)
        scaled = q_ref[:, g * HD : (g + 1) * HD].astype(jnp.float32) * (LOG2E * HD**-0.5)
        high = scaled.astype(jnp.bfloat16)
        split_ref[rows, :HD] = high
        split_ref[rows, HD:] = (scaled - high.astype(jnp.float32)).astype(jnp.bfloat16)
    acc_ref[...] = jnp.zeros_like(acc_ref)
    attention.add(acc_ref)


def other_line_kernel(len_ref, first_ref, split_ref, before_ref, line_got, acc_ref, kv_scr, ids, kinds, kv_sem):
    attention = Attention(len_ref, first_ref, line_got, line_got, split_ref, kv_scr, ids, kinds, kv_sem, near_only=True)
    attention.fetch((1,))
    acc_ref[...] = before_ref[...]
    attention.add(acc_ref)


def part_kernel(
    len_ref, first_ref, split_hbm, before_hbm, fetched, acc_ref, kv_scr, ids, kinds, kv_sem, q_scr, in_sem
):
    attention = Attention(len_ref, first_ref, fetched, None, q_scr, kv_scr, ids, kinds, kv_sem)
    inputs = [
        pltpu.make_async_copy(split_hbm, q_scr, in_sem.at[0]),
        pltpu.make_async_copy(before_hbm, acc_ref, in_sem.at[1]),
    ]
    for copy in inputs:
        copy.start()
    attention.fetch((0,))
    for copy in inputs:
        copy.wait()
    attention.add(acc_ref)


def mix_kernel(
    len_ref,
    first_ref,
    split_hbm,
    act_hbm,
    before_hbm,
    fetched,
    other,
    wa_hbm,
    ws_hbm,
    o_hbm,
    kv_scr,
    ids,
    kinds,
    kv_sem,
    q_scr,
    acc_scr,
    m_scr,
    w_scr,
    in_scr,
    o_scr,
    in_sem,
    w_sem,
    o_sem,
):
    attention = Attention(len_ref, first_ref, fetched, other, q_scr, kv_scr, ids, kinds, kv_sem)
    inputs = [
        pltpu.make_async_copy(split_hbm, q_scr, in_sem.at[0]),
        pltpu.make_async_copy(before_hbm, acc_scr, in_sem.at[1]),
        pltpu.make_async_copy(act_hbm, in_scr.at[:, pl.ds(2 * HD, HP)], in_sem.at[2]),
    ]
    for copy in inputs[:2]:
        copy.start()
    attention.fetch((1,))
    weights = []
    for i in range(DM // COLS):
        cols = pl.ds(i * COLS, COLS)
        weights.append(
            (
                pltpu.make_async_copy(wa_hbm.at[:, cols], w_scr.at[pl.ds(0, 2 * HD), cols], w_sem.at[2 * i]),
                pltpu.make_async_copy(ws_hbm.at[:, cols], w_scr.at[pl.ds(2 * HD, HP), cols], w_sem.at[2 * i + 1]),
            )
        )
    inputs[2].start()
    for pair in weights:
        for copy in pair:
            copy.start()
    for copy in inputs[:2]:
        copy.wait()

    attention.add(acc_scr)
    total = acc_scr[:, HD:]
    fine = (jnp.min(total) > 2.0**-60) & (jnp.max(total) < 2.0**110)

    @pl.when(jnp.logical_not(fine))
    def _():
        attention.fetch((0, 1), every=True)
        acc_scr[...] = jnp.zeros_like(acc_scr)
        m_scr[...] = jnp.full(m_scr.shape, LOW, jnp.float32)
        attention.add_shifted(acc_scr, m_scr)

    for g in range(2):
        rows = slice(g * ROWS, (g + 1) * ROWS)
        in_scr[:, g * HD : (g + 1) * HD] = (acc_scr[rows, :HD] / acc_scr[rows, HD:]).astype(jnp.bfloat16)
    inputs[2].wait()

    def out_copy(i):
        cols = pl.ds(i * COLS, COLS)
        return pltpu.make_async_copy(o_scr.at[:, cols], o_hbm.at[:, cols], o_sem.at[i])

    for i in range(DM // COLS):
        cols = slice(i * COLS, (i + 1) * COLS)
        for copy in weights[i]:
            copy.wait()
        o_scr[:, cols] = jnp.dot(in_scr[...], w_scr[:, cols], preferred_element_type=jnp.float32).astype(jnp.bfloat16)
        out_copy(i).start()
    for i in range(DM // COLS):
        out_copy(i).wait()


def big(limit=LIMIT):
    return pltpu.CompilerParams(vmem_limit_bytes=limit)


def moved(block, route0, route1):
    pairs = []
    for x in range(4):
        for y in range(4):
            for core, route in enumerate((route0, route1)):
                to = route(x, y)
                if to is not None:
                    pairs.append((x * 8 + y * 2 + core, to[0] * 8 + to[1] * 2 + core))
    return lax.ppermute(block, "pack", pairs)


def lines():
    columns = [[x * 8 + y * 2 for x in range(4)] for y in range(4)]
    rows = [[x * 8 + y * 2 + 1 for y in range(4)] for x in range(4)]
    return columns + rows


def along_x(distance):
    return lambda x, y: (x + distance, y) if x + distance < 4 else None


def along_y(distance):
    return lambda x, y: (x, (y + distance) % 4)


def swapped(block):
    return lax.ppermute(block, "pack", [(i, i ^ 1) for i in range(32)])


def call(kernel, shapes, ins, *args, limit=LIMIT):
    return pl.pallas_call(
        kernel,
        out_shape=tuple(jax.ShapeDtypeStruct(shape, jnp.bfloat16) for shape in shapes),
        in_specs=[SMEM] + [VMEM] * ins,
        out_specs=(VMEM,) * len(shapes),
        compiler_params=big(limit),
        cost_estimate=pl.CostEstimate(flops=10**6, bytes_accessed=10**6, transcendentals=0),
    )(*args)


def local(
    queries,
    keys_values,
    ssm_values,
    ssm_gates,
    ssm_maps,
    step_size,
    decay_log,
    skip_gain,
    attn_out_weight,
    ssd_out_weight,
    lengths,
):
    first = jnp.reshape(lax.axis_index("pack") * ROWS, (1,)).astype(jnp.int32)
    kv = keys_values.reshape(ROWS, 2 * HD)
    nowhere = lambda x, y: None
    below = moved(kv, along_y(1), along_x(1))
    above = moved(kv, along_y(3), along_x(3))
    across = moved(kv, along_y(2), along_x(2))
    y_local, run_keep, run_send, fac = pl.pallas_call(
        ssd_kernel,
        out_shape=(
            jax.ShapeDtypeStruct((ROWS, HP), jnp.float32),
            jax.ShapeDtypeStruct((STATE_ROWS, HALF), jnp.bfloat16),
            jax.ShapeDtypeStruct((STATE_ROWS, HALF), jnp.bfloat16),
            jax.ShapeDtypeStruct((ROWS, HEADS), jnp.float32),
        ),
        in_specs=[SMEM] * 4 + [VMEM] * 3,
        out_specs=(VMEM, VMEM, VMEM, VMEM),
        compiler_params=big(EARLY),
        cost_estimate=pl.CostEstimate(flops=10**9, bytes_accessed=4 * 10**6, transcendentals=10**6),
        name="ssd_local",
    )(lengths, decay_log, skip_gain, first, ssm_values, ssm_maps, step_size.T)

    run = (STATE_ROWS, HALF)
    run_got = swapped(run_send)
    chip, token = call(chip_kernel, [run, (16, 128)], 2, first, run_keep, run_got, limit=EARLY)

    below, above, across, token = lax.optimization_barrier((below, above, across, token))
    line = jnp.concatenate([kv, below, above, across], axis=0)
    fetched = lax.all_gather(line, "pack", axis=0, tiled=True, axis_index_groups=lines())
    line_got = swapped(line)
    chips = [moved(chip, along_y(d), along_y(d)) for d in (1, 3, 2)]
    chunks_scratch = [
        pltpu.VMEM((SLOTS * CHUNK, 2 * HD), jnp.bfloat16),
        pltpu.SMEM((SLOTS,), jnp.int32),
        pltpu.SMEM((SLOTS,), jnp.int32),
        pltpu.SemaphoreType.DMA((SLOTS,)),
    ]
    sums = jax.ShapeDtypeStruct((2 * ROWS, 2 * HD), jnp.float32)
    split = jax.ShapeDtypeStruct((2 * ROWS, 2 * HD), jnp.bfloat16)

    def attend(kernel, name, shapes, vmem, *args, scratch=()):
        out = pl.pallas_call(
            kernel,
            out_shape=shapes,
            in_specs=[SMEM] * 2 + [VMEM] * vmem + [ANY] * (len(args) - vmem),
            out_specs=(VMEM,) * len(shapes),
            scratch_shapes=chunks_scratch + list(scratch),
            compiler_params=big(),
            cost_estimate=pl.CostEstimate(flops=3 * 10**9, bytes_accessed=5 * 10**6, transcendentals=5 * 10**6),
            name=name,
        )(lengths, first, *args)
        return out

    acc, queries_split = attend(own_line_kernel, "own_line", (sums, split), 1, queries, line, token)
    chips = lax.optimization_barrier((*chips, acc))[:3]
    prefix, total = call(row_kernel, [run, run], 4, first, chip, *chips)
    rows = [moved(total, along_x(d), along_x(d)) for d in (3, 2, 1)]
    line_got = lax.optimization_barrier((line_got, prefix))[0]
    (acc,) = attend(other_line_kernel, "other_line", (sums,), 2, queries_split, acc, line_got)
    rows = lax.optimization_barrier((*rows, acc))[:3]
    keep, send = call(carry_kernel, [(SN, HALF)] * 2, 6, first, *rows, prefix, run_keep, run_got)
    got = swapped(send)
    act = pl.pallas_call(
        gate_kernel,
        out_shape=jax.ShapeDtypeStruct((ROWS, HP), jnp.bfloat16),
        grid=(2,),
        in_specs=[
            SMEM,
            pl.BlockSpec((ROWS // 2, HP), lambda i: (i, 0)),
            pl.BlockSpec((ROWS // 2, HP), lambda i: (i, 0)),
            pl.BlockSpec((ROWS // 2, SN), lambda i: (i, 1)),
            pl.BlockSpec((ROWS // 2, HEADS), lambda i: (i, 0)),
            pl.BlockSpec((SN, HALF), lambda i: (0, 0)),
            pl.BlockSpec((SN, HALF), lambda i: (0, 0)),
        ],
        out_specs=pl.BlockSpec((ROWS // 2, HP), lambda i: (i, 0)),
        compiler_params=big(),
        cost_estimate=pl.CostEstimate(flops=10**8, bytes_accessed=3 * 10**6, transcendentals=3 * 10**5),
        name="gate",
    )(first, y_local, ssm_gates, ssm_maps, fac, keep, got)

    fetched = lax.optimization_barrier((fetched, act))[0]
    other = swapped(fetched)
    (acc,) = attend(
        part_kernel,
        "part",
        (sums,),
        0,
        queries_split,
        acc,
        fetched,
        scratch=[pltpu.VMEM((2 * ROWS, 2 * HD), jnp.bfloat16), pltpu.SemaphoreType.DMA((2,))],
    )

    terms = pl.pallas_call(
        mix_kernel,
        out_shape=jax.ShapeDtypeStruct((ROWS, DM), jnp.bfloat16),
        in_specs=[SMEM] * 2 + [ANY] * 7,
        out_specs=ANY,
        scratch_shapes=chunks_scratch
        + [
            pltpu.VMEM((2 * ROWS, 2 * HD), jnp.bfloat16),
            pltpu.VMEM((2 * ROWS, 2 * HD), jnp.float32),
            pltpu.VMEM((2 * ROWS, HD), jnp.float32),
            pltpu.VMEM((2 * HD + HP, DM), jnp.bfloat16),
            pltpu.VMEM((ROWS, 2 * HD + HP), jnp.bfloat16),
            pltpu.VMEM((ROWS, DM), jnp.bfloat16),
            pltpu.SemaphoreType.DMA((3,)),
            pltpu.SemaphoreType.DMA((2 * (DM // COLS),)),
            pltpu.SemaphoreType.DMA((DM // COLS,)),
        ],
        compiler_params=big(),
        cost_estimate=pl.CostEstimate(flops=9 * 10**9, bytes_accessed=25 * 10**6, transcendentals=9 * 10**6),
        name="mix",
    )(lengths, first, queries_split, act, acc, fetched, other, attn_out_weight, ssd_out_weight)
    return lax.psum_scatter(terms, "tp", scatter_dimension=0, tiled=True)


def solution(mesh):
    return jax.shard_map(
        local,
        mesh=mesh,
        in_specs=(
            P("pack", "tp"),
            P("pack", "tp", None),
            P("pack", "tp"),
            P("pack", "tp"),
            P("pack", None),
            P("pack", "tp"),
            P("tp"),
            P("tp"),
            P("tp", None),
            P("tp", None),
            P(),
        ),
        out_specs=P(("pack", "tp"), None),
        check_vma=False,
    )
```

```python
import jax
import jax.numpy as jnp
from jax import lax
from jax.experimental import pallas as pl
from jax.experimental.pallas import tpu as pltpu
from jax.sharding import PartitionSpec as P

ROWS = 512
BLOCK = 256
HD = 128
HEADS = 8
HP = 512
SN = 256
DM = 5120
CHUNK = 512
SLOTS = 18
TILE = 256
COLS = 1024
LOW = -1e30
LOG2E = 1.4426950408889634
HIGH = lax.Precision.HIGHEST
LIMIT = 64 * 2**20 - 2**16
HALF = HP // 2
STATE_ROWS = SN + 16
VMEM = pl.BlockSpec(memory_space=pltpu.VMEM)
SMEM = pl.BlockSpec(memory_space=pltpu.SMEM)
ANY = pl.BlockSpec(memory_space=pl.ANY)


def iota(shape, dim):
    return lax.broadcasted_iota(jnp.int32, shape, dim)


def ends_of(len_ref):
    e0 = len_ref[0]
    e1 = e0 + len_ref[1]
    return e0, e1, e1 + len_ref[2]


def start_of(pos, ends):
    e0, e1, e2 = ends
    zero = jnp.zeros_like(pos)
    out = jnp.where(pos >= e0, zero + e0, zero)
    out = jnp.where(pos >= e1, zero + e1, out)
    return jnp.where(pos >= e2, zero + e2, out)


def spread():
    return (iota((HEADS, HP), 1) // (HP // HEADS) == iota((HEADS, HP), 0)).astype(jnp.float32)


def widen(a, expand):
    return jnp.dot(a, expand, precision=HIGH, preferred_element_type=jnp.float32)


def ssd_kernel(len_ref, dl_ref, skip_ref, first_ref, x_ref, maps_ref, step_ref, y_ref, keep_ref, send_ref, fac_ref):
    first = first_ref[0]
    ends = ends_of(len_ref)
    expand = spread()
    head_sub = iota((HEADS, 1), 0)
    wide_lane = iota((1, HP), 1) // (HP // HEADS)
    rate = jnp.zeros((HEADS, 1), jnp.float32)
    skip = jnp.zeros((1, HP), jnp.float32)
    for h in range(HEADS):
        rate = jnp.where(head_sub == h, dl_ref[h], rate)
        skip = jnp.where(wide_lane == h, skip_ref[h], skip)
    rate = -jnp.exp(rate)
    row = iota((BLOCK, 1), 0)
    col = iota((1, BLOCK), 1)
    tri = (row >= col).astype(jnp.float32)
    half = iota((1, 128), 1) < 64
    state = None
    before = None
    for n in range(ROWS // BLOCK):
        rows = slice(n * BLOCK, (n + 1) * BLOCK)
        base = first + n * BLOCK
        start_col = start_of(base + row, ends)
        last_start = start_of(base + (BLOCK - 1), ends)
        cum_t = lax.dot_general(
            rate * step_ref[:, rows], tri, (((1,), (1,)), ((), ())), precision=HIGH, preferred_element_type=jnp.float32
        )
        cum = cum_t.T
        write = maps_ref[rows, :SN]
        read = maps_ref[rows, SN:]
        prod = lax.dot_general(read, write, (((1,), (1,)), ((), ())), preferred_element_type=jnp.float32)
        allowed = (base + col >= start_col) & (col <= row)
        for pair in range(HEADS // 2):
            lanes = slice(pair * 128, (pair + 1) * 128)
            x = x_ref[rows, lanes]
            total = skip[:, lanes] * x.astype(jnp.float32)
            for which in range(2):
                h = pair * 2 + which
                gap = jnp.where(allowed, cum[:, h : h + 1] - cum_t[h : h + 1, :], LOW)
                weights = (jnp.exp(gap) * prod).astype(jnp.bfloat16)
                part = jnp.where(half if which == 0 else ~half, x, jnp.zeros_like(x))
                total = total + jnp.dot(weights, part, preferred_element_type=jnp.float32)
            y_ref[rows, lanes] = total
        ecum = jnp.exp(cum)
        if state is not None:
            local = widen(jnp.where(start_col < base, ecum, 0.0), expand)
            reads = jnp.dot(read, state.astype(jnp.bfloat16), preferred_element_type=jnp.float32)
            y_ref[rows, :] += reads * local
        carry = jnp.where(start_col < first, ecum, 0.0)
        if before is not None:
            carry = carry * before
        fac_ref[rows, :] = carry
        tail = jnp.exp(cum[BLOCK - 1 : BLOCK, :] - cum)
        tail = widen(jnp.where(base + row >= last_start, tail, 0.0), expand)
        weighted = (x_ref[rows, :].astype(jnp.float32) * tail).astype(jnp.bfloat16)
        new = lax.dot_general(write, weighted, (((0,), (0,)), ((), ())), preferred_element_type=jnp.float32)
        end = ecum[BLOCK - 8 :, :]
        if state is not None:
            keep = jnp.where(last_start < base, 1.0, 0.0)
            new = new + (keep * widen(end, expand)[7:8, :]) * state
            end = end * before
        state = new
        before = end[7:8, :]
    through = jnp.where(last_start < first, 1.0, 0.0) * widen(end, expand)[7:8, :]
    core = (first // ROWS) % 2
    left, right = slice(0, HALF), slice(HALF, HP)
    for ref, wanted in ((keep_ref, 0), (send_ref, 1)):
        store_run(
            ref,
            jnp.where(core == wanted, state[:, left], state[:, right]),
            jnp.where(core == wanted, through[:, left], through[:, right]),
        )


def store_run(ref, state, through):
    high = through.astype(jnp.bfloat16).astype(jnp.float32)
    low = through - high
    sub = iota((16, 1), 0)
    ref[:SN, :] = state.astype(jnp.bfloat16)
    ref[SN:, :] = jnp.where(sub == 0, high, jnp.where(sub == 1, low, 0.0)).astype(jnp.bfloat16)


def load_run(ref):
    tail = ref[SN:, :].astype(jnp.float32)
    return ref[:SN, :].astype(jnp.float32), tail[0:1, :] + tail[1:2, :]


def pick(cond, one, other):
    return jnp.where(cond, one[0], other[0]), jnp.where(cond, one[1], other[1])


def after(earlier, later):
    return later[0] + later[1] * earlier[0], earlier[1] * later[1]


def chip_kernel(first_ref, mine_ref, other_ref, out_ref):
    core = (first_ref[0] // ROWS) % 2
    mine, other = load_run(mine_ref), load_run(other_ref)
    store_run(out_ref, *after(pick(core == 0, mine, other), pick(core == 0, other, mine)))


def row_kernel(first_ref, mine_ref, below_ref, above_ref, across_ref, prefix_ref, total_ref):
    y = (first_ref[0] // (2 * ROWS)) % 4
    by_distance = [load_run(ref) for ref in (mine_ref, below_ref, across_ref, above_ref)]
    run = (jnp.zeros((SN, HALF), jnp.float32), jnp.ones((1, HALF), jnp.float32))
    prefix = run
    for place in range(4):
        distance = (y - place) % 4
        piece = by_distance[0]
        for d in range(1, 4):
            piece = pick(distance == d, by_distance[d], piece)
        prefix = pick(y == place, run, prefix)
        run = after(run, piece)
    store_run(prefix_ref, *prefix)
    store_run(total_ref, *run)


def carry_kernel(first_ref, row3_ref, row2_ref, row1_ref, prefix_ref, mine_ref, other_ref, keep_ref, send_ref):
    core = (first_ref[0] // ROWS) % 2
    run = load_run(row3_ref)
    for ref in (row2_ref, row1_ref, prefix_ref):
        run = after(run, load_run(ref))
    behind = after(run, pick(core == 0, load_run(mine_ref), load_run(other_ref)))
    keep_ref[...] = jnp.where(core == 0, run[0], behind[0]).astype(jnp.bfloat16)
    send_ref[...] = jnp.where(core == 0, behind[0], run[0]).astype(jnp.bfloat16)


def gate_kernel(first_ref, y_ref, z_ref, read_ref, fac_ref, keep_ref, got_ref, act_ref):
    core = (first_ref[0] // ROWS) % 2
    keep, got = keep_ref[...], got_ref[...]
    state = jnp.concatenate([jnp.where(core == 0, keep, got), jnp.where(core == 0, got, keep)], axis=1)
    reads = jnp.dot(read_ref[...], state, preferred_element_type=jnp.float32)
    y = y_ref[...] + reads * widen(fac_ref[...], spread())
    z = z_ref[...].astype(jnp.float32)
    act_ref[...] = (y * (z / (1.0 + jnp.exp(-z)))).astype(jnp.bfloat16)


class Attention:
    def __init__(self, len_ref, first_ref, fetched, other, q_scr, kv_scr, ids, kinds, kv_sem, near_only=False):
        self.first = first_ref[0]
        self.ends = ends_of(len_ref)
        self.mine = self.first // CHUNK
        self.low = start_of(self.first, self.ends) // CHUNK
        self.last_start = start_of(self.first + ROWS - 1, self.ends)
        self.arrays = (fetched, other)
        self.near_only = near_only
        self.q_scr, self.kv_scr, self.ids, self.kinds, self.kv_sem = q_scr, kv_scr, ids, kinds, kv_sem

    def count(self, far):
        return 4 if self.near_only else (self.mine - far - self.low) // 2 + 1

    def block(self, far, i):
        if not self.near_only:
            return self.mine - far - 2 * i
        core = self.mine % 2
        step = jnp.where(core == far, 2, 8)
        return self.mine + jnp.where(core == 0, far, -far) - step * i

    def in_line(self, block):
        row = block // 8 == self.mine // 8
        column = (block // 2) % 4 == (self.mine // 2) % 4
        return jnp.where(block % 2 == 0, row, column)

    def place(self, block):
        x, y, even = block // 8, (block // 2) % 4, block % 2 == 0
        my_x, my_y = self.mine // 8, (self.mine // 2) % 4
        distance = jnp.where(even, (my_y - y) % 4, (my_x - x) % 4)
        place = distance ^ (distance >> 1)
        if not self.near_only:
            place = place + 4 * jnp.where(even, x, y)
        return place

    def copy(self, far, place, slot):
        rows = pl.ds(pl.multiple_of(place * CHUNK, CHUNK), CHUNK)
        to = pl.ds(pl.multiple_of(slot * CHUNK, CHUNK), CHUNK)
        return pltpu.make_async_copy(self.arrays[far].at[rows], self.kv_scr.at[to], self.kv_sem.at[slot])

    def fetch(self, fars, every=False):
        def one_chunk(far, i, carry):
            plain, masked = carry
            block = self.block(far, i)
            if self.near_only:
                wanted = (block >= self.low) & (block <= self.mine) & self.in_line(block)
            elif every:
                wanted = block >= self.low
            else:
                wanted = jnp.logical_not(self.in_line(block))
            mask = (block == self.mine) | (block * CHUNK < self.last_start)
            slot = jnp.where(mask, SLOTS - 1 - masked, plain)

            @pl.when(wanted)
            def _():
                self.ids[slot] = block
                inside = start_of(block * CHUNK + (CHUNK - 1), self.ends) > block * CHUNK
                self.kinds[slot] = jnp.where((block == self.mine) | inside, 1, 0)
                self.copy(far, self.place(block), slot).start()

            new = wanted.astype(jnp.int32)
            return plain + jnp.where(mask, 0, new), masked + jnp.where(mask, new, 0)

        carry = (jnp.int32(0), jnp.int32(0))
        for far in fars:
            carry = lax.fori_loop(0, self.count(far), lambda i, c, far=far: one_chunk(far, i, c), carry)
        self.plain, self.masked = carry

    def wait(self, slot):
        self.copy(0, 0, slot).wait()

    def keys(self, slot, chunks):
        return pl.ds(pl.multiple_of(slot * CHUNK, CHUNK), chunks * CHUNK)

    def scores(self, slot, chunks, r, masked):
        rows = slice(r * TILE, (r + 1) * TILE)
        k = self.kv_scr[self.keys(slot, chunks), :HD]
        s = lax.dot_general(
            self.q_scr[rows, :],
            jnp.concatenate([k, k], axis=1),
            (((1,), (1,)), ((), ())),
            preferred_element_type=jnp.float32,
        )
        if masked:
            pos = self.first + rows.start % ROWS + iota((TILE, 1), 0)
            key = self.ids[slot] * CHUNK + iota((1, CHUNK), 1)
            s = jnp.where((key >= start_of(pos, self.ends)) & (key <= pos), s, LOW)
        return s

    def values(self, slot, chunks):
        v = self.kv_scr[self.keys(slot, chunks), HD:]
        return jnp.concatenate([v, jnp.ones((chunks * CHUNK, HD), jnp.bfloat16)], axis=1)

    def step(self, acc, slot, chunks, masked, by_row=False):
        v = self.values(slot, chunks)
        tiles = 2 * ROWS // TILE
        s = self.scores(slot, chunks, 0, masked)
        for r in range(tiles):
            following = self.scores(slot, chunks, r + 1, masked) if r + 1 < tiles else None
            p = jnp.exp2(s).astype(jnp.bfloat16)
            out = jnp.dot(p, v, preferred_element_type=jnp.float32)
            if by_row:
                pos = self.first + (r * TILE) % ROWS + iota((TILE, 1), 0)
                out = jnp.where(start_of(pos, self.ends) <= self.ids[slot] * CHUNK, out, 0.0)
            acc[r * TILE : (r + 1) * TILE, :] += out
            s = following

    def add(self, acc):
        def one_masked(j, _):
            slot = SLOTS - 1 - j
            self.wait(slot)
            pl.when(self.kinds[slot] == 0)(lambda: self.step(acc, slot, 1, False, by_row=True))
            pl.when(self.kinds[slot] == 1)(lambda: self.step(acc, slot, 1, True))
            return 0

        def two_plain(j, _):
            self.wait(2 * j)
            self.wait(2 * j + 1)
            self.step(acc, 2 * j, 2, False)
            return 0

        lax.fori_loop(0, self.masked, one_masked, 0)
        lax.fori_loop(0, self.plain // 2, two_plain, 0)

        @pl.when(self.plain % 2 == 1)
        def _():
            self.wait(self.plain - 1)
            self.step(acc, self.plain - 1, 1, False)

    def add_shifted(self, acc, m_scr):
        def one_chunk(j, _):
            slot = jnp.where(j < self.plain, j, SLOTS - 1 - (j - self.plain))
            self.wait(slot)
            v = self.values(slot, 1)
            for r in range(2 * ROWS // TILE):
                rows = slice(r * TILE, (r + 1) * TILE)
                s = self.scores(slot, 1, r, True)
                old = m_scr[rows, :]
                m = jnp.maximum(old, jnp.max(s, axis=1, keepdims=True))
                alpha = jnp.exp2(old - m)
                p = jnp.exp2(s - jnp.concatenate([m] * (CHUNK // 128), axis=1)).astype(jnp.bfloat16)
                out = jnp.dot(p, v, preferred_element_type=jnp.float32)
                acc[rows, :] = acc[rows, :] * jnp.concatenate([alpha, alpha], axis=1) + out
                m_scr[rows, :] = m
            return 0

        lax.fori_loop(0, self.plain + self.masked, one_chunk, 0)


def own_line_kernel(len_ref, first_ref, q_ref, line, acc_ref, split_ref, kv_scr, ids, kinds, kv_sem):
    attention = Attention(len_ref, first_ref, line, None, split_ref, kv_scr, ids, kinds, kv_sem, near_only=True)
    attention.fetch((0,))
    for g in range(2):
        rows = slice(g * ROWS, (g + 1) * ROWS)
        scaled = q_ref[:, g * HD : (g + 1) * HD].astype(jnp.float32) * (LOG2E * HD**-0.5)
        high = scaled.astype(jnp.bfloat16)
        split_ref[rows, :HD] = high
        split_ref[rows, HD:] = (scaled - high.astype(jnp.float32)).astype(jnp.bfloat16)
    acc_ref[...] = jnp.zeros_like(acc_ref)
    attention.add(acc_ref)


def other_line_kernel(len_ref, first_ref, split_ref, before_ref, line_got, acc_ref, kv_scr, ids, kinds, kv_sem):
    attention = Attention(len_ref, first_ref, line_got, line_got, split_ref, kv_scr, ids, kinds, kv_sem, near_only=True)
    attention.fetch((1,))
    acc_ref[...] = before_ref[...]
    attention.add(acc_ref)


def part_kernel(
    len_ref, first_ref, split_hbm, before_hbm, fetched, acc_ref, kv_scr, ids, kinds, kv_sem, q_scr, in_sem
):
    attention = Attention(len_ref, first_ref, fetched, None, q_scr, kv_scr, ids, kinds, kv_sem)
    inputs = [
        pltpu.make_async_copy(split_hbm, q_scr, in_sem.at[0]),
        pltpu.make_async_copy(before_hbm, acc_ref, in_sem.at[1]),
    ]
    for copy in inputs:
        copy.start()
    attention.fetch((0,))
    for copy in inputs:
        copy.wait()
    attention.add(acc_ref)


def mix_kernel(
    len_ref,
    first_ref,
    split_hbm,
    act_hbm,
    before_hbm,
    fetched,
    other,
    wa_hbm,
    ws_hbm,
    o_hbm,
    kv_scr,
    ids,
    kinds,
    kv_sem,
    q_scr,
    acc_scr,
    m_scr,
    w_scr,
    in_scr,
    o_scr,
    in_sem,
    w_sem,
    o_sem,
):
    attention = Attention(len_ref, first_ref, fetched, other, q_scr, kv_scr, ids, kinds, kv_sem)
    inputs = [
        pltpu.make_async_copy(split_hbm, q_scr, in_sem.at[0]),
        pltpu.make_async_copy(before_hbm, acc_scr, in_sem.at[1]),
        pltpu.make_async_copy(act_hbm, in_scr.at[:, pl.ds(2 * HD, HP)], in_sem.at[2]),
    ]
    for copy in inputs[:2]:
        copy.start()
    attention.fetch((1,))
    weights = []
    for i in range(DM // COLS):
        cols = pl.ds(i * COLS, COLS)
        weights.append(
            (
                pltpu.make_async_copy(wa_hbm.at[:, cols], w_scr.at[pl.ds(0, 2 * HD), cols], w_sem.at[2 * i]),
                pltpu.make_async_copy(ws_hbm.at[:, cols], w_scr.at[pl.ds(2 * HD, HP), cols], w_sem.at[2 * i + 1]),
            )
        )
    inputs[2].start()
    for pair in weights:
        for copy in pair:
            copy.start()
    for copy in inputs[:2]:
        copy.wait()

    attention.add(acc_scr)
    total = acc_scr[:, HD:]
    fine = (jnp.min(total) > 2.0**-60) & (jnp.max(total) < 2.0**110)

    @pl.when(jnp.logical_not(fine))
    def _():
        attention.fetch((0, 1), every=True)
        acc_scr[...] = jnp.zeros_like(acc_scr)
        m_scr[...] = jnp.full(m_scr.shape, LOW, jnp.float32)
        attention.add_shifted(acc_scr, m_scr)

    for g in range(2):
        rows = slice(g * ROWS, (g + 1) * ROWS)
        in_scr[:, g * HD : (g + 1) * HD] = (acc_scr[rows, :HD] / acc_scr[rows, HD:]).astype(jnp.bfloat16)
    inputs[2].wait()

    def out_copy(i):
        cols = pl.ds(i * COLS, COLS)
        return pltpu.make_async_copy(o_scr.at[:, cols], o_hbm.at[:, cols], o_sem.at[i])

    for i in range(DM // COLS):
        cols = slice(i * COLS, (i + 1) * COLS)
        for copy in weights[i]:
            copy.wait()
        o_scr[:, cols] = jnp.dot(in_scr[...], w_scr[:, cols], preferred_element_type=jnp.float32).astype(jnp.bfloat16)
        out_copy(i).start()
    for i in range(DM // COLS):
        out_copy(i).wait()


def big(limit=LIMIT):
    return pltpu.CompilerParams(vmem_limit_bytes=limit)


def moved(block, route0, route1):
    pairs = []
    for x in range(4):
        for y in range(4):
            for core, route in enumerate((route0, route1)):
                to = route(x, y)
                if to is not None:
                    pairs.append((x * 8 + y * 2 + core, to[0] * 8 + to[1] * 2 + core))
    return lax.ppermute(block, "pack", pairs)


def lines():
    columns = [[x * 8 + y * 2 for x in range(4)] for y in range(4)]
    rows = [[x * 8 + y * 2 + 1 for y in range(4)] for x in range(4)]
    return columns + rows


def along_x(distance):
    return lambda x, y: (x + distance, y) if x + distance < 4 else None


def along_y(distance):
    return lambda x, y: (x, (y + distance) % 4)


def swapped(block):
    return lax.ppermute(block, "pack", [(i, i ^ 1) for i in range(32)])


def call(kernel, shapes, ins, *args):
    return pl.pallas_call(
        kernel,
        out_shape=tuple(jax.ShapeDtypeStruct(shape, jnp.bfloat16) for shape in shapes),
        in_specs=[SMEM] + [VMEM] * ins,
        out_specs=(VMEM,) * len(shapes),
        compiler_params=big(),
        cost_estimate=pl.CostEstimate(flops=10**6, bytes_accessed=10**6, transcendentals=0),
    )(*args)


def local(
    queries,
    keys_values,
    ssm_values,
    ssm_gates,
    ssm_maps,
    step_size,
    decay_log,
    skip_gain,
    attn_out_weight,
    ssd_out_weight,
    lengths,
):
    first = jnp.reshape(lax.axis_index("pack") * ROWS, (1,)).astype(jnp.int32)
    kv = keys_values.reshape(ROWS, 2 * HD)
    nowhere = lambda x, y: None
    below = moved(kv, along_y(1), along_x(1))
    above = moved(kv, along_y(3), along_x(3))
    across = moved(kv, along_y(2), along_x(2))
    y_local, run_keep, run_send, fac = pl.pallas_call(
        ssd_kernel,
        out_shape=(
            jax.ShapeDtypeStruct((ROWS, HP), jnp.float32),
            jax.ShapeDtypeStruct((STATE_ROWS, HALF), jnp.bfloat16),
            jax.ShapeDtypeStruct((STATE_ROWS, HALF), jnp.bfloat16),
            jax.ShapeDtypeStruct((ROWS, HEADS), jnp.float32),
        ),
        in_specs=[SMEM] * 4 + [VMEM] * 3,
        out_specs=(VMEM, VMEM, VMEM, VMEM),
        compiler_params=big(62 * 2**20),
        cost_estimate=pl.CostEstimate(flops=10**9, bytes_accessed=4 * 10**6, transcendentals=10**6),
        name="ssd_local",
    )(lengths, decay_log, skip_gain, first, ssm_values, ssm_maps, step_size.T)

    run = (STATE_ROWS, HALF)
    run_got = swapped(run_send)
    below, above, across, run_got = lax.optimization_barrier((below, above, across, run_got))
    line = jnp.concatenate([kv, below, above, across], axis=0)
    fetched = lax.all_gather(line, "pack", axis=0, tiled=True, axis_index_groups=lines())
    (chip,) = call(chip_kernel, [run], 2, first, run_keep, run_got)
    chips = [moved(chip, along_y(d), along_y(d)) for d in (1, 3, 2)]
    chunks_scratch = [
        pltpu.VMEM((SLOTS * CHUNK, 2 * HD), jnp.bfloat16),
        pltpu.SMEM((SLOTS,), jnp.int32),
        pltpu.SMEM((SLOTS,), jnp.int32),
        pltpu.SemaphoreType.DMA((SLOTS,)),
    ]
    sums = jax.ShapeDtypeStruct((2 * ROWS, 2 * HD), jnp.float32)
    split = jax.ShapeDtypeStruct((2 * ROWS, 2 * HD), jnp.bfloat16)

    def attend(kernel, name, shapes, vmem, *args, scratch=()):
        out = pl.pallas_call(
            kernel,
            out_shape=shapes,
            in_specs=[SMEM] * 2 + [VMEM] * vmem + [ANY] * (len(args) - vmem),
            out_specs=(VMEM,) * len(shapes),
            scratch_shapes=chunks_scratch + list(scratch),
            compiler_params=big(),
            cost_estimate=pl.CostEstimate(flops=3 * 10**9, bytes_accessed=5 * 10**6, transcendentals=5 * 10**6),
            name=name,
        )(lengths, first, *args)
        return out

    line = lax.optimization_barrier((line, chip))[0]
    line_got = swapped(line)
    acc, queries_split = attend(own_line_kernel, "own_line", (sums, split), 1, queries, line)
    chips = lax.optimization_barrier((*chips, acc))[:3]
    prefix, total = call(row_kernel, [run, run], 4, first, chip, *chips)
    rows = [moved(total, along_x(d), along_x(d)) for d in (3, 2, 1)]
    line_got = lax.optimization_barrier((line_got, prefix))[0]
    (acc,) = attend(other_line_kernel, "other_line", (sums,), 2, queries_split, acc, line_got)
    rows = lax.optimization_barrier((*rows, acc))[:3]
    keep, send = call(carry_kernel, [(SN, HALF)] * 2, 6, first, *rows, prefix, run_keep, run_got)
    got = swapped(send)
    act = pl.pallas_call(
        gate_kernel,
        out_shape=jax.ShapeDtypeStruct((ROWS, HP), jnp.bfloat16),
        grid=(2,),
        in_specs=[
            SMEM,
            pl.BlockSpec((ROWS // 2, HP), lambda i: (i, 0)),
            pl.BlockSpec((ROWS // 2, HP), lambda i: (i, 0)),
            pl.BlockSpec((ROWS // 2, SN), lambda i: (i, 1)),
            pl.BlockSpec((ROWS // 2, HEADS), lambda i: (i, 0)),
            pl.BlockSpec((SN, HALF), lambda i: (0, 0)),
            pl.BlockSpec((SN, HALF), lambda i: (0, 0)),
        ],
        out_specs=pl.BlockSpec((ROWS // 2, HP), lambda i: (i, 0)),
        compiler_params=big(),
        cost_estimate=pl.CostEstimate(flops=10**8, bytes_accessed=3 * 10**6, transcendentals=3 * 10**5),
        name="gate",
    )(first, y_local, ssm_gates, ssm_maps, fac, keep, got)

    fetched = lax.optimization_barrier((fetched, act))[0]
    other = swapped(fetched)
    (acc,) = attend(
        part_kernel,
        "part",
        (sums,),
        0,
        queries_split,
        acc,
        fetched,
        scratch=[pltpu.VMEM((2 * ROWS, 2 * HD), jnp.bfloat16), pltpu.SemaphoreType.DMA((2,))],
    )

    terms = pl.pallas_call(
        mix_kernel,
        out_shape=jax.ShapeDtypeStruct((ROWS, DM), jnp.bfloat16),
        in_specs=[SMEM] * 2 + [ANY] * 7,
        out_specs=ANY,
        scratch_shapes=chunks_scratch
        + [
            pltpu.VMEM((2 * ROWS, 2 * HD), jnp.bfloat16),
            pltpu.VMEM((2 * ROWS, 2 * HD), jnp.float32),
            pltpu.VMEM((2 * ROWS, HD), jnp.float32),
            pltpu.VMEM((2 * HD + HP, DM), jnp.bfloat16),
            pltpu.VMEM((ROWS, 2 * HD + HP), jnp.bfloat16),
            pltpu.VMEM((ROWS, DM), jnp.bfloat16),
            pltpu.SemaphoreType.DMA((3,)),
            pltpu.SemaphoreType.DMA((2 * (DM // COLS),)),
            pltpu.SemaphoreType.DMA((DM // COLS,)),
        ],
        compiler_params=big(),
        cost_estimate=pl.CostEstimate(flops=9 * 10**9, bytes_accessed=25 * 10**6, transcendentals=9 * 10**6),
        name="mix",
    )(lengths, first, queries_split, act, acc, fetched, other, attn_out_weight, ssd_out_weight)
    return lax.psum_scatter(terms, "tp", scatter_dimension=0, tiled=True)


def solution(mesh):
    return jax.shard_map(
        local,
        mesh=mesh,
        in_specs=(
            P("pack", "tp"),
            P("pack", "tp", None),
            P("pack", "tp"),
            P("pack", "tp"),
            P("pack", None),
            P("pack", "tp"),
            P("tp"),
            P("tp"),
            P("tp", None),
            P("tp", None),
            P(),
        ),
        out_specs=P(("pack", "tp"), None),
        check_vma=False,
    )
```

```python
import jax
import jax.numpy as jnp
from jax import lax
from jax.experimental import pallas as pl
from jax.experimental.pallas import tpu as pltpu
from jax.sharding import PartitionSpec as P

ROWS = 512
BLOCK = 256
HD = 128
HEADS = 8
HP = 512
SN = 256
DM = 5120
CHUNK = 512
SLOTS = 18
TILE = 256
COLS = 1024
LOW = -1e30
LOG2E = 1.4426950408889634
HIGH = lax.Precision.HIGHEST
LIMIT = 64 * 2**20 - 2**16
HALF = HP // 2
STATE_ROWS = SN + 16
VMEM = pl.BlockSpec(memory_space=pltpu.VMEM)
SMEM = pl.BlockSpec(memory_space=pltpu.SMEM)
ANY = pl.BlockSpec(memory_space=pl.ANY)


def iota(shape, dim):
    return lax.broadcasted_iota(jnp.int32, shape, dim)


def ends_of(len_ref):
    e0 = len_ref[0]
    e1 = e0 + len_ref[1]
    return e0, e1, e1 + len_ref[2]


def start_of(pos, ends):
    e0, e1, e2 = ends
    zero = jnp.zeros_like(pos)
    out = jnp.where(pos >= e0, zero + e0, zero)
    out = jnp.where(pos >= e1, zero + e1, out)
    return jnp.where(pos >= e2, zero + e2, out)


def spread():
    return (iota((HEADS, HP), 1) // (HP // HEADS) == iota((HEADS, HP), 0)).astype(jnp.float32)


def widen(a, expand):
    return jnp.dot(a, expand, precision=HIGH, preferred_element_type=jnp.float32)


def ssd_kernel(len_ref, dl_ref, skip_ref, first_ref, x_ref, maps_ref, step_ref, y_ref, keep_ref, send_ref, fac_ref):
    first = first_ref[0]
    ends = ends_of(len_ref)
    expand = spread()
    head_sub = iota((HEADS, 1), 0)
    wide_lane = iota((1, HP), 1) // (HP // HEADS)
    rate = jnp.zeros((HEADS, 1), jnp.float32)
    skip = jnp.zeros((1, HP), jnp.float32)
    for h in range(HEADS):
        rate = jnp.where(head_sub == h, dl_ref[h], rate)
        skip = jnp.where(wide_lane == h, skip_ref[h], skip)
    rate = -jnp.exp(rate)
    row = iota((BLOCK, 1), 0)
    col = iota((1, BLOCK), 1)
    tri = (row >= col).astype(jnp.float32)
    half = iota((1, 128), 1) < 64
    state = None
    before = None
    for n in range(ROWS // BLOCK):
        rows = slice(n * BLOCK, (n + 1) * BLOCK)
        base = first + n * BLOCK
        start_col = start_of(base + row, ends)
        last_start = start_of(base + (BLOCK - 1), ends)
        cum_t = lax.dot_general(
            rate * step_ref[:, rows], tri, (((1,), (1,)), ((), ())), precision=HIGH, preferred_element_type=jnp.float32
        )
        cum = cum_t.T
        write = maps_ref[rows, :SN]
        read = maps_ref[rows, SN:]
        prod = lax.dot_general(read, write, (((1,), (1,)), ((), ())), preferred_element_type=jnp.float32)
        allowed = (base + col >= start_col) & (col <= row)
        for pair in range(HEADS // 2):
            lanes = slice(pair * 128, (pair + 1) * 128)
            x = x_ref[rows, lanes]
            total = skip[:, lanes] * x.astype(jnp.float32)
            for which in range(2):
                h = pair * 2 + which
                gap = jnp.where(allowed, cum[:, h : h + 1] - cum_t[h : h + 1, :], LOW)
                weights = (jnp.exp(gap) * prod).astype(jnp.bfloat16)
                part = jnp.where(half if which == 0 else ~half, x, jnp.zeros_like(x))
                total = total + jnp.dot(weights, part, preferred_element_type=jnp.float32)
            y_ref[rows, lanes] = total
        ecum = jnp.exp(cum)
        if state is not None:
            local = widen(jnp.where(start_col < base, ecum, 0.0), expand)
            reads = jnp.dot(read, state.astype(jnp.bfloat16), preferred_element_type=jnp.float32)
            y_ref[rows, :] += reads * local
        carry = jnp.where(start_col < first, ecum, 0.0)
        if before is not None:
            carry = carry * before
        fac_ref[rows, :] = carry
        tail = jnp.exp(cum[BLOCK - 1 : BLOCK, :] - cum)
        tail = widen(jnp.where(base + row >= last_start, tail, 0.0), expand)
        weighted = (x_ref[rows, :].astype(jnp.float32) * tail).astype(jnp.bfloat16)
        new = lax.dot_general(write, weighted, (((0,), (0,)), ((), ())), preferred_element_type=jnp.float32)
        end = ecum[BLOCK - 8 :, :]
        if state is not None:
            keep = jnp.where(last_start < base, 1.0, 0.0)
            new = new + (keep * widen(end, expand)[7:8, :]) * state
            end = end * before
        state = new
        before = end[7:8, :]
    through = jnp.where(last_start < first, 1.0, 0.0) * widen(end, expand)[7:8, :]
    core = (first // ROWS) % 2
    left, right = slice(0, HALF), slice(HALF, HP)
    for ref, wanted in ((keep_ref, 0), (send_ref, 1)):
        store_run(
            ref,
            jnp.where(core == wanted, state[:, left], state[:, right]),
            jnp.where(core == wanted, through[:, left], through[:, right]),
        )


def store_run(ref, state, through):
    high = through.astype(jnp.bfloat16).astype(jnp.float32)
    low = through - high
    sub = iota((16, 1), 0)
    ref[:SN, :] = state.astype(jnp.bfloat16)
    ref[SN:, :] = jnp.where(sub == 0, high, jnp.where(sub == 1, low, 0.0)).astype(jnp.bfloat16)


def load_run(ref):
    tail = ref[SN:, :].astype(jnp.float32)
    return ref[:SN, :].astype(jnp.float32), tail[0:1, :] + tail[1:2, :]


def pick(cond, one, other):
    return jnp.where(cond, one[0], other[0]), jnp.where(cond, one[1], other[1])


def after(earlier, later):
    return later[0] + later[1] * earlier[0], earlier[1] * later[1]


def chip_kernel(first_ref, mine_ref, other_ref, out_ref):
    core = (first_ref[0] // ROWS) % 2
    mine, other = load_run(mine_ref), load_run(other_ref)
    store_run(out_ref, *after(pick(core == 0, mine, other), pick(core == 0, other, mine)))


def row_kernel(first_ref, mine_ref, below_ref, above_ref, across_ref, prefix_ref, total_ref):
    y = (first_ref[0] // (2 * ROWS)) % 4
    by_distance = [load_run(ref) for ref in (mine_ref, below_ref, across_ref, above_ref)]
    run = (jnp.zeros((SN, HALF), jnp.float32), jnp.ones((1, HALF), jnp.float32))
    prefix = run
    for place in range(4):
        distance = (y - place) % 4
        piece = by_distance[0]
        for d in range(1, 4):
            piece = pick(distance == d, by_distance[d], piece)
        prefix = pick(y == place, run, prefix)
        run = after(run, piece)
    store_run(prefix_ref, *prefix)
    store_run(total_ref, *run)


def carry_kernel(first_ref, row3_ref, row2_ref, row1_ref, prefix_ref, mine_ref, other_ref, keep_ref, send_ref):
    core = (first_ref[0] // ROWS) % 2
    run = load_run(row3_ref)
    for ref in (row2_ref, row1_ref, prefix_ref):
        run = after(run, load_run(ref))
    behind = after(run, pick(core == 0, load_run(mine_ref), load_run(other_ref)))
    keep_ref[...] = jnp.where(core == 0, run[0], behind[0]).astype(jnp.bfloat16)
    send_ref[...] = jnp.where(core == 0, behind[0], run[0]).astype(jnp.bfloat16)


def gate_kernel(first_ref, y_ref, z_ref, read_ref, fac_ref, keep_ref, got_ref, act_ref):
    core = (first_ref[0] // ROWS) % 2
    keep, got = keep_ref[...], got_ref[...]
    state = jnp.concatenate([jnp.where(core == 0, keep, got), jnp.where(core == 0, got, keep)], axis=1)
    reads = jnp.dot(read_ref[...], state, preferred_element_type=jnp.float32)
    y = y_ref[...] + reads * widen(fac_ref[...], spread())
    z = z_ref[...].astype(jnp.float32)
    act_ref[...] = (y * (z / (1.0 + jnp.exp(-z)))).astype(jnp.bfloat16)


class Attention:
    def __init__(self, len_ref, first_ref, fetched, other, q_scr, kv_scr, ids, kinds, kv_sem, near_only=False):
        self.first = first_ref[0]
        self.ends = ends_of(len_ref)
        self.mine = self.first // CHUNK
        self.low = start_of(self.first, self.ends) // CHUNK
        self.last_start = start_of(self.first + ROWS - 1, self.ends)
        self.arrays = (fetched, other)
        self.near_only = near_only
        self.q_scr, self.kv_scr, self.ids, self.kinds, self.kv_sem = q_scr, kv_scr, ids, kinds, kv_sem

    def count(self, far):
        return 4 if self.near_only else (self.mine - far - self.low) // 2 + 1

    def block(self, far, i):
        if not self.near_only:
            return self.mine - far - 2 * i
        core = self.mine % 2
        step = jnp.where(core == far, 2, 8)
        return self.mine + jnp.where(core == 0, far, -far) - step * i

    def in_line(self, block):
        row = block // 8 == self.mine // 8
        column = (block // 2) % 4 == (self.mine // 2) % 4
        return jnp.where(block % 2 == 0, row, column)

    def place(self, block):
        x, y, even = block // 8, (block // 2) % 4, block % 2 == 0
        my_x, my_y = self.mine // 8, (self.mine // 2) % 4
        distance = jnp.where(even, (my_y - y) % 4, (my_x - x) % 4)
        place = distance ^ (distance >> 1)
        if not self.near_only:
            place = place + 4 * jnp.where(even, x, y)
        return place

    def copy(self, far, place, slot):
        rows = pl.ds(pl.multiple_of(place * CHUNK, CHUNK), CHUNK)
        to = pl.ds(pl.multiple_of(slot * CHUNK, CHUNK), CHUNK)
        return pltpu.make_async_copy(self.arrays[far].at[rows], self.kv_scr.at[to], self.kv_sem.at[slot])

    def fetch(self, fars, every=False):
        def one_chunk(far, i, carry):
            plain, masked = carry
            block = self.block(far, i)
            if self.near_only:
                wanted = (block >= self.low) & (block <= self.mine) & self.in_line(block)
            elif every:
                wanted = block >= self.low
            else:
                wanted = jnp.logical_not(self.in_line(block))
            mask = (block == self.mine) | (block * CHUNK < self.last_start)
            slot = jnp.where(mask, SLOTS - 1 - masked, plain)

            @pl.when(wanted)
            def _():
                self.ids[slot] = block
                inside = start_of(block * CHUNK + (CHUNK - 1), self.ends) > block * CHUNK
                self.kinds[slot] = jnp.where((block == self.mine) | inside, 1, 0)
                self.copy(far, self.place(block), slot).start()

            new = wanted.astype(jnp.int32)
            return plain + jnp.where(mask, 0, new), masked + jnp.where(mask, new, 0)

        carry = (jnp.int32(0), jnp.int32(0))
        for far in fars:
            carry = lax.fori_loop(0, self.count(far), lambda i, c, far=far: one_chunk(far, i, c), carry)
        self.plain, self.masked = carry

    def wait(self, slot):
        self.copy(0, 0, slot).wait()

    def keys(self, slot, chunks):
        return pl.ds(pl.multiple_of(slot * CHUNK, CHUNK), chunks * CHUNK)

    def scores(self, slot, chunks, r, masked):
        rows = slice(r * TILE, (r + 1) * TILE)
        k = self.kv_scr[self.keys(slot, chunks), :HD]
        s = lax.dot_general(
            self.q_scr[rows, :],
            jnp.concatenate([k, k], axis=1),
            (((1,), (1,)), ((), ())),
            preferred_element_type=jnp.float32,
        )
        if masked:
            pos = self.first + rows.start % ROWS + iota((TILE, 1), 0)
            key = self.ids[slot] * CHUNK + iota((1, CHUNK), 1)
            s = jnp.where((key >= start_of(pos, self.ends)) & (key <= pos), s, LOW)
        return s

    def values(self, slot, chunks):
        v = self.kv_scr[self.keys(slot, chunks), HD:]
        return jnp.concatenate([v, jnp.ones((chunks * CHUNK, HD), jnp.bfloat16)], axis=1)

    def step(self, acc, slot, chunks, masked, by_row=False):
        v = self.values(slot, chunks)
        tiles = 2 * ROWS // TILE
        s = self.scores(slot, chunks, 0, masked)
        for r in range(tiles):
            following = self.scores(slot, chunks, r + 1, masked) if r + 1 < tiles else None
            p = jnp.exp2(s).astype(jnp.bfloat16)
            out = jnp.dot(p, v, preferred_element_type=jnp.float32)
            if by_row:
                pos = self.first + (r * TILE) % ROWS + iota((TILE, 1), 0)
                out = jnp.where(start_of(pos, self.ends) <= self.ids[slot] * CHUNK, out, 0.0)
            acc[r * TILE : (r + 1) * TILE, :] += out
            s = following

    def add(self, acc):
        def one_masked(j, _):
            slot = SLOTS - 1 - j
            self.wait(slot)
            pl.when(self.kinds[slot] == 0)(lambda: self.step(acc, slot, 1, False, by_row=True))
            pl.when(self.kinds[slot] == 1)(lambda: self.step(acc, slot, 1, True))
            return 0

        def two_plain(j, _):
            self.wait(2 * j)
            self.wait(2 * j + 1)
            self.step(acc, 2 * j, 2, False)
            return 0

        lax.fori_loop(0, self.masked, one_masked, 0)
        lax.fori_loop(0, self.plain // 2, two_plain, 0)

        @pl.when(self.plain % 2 == 1)
        def _():
            self.wait(self.plain - 1)
            self.step(acc, self.plain - 1, 1, False)

    def add_shifted(self, acc, m_scr):
        def one_chunk(j, _):
            slot = jnp.where(j < self.plain, j, SLOTS - 1 - (j - self.plain))
            self.wait(slot)
            v = self.values(slot, 1)
            for r in range(2 * ROWS // TILE):
                rows = slice(r * TILE, (r + 1) * TILE)
                s = self.scores(slot, 1, r, True)
                old = m_scr[rows, :]
                m = jnp.maximum(old, jnp.max(s, axis=1, keepdims=True))
                alpha = jnp.exp2(old - m)
                p = jnp.exp2(s - jnp.concatenate([m] * (CHUNK // 128), axis=1)).astype(jnp.bfloat16)
                out = jnp.dot(p, v, preferred_element_type=jnp.float32)
                acc[rows, :] = acc[rows, :] * jnp.concatenate([alpha, alpha], axis=1) + out
                m_scr[rows, :] = m
            return 0

        lax.fori_loop(0, self.plain + self.masked, one_chunk, 0)


def own_line_kernel(len_ref, first_ref, q_ref, line, acc_ref, split_ref, kv_scr, ids, kinds, kv_sem):
    attention = Attention(len_ref, first_ref, line, None, split_ref, kv_scr, ids, kinds, kv_sem, near_only=True)
    attention.fetch((0,))
    for g in range(2):
        rows = slice(g * ROWS, (g + 1) * ROWS)
        scaled = q_ref[:, g * HD : (g + 1) * HD].astype(jnp.float32) * (LOG2E * HD**-0.5)
        high = scaled.astype(jnp.bfloat16)
        split_ref[rows, :HD] = high
        split_ref[rows, HD:] = (scaled - high.astype(jnp.float32)).astype(jnp.bfloat16)
    acc_ref[...] = jnp.zeros_like(acc_ref)
    attention.add(acc_ref)


def other_line_kernel(len_ref, first_ref, split_ref, before_ref, line_got, acc_ref, kv_scr, ids, kinds, kv_sem):
    attention = Attention(len_ref, first_ref, line_got, line_got, split_ref, kv_scr, ids, kinds, kv_sem, near_only=True)
    attention.fetch((1,))
    acc_ref[...] = before_ref[...]
    attention.add(acc_ref)


def part_kernel(
    len_ref, first_ref, split_hbm, before_hbm, fetched, acc_ref, kv_scr, ids, kinds, kv_sem, q_scr, in_sem
):
    attention = Attention(len_ref, first_ref, fetched, None, q_scr, kv_scr, ids, kinds, kv_sem)
    inputs = [
        pltpu.make_async_copy(split_hbm, q_scr, in_sem.at[0]),
        pltpu.make_async_copy(before_hbm, acc_ref, in_sem.at[1]),
    ]
    for copy in inputs:
        copy.start()
    attention.fetch((0,))
    for copy in inputs:
        copy.wait()
    attention.add(acc_ref)


def mix_kernel(
    len_ref,
    first_ref,
    split_hbm,
    act_hbm,
    before_hbm,
    fetched,
    other,
    wa_hbm,
    ws_hbm,
    o_hbm,
    kv_scr,
    ids,
    kinds,
    kv_sem,
    q_scr,
    acc_scr,
    m_scr,
    w_scr,
    in_scr,
    o_scr,
    in_sem,
    w_sem,
    o_sem,
):
    attention = Attention(len_ref, first_ref, fetched, other, q_scr, kv_scr, ids, kinds, kv_sem)
    inputs = [
        pltpu.make_async_copy(split_hbm, q_scr, in_sem.at[0]),
        pltpu.make_async_copy(before_hbm, acc_scr, in_sem.at[1]),
        pltpu.make_async_copy(act_hbm, in_scr.at[:, pl.ds(2 * HD, HP)], in_sem.at[2]),
    ]
    for copy in inputs[:2]:
        copy.start()
    attention.fetch((1,))
    weights = []
    for i in range(DM // COLS):
        cols = pl.ds(i * COLS, COLS)
        weights.append(
            (
                pltpu.make_async_copy(wa_hbm.at[:, cols], w_scr.at[pl.ds(0, 2 * HD), cols], w_sem.at[2 * i]),
                pltpu.make_async_copy(ws_hbm.at[:, cols], w_scr.at[pl.ds(2 * HD, HP), cols], w_sem.at[2 * i + 1]),
            )
        )
    inputs[2].start()
    for pair in weights:
        for copy in pair:
            copy.start()
    for copy in inputs[:2]:
        copy.wait()

    attention.add(acc_scr)
    total = acc_scr[:, HD:]
    fine = (jnp.min(total) > 2.0**-60) & (jnp.max(total) < 2.0**110)

    @pl.when(jnp.logical_not(fine))
    def _():
        attention.fetch((0, 1), every=True)
        acc_scr[...] = jnp.zeros_like(acc_scr)
        m_scr[...] = jnp.full(m_scr.shape, LOW, jnp.float32)
        attention.add_shifted(acc_scr, m_scr)

    for g in range(2):
        rows = slice(g * ROWS, (g + 1) * ROWS)
        in_scr[:, g * HD : (g + 1) * HD] = (acc_scr[rows, :HD] / acc_scr[rows, HD:]).astype(jnp.bfloat16)
    inputs[2].wait()

    def out_copy(i):
        cols = pl.ds(i * COLS, COLS)
        return pltpu.make_async_copy(o_scr.at[:, cols], o_hbm.at[:, cols], o_sem.at[i])

    for i in range(DM // COLS):
        cols = slice(i * COLS, (i + 1) * COLS)
        for copy in weights[i]:
            copy.wait()
        o_scr[:, cols] = jnp.dot(in_scr[...], w_scr[:, cols], preferred_element_type=jnp.float32).astype(jnp.bfloat16)
        out_copy(i).start()
    for i in range(DM // COLS):
        out_copy(i).wait()


def big(limit=LIMIT):
    return pltpu.CompilerParams(vmem_limit_bytes=limit)


def moved(block, route0, route1):
    pairs = []
    for x in range(4):
        for y in range(4):
            for core, route in enumerate((route0, route1)):
                to = route(x, y)
                if to is not None:
                    pairs.append((x * 8 + y * 2 + core, to[0] * 8 + to[1] * 2 + core))
    return lax.ppermute(block, "pack", pairs)


def lines():
    columns = [[x * 8 + y * 2 for x in range(4)] for y in range(4)]
    rows = [[x * 8 + y * 2 + 1 for y in range(4)] for x in range(4)]
    return columns + rows


def along_x(distance):
    return lambda x, y: (x + distance, y) if x + distance < 4 else None


def along_y(distance):
    return lambda x, y: (x, (y + distance) % 4)


def swapped(block):
    return lax.ppermute(block, "pack", [(i, i ^ 1) for i in range(32)])


def call(kernel, shapes, ins, *args):
    return pl.pallas_call(
        kernel,
        out_shape=tuple(jax.ShapeDtypeStruct(shape, jnp.bfloat16) for shape in shapes),
        in_specs=[SMEM] + [VMEM] * ins,
        out_specs=(VMEM,) * len(shapes),
        compiler_params=big(),
        cost_estimate=pl.CostEstimate(flops=10**6, bytes_accessed=10**6, transcendentals=0),
    )(*args)


def local(
    queries,
    keys_values,
    ssm_values,
    ssm_gates,
    ssm_maps,
    step_size,
    decay_log,
    skip_gain,
    attn_out_weight,
    ssd_out_weight,
    lengths,
):
    first = jnp.reshape(lax.axis_index("pack") * ROWS, (1,)).astype(jnp.int32)
    kv = keys_values.reshape(ROWS, 2 * HD)
    nowhere = lambda x, y: None
    below = moved(kv, along_y(1), along_x(1))
    above = moved(kv, along_y(3), along_x(3))
    across = moved(kv, along_y(2), along_x(2))
    y_local, run_keep, run_send, fac = pl.pallas_call(
        ssd_kernel,
        out_shape=(
            jax.ShapeDtypeStruct((ROWS, HP), jnp.float32),
            jax.ShapeDtypeStruct((STATE_ROWS, HALF), jnp.bfloat16),
            jax.ShapeDtypeStruct((STATE_ROWS, HALF), jnp.bfloat16),
            jax.ShapeDtypeStruct((ROWS, HEADS), jnp.float32),
        ),
        in_specs=[SMEM] * 4 + [VMEM] * 3,
        out_specs=(VMEM, VMEM, VMEM, VMEM),
        compiler_params=big(62 * 2**20),
        cost_estimate=pl.CostEstimate(flops=10**9, bytes_accessed=4 * 10**6, transcendentals=10**6),
        name="ssd_local",
    )(lengths, decay_log, skip_gain, first, ssm_values, ssm_maps, step_size.T)

    below, above, across = lax.optimization_barrier((below, above, across, fac))[:3]
    line = jnp.concatenate([kv, below, above, across], axis=0)
    fetched = lax.all_gather(line, "pack", axis=0, tiled=True, axis_index_groups=lines())
    line_got = swapped(line)

    run = (STATE_ROWS, HALF)
    run_got = swapped(run_send)
    (chip,) = call(chip_kernel, [run], 2, first, run_keep, run_got)
    chips = [moved(chip, along_y(d), along_y(d)) for d in (1, 3, 2)]
    chunks_scratch = [
        pltpu.VMEM((SLOTS * CHUNK, 2 * HD), jnp.bfloat16),
        pltpu.SMEM((SLOTS,), jnp.int32),
        pltpu.SMEM((SLOTS,), jnp.int32),
        pltpu.SemaphoreType.DMA((SLOTS,)),
    ]
    sums = jax.ShapeDtypeStruct((2 * ROWS, 2 * HD), jnp.float32)
    split = jax.ShapeDtypeStruct((2 * ROWS, 2 * HD), jnp.bfloat16)

    def attend(kernel, name, shapes, vmem, *args, scratch=()):
        out = pl.pallas_call(
            kernel,
            out_shape=shapes,
            in_specs=[SMEM] * 2 + [VMEM] * vmem + [ANY] * (len(args) - vmem),
            out_specs=(VMEM,) * len(shapes),
            scratch_shapes=chunks_scratch + list(scratch),
            compiler_params=big(),
            cost_estimate=pl.CostEstimate(flops=3 * 10**9, bytes_accessed=5 * 10**6, transcendentals=5 * 10**6),
            name=name,
        )(lengths, first, *args)
        return out

    line = lax.optimization_barrier((line, chip))[0]
    acc, queries_split = attend(own_line_kernel, "own_line", (sums, split), 1, queries, line)
    chips = lax.optimization_barrier((*chips, acc))[:3]
    prefix, total = call(row_kernel, [run, run], 4, first, chip, *chips)
    rows = [moved(total, along_x(d), along_x(d)) for d in (3, 2, 1)]
    line_got = lax.optimization_barrier((line_got, prefix))[0]
    (acc,) = attend(other_line_kernel, "other_line", (sums,), 2, queries_split, acc, line_got)
    rows = lax.optimization_barrier((*rows, acc))[:3]
    keep, send = call(carry_kernel, [(SN, HALF)] * 2, 6, first, *rows, prefix, run_keep, run_got)
    got = swapped(send)
    act = pl.pallas_call(
        gate_kernel,
        out_shape=jax.ShapeDtypeStruct((ROWS, HP), jnp.bfloat16),
        grid=(4,),
        in_specs=[
            SMEM,
            pl.BlockSpec((ROWS // 4, HP), lambda i: (i, 0)),
            pl.BlockSpec((ROWS // 4, HP), lambda i: (i, 0)),
            pl.BlockSpec((ROWS // 4, SN), lambda i: (i, 1)),
            pl.BlockSpec((ROWS // 4, HEADS), lambda i: (i, 0)),
            pl.BlockSpec((SN, HALF), lambda i: (0, 0)),
            pl.BlockSpec((SN, HALF), lambda i: (0, 0)),
        ],
        out_specs=pl.BlockSpec((ROWS // 4, HP), lambda i: (i, 0)),
        compiler_params=big(),
        cost_estimate=pl.CostEstimate(flops=10**8, bytes_accessed=3 * 10**6, transcendentals=3 * 10**5),
        name="gate",
    )(first, y_local, ssm_gates, ssm_maps, fac, keep, got)

    fetched = lax.optimization_barrier((fetched, act))[0]
    other = swapped(fetched)
    (acc,) = attend(
        part_kernel,
        "part",
        (sums,),
        0,
        queries_split,
        acc,
        fetched,
        scratch=[pltpu.VMEM((2 * ROWS, 2 * HD), jnp.bfloat16), pltpu.SemaphoreType.DMA((2,))],
    )

    terms = pl.pallas_call(
        mix_kernel,
        out_shape=jax.ShapeDtypeStruct((ROWS, DM), jnp.bfloat16),
        in_specs=[SMEM] * 2 + [ANY] * 7,
        out_specs=ANY,
        scratch_shapes=chunks_scratch
        + [
            pltpu.VMEM((2 * ROWS, 2 * HD), jnp.bfloat16),
            pltpu.VMEM((2 * ROWS, 2 * HD), jnp.float32),
            pltpu.VMEM((2 * ROWS, HD), jnp.float32),
            pltpu.VMEM((2 * HD + HP, DM), jnp.bfloat16),
            pltpu.VMEM((ROWS, 2 * HD + HP), jnp.bfloat16),
            pltpu.VMEM((ROWS, DM), jnp.bfloat16),
            pltpu.SemaphoreType.DMA((3,)),
            pltpu.SemaphoreType.DMA((2 * (DM // COLS),)),
            pltpu.SemaphoreType.DMA((DM // COLS,)),
        ],
        compiler_params=big(),
        cost_estimate=pl.CostEstimate(flops=9 * 10**9, bytes_accessed=25 * 10**6, transcendentals=9 * 10**6),
        name="mix",
    )(lengths, first, queries_split, act, acc, fetched, other, attn_out_weight, ssd_out_weight)
    return lax.psum_scatter(terms, "tp", scatter_dimension=0, tiled=True)


def solution(mesh):
    return jax.shard_map(
        local,
        mesh=mesh,
        in_specs=(
            P("pack", "tp"),
            P("pack", "tp", None),
            P("pack", "tp"),
            P("pack", "tp"),
            P("pack", None),
            P("pack", "tp"),
            P("tp"),
            P("tp"),
            P("tp", None),
            P("tp", None),
            P(),
        ),
        out_specs=P(("pack", "tp"), None),
        check_vma=False,
    )
```
